512 devices in a mesh: video: 64 (over x, z), audio: 8 (over y, core).
Axes of the slice: x: 4, y: 4, z: 16, core: 2. Of those that a mesh axis runs over, the one named last changes fastest.
Arguments:
- queries: bfloat16 [65536, 1536], P(('video', 'audio')), may hold values from -160 to 160
- keys: bfloat16 [16384, 1536], P('video'), may hold values from -6 to 6
- values: bfloat16 [16384, 1536], P('video'), may hold values from -6 to 6
- out_grad: bfloat16 [65536, 1536], P(('video', 'audio')), may hold values from -6 to 6
- delta: float32 [12, 65536], P(None, ('video', 'audio')), may hold values from -4 to 4
- window_low: int32 [1024], P(('video', 'audio')), may hold values from 0 to 511, as said below
- window_high: int32 [1024], P(('video', 'audio')), may hold values from 1 to 512, as said below
Outputs:
- query_grad: bfloat16 [65536, 1536], P(('video', 'audio'))
- key_grad: bfloat16 [16384, 1536], P('video', 'audio')
- value_grad: bfloat16 [16384, 1536], P('video', 'audio')
The draws below stay inside these ranges and needn't reach their ends.
Inputs may be any that keep to these rules, and one draw needn't show every extreme that they name: `window_low`: A window holds 1 to 3 audio blocks; video block j's window always holds audio block ((2 j + 1) * 512) // 2048 and reaches at most one block to either side of it. `window_high`: see window_low.
All inputs are finite; a program needn't handle non-finite values.
Results may differ from the reference program's by a relative error of at most 0.015.
Values may be sent and summed in bfloat16 or wider, within the bound.
A program may use at most 64 MiB of HBM per device.

```python
import math
import jax
import jax.numpy as jnp
from jax import lax

HEADS = 12
HEAD_DIM = 128
WIDTH = 1536
VBLOCK = 64
ABLOCK = 32
WINDOW = 3
NV = 65536
NA = 16384
NVB = 1024
NAB = 512
N_VIDEO = 64


def shared_keys(key):
    return jnp.clip(jax.random.normal(key, (NA, WIDTH), jnp.float32), -6.0, 6.0)


def block_centers():
    blocks = jnp.arange(NVB, dtype=jnp.int32)
    return (blocks, (2 * blocks + 1) * NAB // (2 * NVB))


def draw_keys(key, part):
    drawn = shared_keys(key)
    return drawn.astype(jnp.bfloat16)


def draw_queries(key, part):
    key = jax.random.fold_in(key, 5)
    drawn = jnp.clip(jax.random.normal(key, (NV, WIDTH), jnp.float32), -6.0, 6.0)
    return drawn.astype(jnp.bfloat16)


def draw_window_low(key, part):
    key = jax.random.fold_in(key, 7)
    blocks, centers = block_centers()
    per_index = NVB // N_VIDEO
    at_edge = (blocks % per_index == 0) | (blocks % per_index == per_index - 1)
    extent = jnp.where(at_edge, 1, jax.random.randint(key, (NVB,), 0, 2))
    return jnp.maximum(centers - extent, 0).astype(jnp.int32)


def draw_window_high(key, part):
    key = jax.random.fold_in(key, 11)
    blocks, centers = block_centers()
    per_index = NVB // N_VIDEO
    at_edge = (blocks % per_index == 0) | (blocks % per_index == per_index - 1)
    extent = jnp.where(at_edge, 1, jax.random.randint(key, (NVB,), 0, 2))
    return jnp.minimum(centers + 1 + extent, NAB).astype(jnp.int32)


def block_levels(own_key, shape, shards, low, largest):
    level = 1.0
    for axis_at, parts in shards:
        draws = jax.random.uniform(jax.random.fold_in(jax.random.fold_in(own_key, 6), axis_at), (parts,), jnp.float32, low / len(shards), largest / len(shards))
        level = level * jnp.repeat(jnp.exp(draws), shape[axis_at] // parts).reshape((-1,) + (1,) * (len(shape) - 1 - axis_at))
    return level


def gaussian(own_key, shape, spread, limit, pieces=(), kind=jnp.bfloat16):
    entries = spread * jax.random.normal(own_key, shape, jnp.float32)
    if pieces:
        entries = entries * block_levels(own_key, shape, pieces, -0.22, 0.18)
    return jnp.clip(entries, -limit, limit).astype(kind)


def setup_inputs(seed: int = 0) -> dict:
    key_of = jax.random.split(jax.random.key(seed), 8)
    queries = draw_queries(jax.random.fold_in(key_of[7], 71), 0)
    keys = draw_keys(jax.random.fold_in(key_of[7], 71), 0)
    values = gaussian(key_of[2], (NA, WIDTH), 1.0, 6.0, ((0, 64),))
    out_grad = gaussian(key_of[3], (NV, WIDTH), 1.0, 6.0, ((0, 512),))
    delta = gaussian(key_of[4], (HEADS, NV), 0.5, 4.0, ((1, 512),), jnp.float32)
    window_low = draw_window_low(jax.random.fold_in(key_of[7], 71), 0)
    window_high = draw_window_high(jax.random.fold_in(key_of[7], 71), 0)
    return {"queries": queries, "keys": keys, "values": values, "out_grad": out_grad, "delta": delta, "window_low": window_low, "window_high": window_high}


masked_score = -1e+30

def reference(queries, keys, values, out_grad, delta, window_low, window_high):
    logit_scale = 1.0 / math.sqrt(HEAD_DIM)
    window_rows = WINDOW * ABLOCK

    def block_step(totals, block_index):
        key_total, value_total = totals
        low_block = window_low[block_index]
        high_block = window_high[block_index]
        first_block = jnp.clip(low_block, 0, NAB - WINDOW).astype(jnp.int32)
        offset = (first_block * ABLOCK).astype(jnp.int32)
        row_begin = (block_index * VBLOCK).astype(jnp.int32)
        query_segment = lax.dynamic_slice_in_dim(queries, row_begin, VBLOCK, 0).astype(jnp.float32).reshape(VBLOCK, HEADS, HEAD_DIM)
        gradient_tile = lax.dynamic_slice_in_dim(out_grad, row_begin, VBLOCK, 0).astype(jnp.float32).reshape(VBLOCK, HEADS, HEAD_DIM)
        key_segment = lax.dynamic_slice_in_dim(keys, offset, window_rows, 0).astype(jnp.float32).reshape(window_rows, HEADS, HEAD_DIM)
        value_segment = lax.dynamic_slice_in_dim(values, offset, window_rows, 0).astype(jnp.float32).reshape(window_rows, HEADS, HEAD_DIM)
        delta_block = lax.dynamic_slice_in_dim(delta, row_begin, VBLOCK, 1)
        blocks_of = first_block + jnp.arange(window_rows, dtype=jnp.int32) // ABLOCK
        inside = (blocks_of >= low_block) & (blocks_of < high_block)
        attention_logits = jnp.einsum('tug,sug->uts', query_segment, key_segment) * logit_scale
        attention_logits = jnp.where(inside, attention_logits, masked_score)
        row_peak = lax.optimization_barrier(jnp.max(attention_logits, axis=2, keepdims=True))
        weights = jnp.where(inside, jnp.exp(attention_logits - row_peak), 0.0)
        probabilities = weights / lax.optimization_barrier(jnp.sum(weights, axis=2, keepdims=True))
        probability_halves = lax.optimization_barrier(probabilities.astype(jnp.bfloat16)).astype(jnp.float32)
        value_portion = jnp.einsum('egc,gex->cex', probability_halves, gradient_tile)
        probability_gradient = jnp.einsum('tug,sug->uts', gradient_tile, value_segment)
        score_grad = probabilities * (probability_gradient - delta_block[:, :, None])
        score_halves = lax.optimization_barrier(score_grad.astype(jnp.bfloat16)).astype(jnp.float32)
        query_portion = jnp.einsum('efr,res->fes', score_halves, key_segment) * logit_scale
        key_portion = jnp.einsum('egc,gex->cex', score_halves, query_segment) * logit_scale
        key_total = lax.dynamic_update_slice_in_dim(key_total, lax.dynamic_slice_in_dim(key_total, offset, window_rows, 0) + key_portion.reshape(window_rows, WIDTH), offset, 0)
        value_total = lax.dynamic_update_slice_in_dim(value_total, lax.dynamic_slice_in_dim(value_total, offset, window_rows, 0) + value_portion.reshape(window_rows, WIDTH), offset, 0)
        return ((key_total, value_total), query_portion.reshape(VBLOCK, WIDTH).astype(jnp.bfloat16))
    empty_sum = jnp.zeros((NA, WIDTH), jnp.float32)
    totals, query_blocks = lax.scan(block_step, (empty_sum, empty_sum), jnp.arange(NVB, dtype=jnp.int32))
    key_total, value_total = totals
    return (query_blocks.reshape(NV, WIDTH), key_total.astype(jnp.bfloat16), value_total.astype(jnp.bfloat16))
```

```python
import math

import jax
import jax.numpy as jnp
from jax import lax
from jax.experimental import pallas as pl
from jax.experimental.pallas import tpu as pltpu
from jax.sharding import PartitionSpec as P

HEAD_DIM = 128
VBLOCK = 64
ABLOCK = 32
SPANS = 64
CHIPS = 4
ROWS = 128
AROWS = 128
GROUP = 384
PARTS = ((0, 32), (32, 64), (96, 32))

MESH = pl.DeviceIdType.MESH
masked_score = -1e30
logit_scale = 1.0 / math.sqrt(HEAD_DIM)


def nt(a, b):
    return lax.dot_general(a, b, (((1,), (1,)), ((), ())), preferred_element_type=jnp.float32)


def nn(a, b):
    return lax.dot_general(a, b, (((1,), (0,)), ((), ())), preferred_element_type=jnp.float32)


def tn(a, b):
    return lax.dot_general(a, b, (((0,), (0,)), ((), ())), preferred_element_type=jnp.float32)


def kernel(
    q_hbm, k_hbm, v_hbm, og_hbm, delta_hbm, low_hbm, high_hbm,
    dq_hbm, dk_hbm, dv_hbm,
    q_buf, og_buf, k_buf, v_buf, delta_buf, win_buf, bias_buf, dq_buf, stage, landed, dk_buf, dv_buf,
    low_smem, high_smem,
    win_sem, delta_sem, rows_sem, audio_sem, out_sem,
    swap_send, swap_recv, small_send, small_recv, halo_send, halo_recv,
    part_send, part_recv, dq_send, dq_recv,
):
    v = lax.axis_index("video")
    a = lax.axis_index("audio")
    y, c = a // 2, a % 2
    other = 1 - c
    before, after = (v + SPANS - 1) % SPANS, (v + 1) % SPANS
    partner = (v, 2 * y + other)

    def group_of(core, g):
        distance = jnp.where(core == 0, 1 - g, 2 + g)
        return (y + distance) % CHIPS

    barrier = pltpu.get_barrier_semaphore()
    greeted = (
        partner,
        (v, 2 * ((y + 3) % CHIPS)),
        (v, 2 * ((y + 2) % CHIPS) + 1),
        (v, 2 * ((y + 1) % CHIPS) + 1),
        (after, y // 2),
        (before, 6 + ((y + 1) % CHIPS) // 2),
    )
    for device in greeted:
        pl.semaphore_signal(barrier, inc=1, device_id=device, device_id_type=MESH)

    @pl.when(y == 0)
    def _():
        pl.semaphore_signal(barrier, inc=1, device_id=(before, c), device_id_type=MESH)

    @pl.when(y == CHIPS - 1)
    def _():
        pl.semaphore_signal(barrier, inc=1, device_id=(after, 6 + c), device_id_type=MESH)

    low_copy = pltpu.make_async_copy(low_hbm, low_smem, win_sem.at[0])
    high_copy = pltpu.make_async_copy(high_hbm, high_smem, win_sem.at[1])
    delta_copy = pltpu.make_async_copy(delta_hbm, delta_buf.at[c], delta_sem)
    low_copy.start()
    high_copy.start()
    delta_copy.start()

    def lanes(k):
        return pl.ds(pl.multiple_of(k * GROUP, GROUP), GROUP)

    def row_copies(g):
        k = group_of(c, g)
        return [
            pltpu.make_async_copy(q_hbm.at[:, lanes(k)], q_buf.at[g, c], rows_sem.at[0, g]),
            pltpu.make_async_copy(og_hbm.at[:, lanes(k)], og_buf.at[g, c], rows_sem.at[1, g]),
        ]

    def audio_copies(g, do):
        k = group_of(c, g)
        for i, (source, target) in enumerate(((k_hbm, k_buf), (v_hbm, v_buf))):
            sem = audio_sem.at[i, g]

            @pl.when(y == 0)
            def _():
                do(pltpu.make_async_copy(source.at[pl.ds(0, 96), lanes(k)], target.at[g, pl.ds(32, 96)], sem))

            @pl.when(y == CHIPS - 1)
            def _():
                do(pltpu.make_async_copy(source.at[pl.ds(160, 96), lanes(k)], target.at[g, pl.ds(0, 96)], sem))

            @pl.when((y > 0) & (y < CHIPS - 1))
            def _():
                first = pl.multiple_of(64 * y - 32, 32)
                do(pltpu.make_async_copy(source.at[pl.ds(first, AROWS), lanes(k)], target.at[g], sem))

    for g in range(2):
        for copy in row_copies(g):
            copy.start()
        audio_copies(g, lambda copy: copy.start())

    edge = (y == 0) | (y == CHIPS - 1)
    pl.semaphore_wait(barrier, 3 + 2 * c + jnp.where(edge, 5, 0))

    def halo_copies(do):
        for g in range(2):
            k = group_of(c, g)
            for i, (source, target) in enumerate(((k_hbm, k_buf), (v_hbm, v_buf))):

                @pl.when(y == 0)
                def _():
                    do(
                        pltpu.make_async_remote_copy(
                            source.at[pl.ds(224, 32), lanes(k)], target.at[g, pl.ds(0, 32)],
                            halo_send.at[i, g], halo_recv.at[i, g], device_id=(after, c), device_id_type=MESH,
                        )
                    )

                @pl.when(y == CHIPS - 1)
                def _():
                    do(
                        pltpu.make_async_remote_copy(
                            source.at[pl.ds(0, 32), lanes(k)], target.at[g, pl.ds(96, 32)],
                            halo_send.at[i, g], halo_recv.at[i, g], device_id=(before, 6 + c), device_id_type=MESH,
                        )
                    )

    halo_copies(lambda copy: copy.start())

    def swap_copies(g, slot):
        k = group_of(other, g)
        return [
            pltpu.make_async_remote_copy(
                source.at[:, lanes(k)], target.at[g, slot], swap_send.at[i, g], swap_recv.at[i, g],
                device_id=partner, device_id_type=MESH,
            )
            for i, (source, target) in enumerate(((q_hbm, q_buf), (og_hbm, og_buf)))
        ]

    for g in range(2):
        for copy in swap_copies(g, c):
            copy.start()

    low_copy.wait()
    high_copy.wait()
    lane = lax.broadcasted_iota(jnp.int32, (8, ROWS), 1)
    row = lax.broadcasted_iota(jnp.int32, (8, ROWS), 0)
    lows = jnp.where(lane < VBLOCK, low_smem[0], low_smem[1])
    highs = jnp.where(lane < VBLOCK, high_smem[0], high_smem[1])
    win_buf[c] = jnp.where(row == 0, lows, highs).astype(jnp.float32)

    def small_copies(slot):
        return [
            pltpu.make_async_remote_copy(
                buf.at[slot], buf.at[slot], small_send.at[i], small_recv.at[i], device_id=partner, device_id_type=MESH
            )
            for i, buf in enumerate((win_buf, delta_buf))
        ]

    small = small_copies(c)
    small[0].start()
    delta_copy.wait()
    small[1].start()
    for copy in small_copies(other):
        copy.wait_recv()

    first_block = (8 * v + 2 * y - 1).astype(jnp.float32)
    blocks = (lax.broadcasted_iota(jnp.int32, (AROWS, ROWS), 0) // ABLOCK).astype(jnp.float32) + first_block
    for slot in range(2):
        inside = (blocks >= win_buf[slot, 0:1, :]) & (blocks < win_buf[slot, 1:2, :])
        bias_buf[:, slot * ROWS : (slot + 1) * ROWS] = jnp.where(inside, 0.0, masked_score)

    half = lax.broadcasted_iota(jnp.int32, (AROWS, HEAD_DIM), 1) < HEAD_DIM // 2

    def part_copies(g, do, do_local):
        k = group_of(c, g)
        for core in range(2):
            for p, (start, size) in enumerate(PARTS):
                span = v
                if p == 0:
                    span = jnp.where(y == 0, before, v)
                if p == 2:
                    span = jnp.where(y == CHIPS - 1, after, v)
                source = stage.at[g, core, :, pl.ds(start, size)]
                target = landed.at[y, :, pl.ds(start, size)]
                here = (span == v) & (2 * k + core == a)

                @pl.when(jnp.logical_not(here))
                def _():
                    do(
                        pltpu.make_async_remote_copy(
                            source, target, part_send.at[g, core, p], part_recv.at[y, p],
                            device_id=(span, 2 * k + core), device_id_type=MESH,
                        )
                    )

                @pl.when(here)
                def _():
                    do_local(pltpu.make_async_copy(source, target, part_recv.at[y, p]))

    def dq_copies(g):
        k = group_of(c, g)
        return (
            pltpu.make_async_copy(dq_buf.at[g, c], dq_hbm.at[:, lanes(k)], out_sem.at[g]),
            pltpu.make_async_remote_copy(
                dq_buf.at[g, other], dq_hbm.at[:, lanes(k)], dq_send.at[g], dq_recv.at[g],
                device_id=partner, device_id_type=MESH,
            ),
        )

    def work(g, carry):
        k = group_of(c, g)
        for copy in row_copies(g):
            copy.wait()
        audio_copies(g, lambda copy: copy.wait())
        for copy in swap_copies(g, other):
            copy.wait_recv()

        @pl.when(edge)
        def _():
            for i, buf in enumerate((k_buf, v_buf)):
                pltpu.make_async_remote_copy(
                    buf.at[g, pl.ds(0, 32)], buf.at[g, pl.ds(0, 32)], halo_send.at[i, g], halo_recv.at[i, g],
                    device_id=partner, device_id_type=MESH,
                ).wait_recv()

        bias = bias_buf[...]
        for i in range(3):
            cols = slice(i * HEAD_DIM, (i + 1) * HEAD_DIM)
            queries = q_buf[g, :, :, cols].reshape(2 * ROWS, HEAD_DIM)
            grads = og_buf[g, :, :, cols].reshape(2 * ROWS, HEAD_DIM)
            keys = k_buf[g, :, cols]
            values = v_buf[g, :, cols]
            delta = jnp.concatenate([delta_buf[slot, pl.ds(3 * k + i, 1), :] for slot in range(2)], axis=1)
            scores = nt(keys, queries) + bias
            peak = jnp.max(scores, axis=0, keepdims=True)
            weights = jnp.exp2((scores - peak) * (logit_scale * math.log2(math.e)))
            probs = weights * (1.0 / jnp.sum(weights, axis=0, keepdims=True))
            prob_grad = nt(values, grads)
            score_half = (probs * (prob_grad - delta)).astype(jnp.bfloat16)
            value_part = nn(probs.astype(jnp.bfloat16), grads)
            key_part = nn(score_half, queries) * logit_scale
            query_part = (tn(score_half, keys) * logit_scale).astype(jnp.bfloat16)
            dq_buf[g, :, :, cols] = query_part.reshape(2, ROWS, HEAD_DIM)
            if i == 1:
                stage[g, 0, 2] = jnp.where(half, key_part, pltpu.roll(value_part, 64, 1)).astype(jnp.bfloat16)
                stage[g, 1, 2] = jnp.where(half, pltpu.roll(key_part, 64, 1), value_part).astype(jnp.bfloat16)
            else:
                stage[g, i // 2, 0] = key_part.astype(jnp.bfloat16)
                stage[g, i // 2, 1] = value_part.astype(jnp.bfloat16)
        part_copies(g, lambda copy: copy.start(), lambda copy: copy.start())
        for copy in dq_copies(g):
            copy.start()
        return carry

    lax.fori_loop(0, 2, work, 0)

    for chip in range(CHIPS):
        for p, (start, size) in enumerate(PARTS):
            part = landed.at[chip, :, pl.ds(start, size)]
            pltpu.make_async_copy(part, part, part_recv.at[chip, p]).wait()
    head_rows = pl.ds(pl.multiple_of(64 * c, 64), 128)
    middle_rows = pl.ds(pl.multiple_of(128 * other, 64), 64)
    for pair in range(2):
        rows = slice(pair * 128, (pair + 1) * 128)
        tiles = []
        for t in range(3):
            blocks_of = []
            for chip in (2 * pair, 2 * pair + 1):
                blocks_of.append(landed[chip, t, 32:64].astype(jnp.float32) + landed[(chip + 3) % 4, t, 96:128].astype(jnp.float32))
                blocks_of.append(landed[chip, t, 64:96].astype(jnp.float32) + landed[(chip + 1) % 4, t, 0:32].astype(jnp.float32))
            tiles.append(jnp.concatenate(blocks_of, axis=0).T.astype(jnp.bfloat16))
        dk_buf[head_rows, rows] = tiles[0]
        dv_buf[head_rows, rows] = tiles[1]
        dk_buf[middle_rows, rows] = tiles[2][0:64]
        dv_buf[middle_rows, rows] = tiles[2][64:128]
    finals = [
        pltpu.make_async_copy(dk_buf, dk_hbm, out_sem.at[2]),
        pltpu.make_async_copy(dv_buf, dv_hbm, out_sem.at[3]),
    ]
    for copy in finals:
        copy.start()

    halo_copies(lambda copy: copy.wait_send())
    for g in range(2):
        for copy in swap_copies(g, c):
            copy.wait_send()
        part_copies(g, lambda copy: copy.wait_send(), lambda copy: None)
        local, remote = dq_copies(g)
        local.wait()
        remote.wait()
    for copy in small:
        copy.wait_send()
    for copy in finals:
        copy.wait()


def on_device(queries, keys, values, out_grad, delta, window_low, window_high):
    any_space = pl.BlockSpec(memory_space=pl.ANY)
    bf16, f32 = jnp.bfloat16, jnp.float32
    dma = pltpu.SemaphoreType.DMA
    query_grad, key_grad, value_grad = pl.pallas_call(
        kernel,
        out_shape=(
            jax.ShapeDtypeStruct((ROWS, 1536), bf16),
            jax.ShapeDtypeStruct((192, 256), bf16),
            jax.ShapeDtypeStruct((192, 256), bf16),
        ),
        in_specs=[any_space] * 7,
        out_specs=(any_space,) * 3,
        scratch_shapes=[
            pltpu.VMEM((2, 2, ROWS, GROUP), bf16),
            pltpu.VMEM((2, 2, ROWS, GROUP), bf16),
            pltpu.VMEM((2, AROWS, GROUP), bf16),
            pltpu.VMEM((2, AROWS, GROUP), bf16),
            pltpu.VMEM((2, 12, ROWS), f32),
            pltpu.VMEM((2, 8, ROWS), f32),
            pltpu.VMEM((AROWS, 2 * ROWS), f32),
            pltpu.VMEM((2, 2, ROWS, GROUP), bf16),
            pltpu.VMEM((2, 2, 3, AROWS, HEAD_DIM), bf16),
            pltpu.VMEM((CHIPS, 3, AROWS, HEAD_DIM), bf16),
            pltpu.VMEM((192, 256), bf16),
            pltpu.VMEM((192, 256), bf16),
            pltpu.SMEM((2,), jnp.int32),
            pltpu.SMEM((2,), jnp.int32),
            dma((2,)),
            dma(()),
            dma((2, 2)),
            dma((2, 2)),
            dma((4,)),
            dma((2, 2)),
            dma((2, 2)),
            dma((2,)),
            dma((2,)),
            dma((2, 2)),
            dma((2, 2)),
            dma((2, 2, 3)),
            dma((CHIPS, 3)),
            dma((2,)),
            dma((2,)),
        ],
        compiler_params=pltpu.CompilerParams(
            collective_id=0, has_side_effects=True, vmem_limit_bytes=60 << 20
        ),
        name="attention_backward",
    )(queries, keys, values, out_grad, delta, window_low, window_high)
    return query_grad, key_grad.T, value_grad.T


def solution(mesh):
    return jax.shard_map(
        on_device,
        mesh=mesh,
        in_specs=(
            P(("video", "audio"), None),
            P("video", None),
            P("video", None),
            P(("video", "audio"), None),
            P(None, ("video", "audio")),
            P(("video", "audio")),
            P(("video", "audio")),
        ),
        out_specs=(P(("video", "audio"), None), P("video", "audio"), P("video", "audio")),
        check_vma=False,
    )
```

```python
import math

import jax
import jax.numpy as jnp
from jax import lax
from jax.experimental import pallas as pl
from jax.experimental.pallas import tpu as pltpu
from jax.sharding import PartitionSpec as P

HEAD_DIM = 128
VBLOCK = 64
ABLOCK = 32
SPANS = 64
CHIPS = 4
ROWS = 128
AROWS = 128
REACH = 96
GROUP = 384
PARTS = ((0, 32), (32, 64), (96, 32))

MESH = pl.DeviceIdType.MESH
masked_score = -1e30
logit_scale = 1.0 / math.sqrt(HEAD_DIM)


def nt(a, b):
    return lax.dot_general(a, b, (((1,), (1,)), ((), ())), preferred_element_type=jnp.float32)


def nn(a, b):
    return lax.dot_general(a, b, (((1,), (0,)), ((), ())), preferred_element_type=jnp.float32)


def tn(a, b):
    return lax.dot_general(a, b, (((0,), (0,)), ((), ())), preferred_element_type=jnp.float32)


def kernel(
    q_hbm, k_hbm, v_hbm, og_hbm, delta_hbm, low_hbm, high_hbm,
    dq_out, landed,
    q_buf, og_buf, k_buf, v_buf, delta_buf, win_buf, bias_buf, dq_buf, key_sum, value_sum, stage,
    low_smem, high_smem,
    win_sem, delta_sem, rows_sem, audio_sem, out_sem,
    swap_send, swap_recv, small_send, small_recv, halo_send, halo_recv,
    part_send, part_recv, dq_send, dq_recv, halo_ready, part_ready,
):
    v = lax.axis_index("video")
    a = lax.axis_index("audio")
    y, c = a // 2, a % 2
    other = 1 - c
    partner = (v, 2 * y + other)
    has_before, has_after = v > 0, v < SPANS - 1
    is_first, is_last = y == 0, y == CHIPS - 1

    def group_of(chip, core, g):
        return (chip + jnp.where(core == 0, 1 - g, 2 + g)) % CHIPS

    def signal(semaphore, device):
        pl.semaphore_signal(semaphore, inc=1, device_id=device, device_id_type=MESH)

    barrier = pltpu.get_barrier_semaphore()
    signal(barrier, partner)

    @pl.when(has_before)
    def _():
        signal(barrier, (v - 1, 6 + ((y + 1) % CHIPS) // 2))

        @pl.when(is_first)
        def _():
            for i in range(4):
                signal(barrier, (v - 1, 4 * c + i))

        @pl.when((is_first | is_last) & (c == 1))
        def _():
            signal(barrier, (v - 1, a))

    signal(barrier, (v, 2 * ((y + 3) % CHIPS)))
    signal(barrier, (v, 2 * ((y + 2) % CHIPS) + 1))
    signal(barrier, (v, 2 * ((y + 1) % CHIPS) + 1))

    low_copy = pltpu.make_async_copy(low_hbm, low_smem, win_sem.at[0])
    high_copy = pltpu.make_async_copy(high_hbm, high_smem, win_sem.at[1])
    delta_copy = pltpu.make_async_copy(delta_hbm, delta_buf.at[c], delta_sem)
    low_copy.start()
    high_copy.start()
    delta_copy.start()

    def lanes(k):
        return pl.ds(pl.multiple_of(k * GROUP, GROUP), GROUP)

    def row_copies(g):
        k = group_of(y, c, g)
        return [
            pltpu.make_async_copy(q_hbm.at[:, lanes(k)], q_buf.at[g, c], rows_sem.at[0, g]),
            pltpu.make_async_copy(og_hbm.at[:, lanes(k)], og_buf.at[g, c], rows_sem.at[1, g]),
        ]

    def audio_copies(g, do):
        k = group_of(y, c, g)
        for i, (source, target) in enumerate(((k_hbm, k_buf), (v_hbm, v_buf))):
            sem = audio_sem.at[i, g]

            @pl.when(is_first)
            def _():
                do(pltpu.make_async_copy(source.at[pl.ds(0, 96), lanes(k)], target.at[g, pl.ds(32, 96)], sem))

            @pl.when(is_last)
            def _():
                do(pltpu.make_async_copy(source.at[pl.ds(160, 96), lanes(k)], target.at[g, pl.ds(0, 96)], sem))

            @pl.when((y > 0) & (y < CHIPS - 1))
            def _():
                first = pl.multiple_of(64 * y - 32, 32)
                do(pltpu.make_async_copy(source.at[pl.ds(first, AROWS), lanes(k)], target.at[g], sem))

    for g in range(2):
        for copy in row_copies(g):
            copy.start()
        audio_copies(g, lambda copy: copy.start())

    @pl.when(jnp.logical_not(has_before))
    def _():
        landed[3, :, 96:128] = jnp.zeros((3, ABLOCK, HEAD_DIM), jnp.bfloat16)

        @pl.when(is_first)
        def _():
            for buf in (k_buf, v_buf):
                buf[:, 0:32] = jnp.zeros((2, ABLOCK, GROUP), jnp.bfloat16)

    @pl.when(jnp.logical_not(has_after))
    def _():
        landed[0, :, 0:32] = jnp.zeros((3, ABLOCK, HEAD_DIM), jnp.bfloat16)

        @pl.when(is_last)
        def _():
            for buf in (k_buf, v_buf):
                buf[:, 96:128] = jnp.zeros((2, ABLOCK, GROUP), jnp.bfloat16)

    pl.semaphore_wait(barrier, 3 + 2 * c + jnp.where(has_after, 1 + jnp.where(is_last, 4 + c, 0) + jnp.where(is_first, c, 0), 0))

    def halo_copies(span, source_row, target_row):
        return [
            pltpu.make_async_remote_copy(
                source.at[pl.ds(source_row, ABLOCK), lanes(group_of(y, c, g))],
                target.at[g, pl.ds(target_row, ABLOCK)],
                halo_send.at[i, g], halo_recv.at[i, g], device_id=(span, a), device_id_type=MESH,
            )
            for g in range(2)
            for i, (source, target) in enumerate(((k_hbm, k_buf), (v_hbm, v_buf)))
        ]

    halo_up = halo_copies(v + 1, 224, 0)
    halo_down = halo_copies(v - 1, 0, 96)

    @pl.when(has_after)
    def _():
        @pl.when(is_last)
        def _():
            signal(halo_ready, (v + 1, a))

        @pl.when(is_first)
        def _():
            for copy in halo_up:
                copy.start()

        signal(part_ready, (v + 1, y // 2))

    def swap_copies(g, slot):
        k = group_of(y, other, g)
        return [
            pltpu.make_async_remote_copy(
                source.at[:, lanes(k)], target.at[g, slot], swap_send.at[i, g], swap_recv.at[i, g],
                device_id=partner, device_id_type=MESH,
            )
            for i, (source, target) in enumerate(((q_hbm, q_buf), (og_hbm, og_buf)))
        ]

    for g in range(2):
        for copy in swap_copies(g, c):
            copy.start()

    low_copy.wait()
    high_copy.wait()
    lane = lax.broadcasted_iota(jnp.int32, (8, ROWS), 1)
    row = lax.broadcasted_iota(jnp.int32, (8, ROWS), 0)
    lows = jnp.where(lane < VBLOCK, low_smem[0], low_smem[1])
    highs = jnp.where(lane < VBLOCK, high_smem[0], high_smem[1])
    win_buf[c] = jnp.where(row == 0, lows, highs).astype(jnp.float32)

    def small_copies(slot):
        return [
            pltpu.make_async_remote_copy(
                buf.at[slot], buf.at[slot], small_send.at[i], small_recv.at[i], device_id=partner, device_id_type=MESH
            )
            for i, buf in enumerate((win_buf, delta_buf))
        ]

    small = small_copies(c)
    small[0].start()
    delta_copy.wait()
    small[1].start()
    for copy in small_copies(other):
        copy.wait_recv()

    first_block = (8 * v + 2 * y - 1).astype(jnp.float32)
    blocks = (lax.broadcasted_iota(jnp.int32, (REACH, ROWS), 0) // ABLOCK).astype(jnp.float32) + first_block
    for slot in range(2):
        inside = (blocks + slot >= win_buf[slot, 0:1, :]) & (blocks + slot < win_buf[slot, 1:2, :])
        bias_buf[slot] = jnp.where(inside, 0.0, masked_score)

    half = lax.broadcasted_iota(jnp.int32, (AROWS, HEAD_DIM), 1) < HEAD_DIM // 2

    def part_copies(p, do, do_local):
        start, size = PARTS[p]
        span, exists = v, True
        if p == 0:
            span, exists = jnp.where(is_first, v - 1, v), has_before | jnp.logical_not(is_first)
        if p == 2:
            span, exists = jnp.where(is_last, v + 1, v), has_after | jnp.logical_not(is_last)
        for g in range(2):
            k = group_of(y, c, g)
            for core in range(2):
                source = stage.at[g, core, :, pl.ds(start, size)]
                target = landed.at[y, :, pl.ds(start, size)]
                here = (span == v) & (2 * k + core == a)
                away = jnp.logical_not(here) if g == 1 and core == 0 else True

                @pl.when(away & exists)
                def _():
                    do(
                        pltpu.make_async_remote_copy(
                            source, target, part_send.at[g, core, p], part_recv.at[y, p],
                            device_id=(span, 2 * k + core), device_id_type=MESH,
                        )
                    )

                if g == 1 and core == 0:

                    @pl.when(here)
                    def _():
                        do_local(pltpu.make_async_copy(source, target, part_recv.at[y, p]))

    def dq_copies(g, slot):
        k = group_of(y, c, g)
        return (
            pltpu.make_async_copy(dq_buf.at[g, slot], dq_out.at[:, lanes(k)], out_sem.at[g]),
            pltpu.make_async_remote_copy(
                dq_buf.at[g, slot], dq_out.at[:, lanes(k)], dq_send.at[g], dq_recv.at[g],
                device_id=partner, device_id_type=MESH,
            ),
        )

    def work(last):
        slot = jnp.where(is_first, 1, 0)
        if last:
            slot = 1 - slot

        @pl.when(slot == c)
        def _():
            for g in range(2):
                for copy in row_copies(g):
                    copy.wait()

        @pl.when(slot != c)
        def _():
            for g in range(2):
                for copy in swap_copies(g, slot):
                    copy.wait_recv()

        if last:

            @pl.when((is_first & has_before) | (is_last & has_after))
            def _():
                for copy in halo_up:
                    copy.wait_recv()
        else:
            for g in range(2):
                audio_copies(g, lambda copy: copy.wait())

        bias = bias_buf[slot]
        reach = pl.ds(pl.multiple_of(ABLOCK * slot, ABLOCK), REACH)
        beyond = pl.ds(pl.multiple_of(REACH * (1 - slot), ABLOCK), ABLOCK)
        heads = [(g, i, slice(i * HEAD_DIM, (i + 1) * HEAD_DIM)) for g in range(2) for i in range(3)]
        scores = [nt(k_buf[g, reach, cols], q_buf[g, slot, :, cols]) for g, _, cols in heads]
        prob_grads = [nt(v_buf[g, reach, cols], og_buf[g, slot, :, cols]) for g, _, cols in heads]
        prob_halves, score_halves = [], []
        for (g, i, _), score, prob_grad in zip(heads, scores, prob_grads):
            delta = delta_buf[slot, pl.ds(3 * group_of(y, c, g) + i, 1), :]
            score = score + bias
            peak = jnp.max(score, axis=0, keepdims=True)
            weights = jnp.exp2((score - peak) * (logit_scale * math.log2(math.e)))
            probs = weights * (1.0 / jnp.sum(weights, axis=0, keepdims=True))
            prob_halves.append(probs.astype(jnp.bfloat16))
            score_halves.append((probs * (prob_grad - delta)).astype(jnp.bfloat16))
        for (g, i, cols), prob_half, score_half in zip(heads, prob_halves, score_halves):
            value_part = nn(prob_half, og_buf[g, slot, :, cols])
            key_part = nn(score_half, q_buf[g, slot, :, cols]) * logit_scale
            if not last:
                for total, part in ((key_sum, key_part), (value_sum, value_part)):
                    total[g, i, reach] = part
                    total[g, i, beyond] = jnp.zeros((ABLOCK, HEAD_DIM), jnp.float32)
                continue
            key_sum[g, i, reach] += key_part
            value_sum[g, i, reach] += value_part
        for g, i, cols in heads if last else []:
            key_part, value_part = key_sum[g, i], value_sum[g, i]
            if i == 1:
                stage[g, 0, 2] = jnp.where(half, key_part, pltpu.roll(value_part, 64, 1)).astype(jnp.bfloat16)
                stage[g, 1, 2] = jnp.where(half, pltpu.roll(key_part, 64, 1), value_part).astype(jnp.bfloat16)
            else:
                stage[g, i // 2, 0] = key_part.astype(jnp.bfloat16)
                stage[g, i // 2, 1] = value_part.astype(jnp.bfloat16)
        for (g, i, cols), score_half in zip(heads, score_halves):
            dq_buf[g, slot, :, cols] = (tn(score_half, k_buf[g, reach, cols]) * logit_scale).astype(jnp.bfloat16)
        if last:
            part_copies(2, lambda copy: copy.start(), lambda copy: copy.start())
            part_copies(1, lambda copy: copy.start(), lambda copy: copy.start())

            @pl.when(is_first & has_before)
            def _():
                pl.semaphore_wait(part_ready, 4)

            part_copies(0, lambda copy: copy.start(), lambda copy: copy.start())

        @pl.when(slot == c)
        def _():
            for g in range(2):
                dq_copies(g, slot)[0].start()

        @pl.when(slot != c)
        def _():
            for g in range(2):
                dq_copies(g, slot)[1].start()

    work(False)

    @pl.when(is_last & has_before)
    def _():
        pl.semaphore_wait(halo_ready, 1)
        for copy in halo_down:
            copy.start()

    work(True)

    @pl.when((is_first & has_after) | (is_last & has_before))
    def _():
        for copy in halo_up:
            copy.wait_send()

    for copy in small:
        copy.wait_send()
    for g in range(2):
        for copy in swap_copies(g, c):
            copy.wait_send()
        dq_copies(g, c)[0].wait()
        dq_copies(g, other)[1].wait()
    for p in range(3):
        part_copies(p, lambda copy: copy.wait_send(), lambda copy: None)
    for chip in range(CHIPS):
        for p, (start, size) in enumerate(PARTS):
            part = landed.at[chip, :, pl.ds(start, size)]
            arrival = pltpu.make_async_copy(part, part, part_recv.at[chip, p])
            if p == 0 and chip == 0:
                pl.when(has_after)(arrival.wait)
            elif p == 2 and chip == CHIPS - 1:
                pl.when(has_before)(arrival.wait)
            else:
                arrival.wait()


def finish(dq_in, landed, dq_hbm, dk_hbm, dv_hbm, dk_buf, dv_buf, sem):
    c = lax.axis_index("audio") % 2
    dq_copy = pltpu.make_async_copy(dq_in, dq_hbm, sem.at[0])
    dq_copy.start()
    head_rows = pl.ds(pl.multiple_of(64 * c, 64), 128)
    middle_rows = pl.ds(pl.multiple_of(128 - 128 * c, 64), 64)
    for pair in range(2):
        rows = slice(pair * 128, (pair + 1) * 128)
        tiles = []
        for t in range(3):
            blocks = []
            for chip in (2 * pair, 2 * pair + 1):
                for own, far_chip, far in ((32, (chip + 3) % CHIPS, 96), (64, (chip + 1) % CHIPS, 0)):
                    own_term = landed[chip, t, own : own + ABLOCK].astype(jnp.float32)
                    blocks.append(own_term + landed[far_chip, t, far : far + ABLOCK].astype(jnp.float32))
            tiles.append(jnp.concatenate(blocks, axis=0).T.astype(jnp.bfloat16))
        dk_buf[head_rows, rows] = tiles[0]
        dv_buf[head_rows, rows] = tiles[1]
        dk_buf[middle_rows, rows] = tiles[2][0:64]
        dv_buf[middle_rows, rows] = tiles[2][64:128]
    copies = [pltpu.make_async_copy(dk_buf, dk_hbm, sem.at[1]), pltpu.make_async_copy(dv_buf, dv_hbm, sem.at[2])]
    for copy in copies:
        copy.start()
    for copy in [dq_copy] + copies:
        copy.wait()


def on_device(queries, keys, values, out_grad, delta, window_low, window_high):
    bf16, f32 = jnp.bfloat16, jnp.float32
    hbm, vmem = pl.BlockSpec(memory_space=pltpu.HBM), pl.BlockSpec(memory_space=pltpu.VMEM)
    dma = pltpu.SemaphoreType.DMA
    arrays = (queries, keys, values, out_grad, delta, window_low, window_high)
    arrays = [pltpu.with_memory_space_constraint(array, pltpu.HBM) for array in arrays]
    query_grad, landed = pl.pallas_call(
        kernel,
        out_shape=(pltpu.VMEM((ROWS, 1536), bf16), pltpu.VMEM((CHIPS, 3, AROWS, HEAD_DIM), bf16)),
        in_specs=[hbm] * 7,
        out_specs=(vmem, vmem),
        scratch_shapes=[
            pltpu.VMEM((2, 2, ROWS, GROUP), bf16),
            pltpu.VMEM((2, 2, ROWS, GROUP), bf16),
            pltpu.VMEM((2, AROWS, GROUP), bf16),
            pltpu.VMEM((2, AROWS, GROUP), bf16),
            pltpu.VMEM((2, 12, ROWS), f32),
            pltpu.VMEM((2, 8, ROWS), f32),
            pltpu.VMEM((2, REACH, ROWS), f32),
            pltpu.VMEM((2, 2, ROWS, GROUP), bf16),
            pltpu.VMEM((2, 3, AROWS, HEAD_DIM), f32),
            pltpu.VMEM((2, 3, AROWS, HEAD_DIM), f32),
            pltpu.VMEM((2, 2, 3, AROWS, HEAD_DIM), bf16),
            pltpu.SMEM((2,), jnp.int32),
            pltpu.SMEM((2,), jnp.int32),
            dma((2,)),
            dma(()),
            dma((2, 2)),
            dma((2, 2)),
            dma((2,)),
            dma((2, 2)),
            dma((2, 2)),
            dma((2,)),
            dma((2,)),
            dma((2, 2)),
            dma((2, 2)),
            dma((2, 2, 3)),
            dma((CHIPS, 3)),
            dma((2,)),
            dma((2,)),
            pltpu.SemaphoreType.REGULAR,
            pltpu.SemaphoreType.REGULAR,
        ],
        compiler_params=pltpu.CompilerParams(
            collective_id=0, has_side_effects=True, vmem_limit_bytes=32 << 20
        ),
        name="attention_backward",
    )(*arrays)
    query_grad, key_grad, value_grad = pl.pallas_call(
        finish,
        out_shape=(
            jax.ShapeDtypeStruct((ROWS, 1536), bf16),
            jax.ShapeDtypeStruct((192, 256), bf16),
            jax.ShapeDtypeStruct((192, 256), bf16),
        ),
        in_specs=[vmem, vmem],
        out_specs=(hbm, hbm, hbm),
        scratch_shapes=[pltpu.VMEM((192, 256), bf16), pltpu.VMEM((192, 256), bf16), dma((3,))],
        compiler_params=pltpu.CompilerParams(vmem_limit_bytes=32 << 20),
        name="sum_partials",
    )(query_grad, landed)
    return query_grad, key_grad.T, value_grad.T


def solution(mesh):
    return jax.shard_map(
        on_device,
        mesh=mesh,
        in_specs=(
            P(("video", "audio"), None),
            P("video", None),
            P("video", None),
            P(("video", "audio"), None),
            P(None, ("video", "audio")),
            P(("video", "audio")),
            P(("video", "audio")),
        ),
        out_specs=(P(("video", "audio"), None), P("video", "audio"), P("video", "audio")),
        check_vma=False,
    )
```

```python
import math

import jax
import jax.numpy as jnp
from jax import lax
from jax.experimental import pallas as pl
from jax.experimental.pallas import tpu as pltpu
from jax.sharding import PartitionSpec as P

HEAD_DIM = 128
VBLOCK = 64
ABLOCK = 32
SPANS = 64
CHIPS = 4
ROWS = 128
AROWS = 128
REACH = 96
GROUP = 384
PARTS = ((0, 32), (32, 64), (96, 32))

MESH = pl.DeviceIdType.MESH
masked_score = -1e30
logit_scale = 1.0 / math.sqrt(HEAD_DIM)


def nt(a, b):
    return lax.dot_general(a, b, (((1,), (1,)), ((), ())), preferred_element_type=jnp.float32)


def nn(a, b):
    return lax.dot_general(a, b, (((1,), (0,)), ((), ())), preferred_element_type=jnp.float32)


def tn(a, b):
    return lax.dot_general(a, b, (((0,), (0,)), ((), ())), preferred_element_type=jnp.float32)


def kernel(
    q_hbm, k_hbm, v_hbm, og_hbm, delta_hbm, low_hbm, high_hbm,
    dq_out, landed,
    q_buf, og_buf, k_buf, v_buf, delta_buf, win_buf, bias_buf, dq_buf, key_sum, value_sum, stage,
    low_smem, high_smem,
    win_sem, delta_sem, rows_sem, audio_sem, out_sem,
    swap_send, swap_recv, small_send, small_recv, halo_send, halo_recv,
    part_send, part_recv, dq_send, dq_recv, part_ready,
):
    v = lax.axis_index("video")
    a = lax.axis_index("audio")
    y, c = a // 2, a % 2
    other = 1 - c
    partner = (v, 2 * y + other)
    has_before, has_after = v > 0, v < SPANS - 1
    is_first, is_last = y == 0, y == CHIPS - 1

    def group_of(chip, core, g):
        return (chip + jnp.where(core == 0, 1 - g, 2 + g)) % CHIPS

    def signal(semaphore, device):
        pl.semaphore_signal(semaphore, inc=1, device_id=device, device_id_type=MESH)

    barrier = pltpu.get_barrier_semaphore()

    @pl.when(is_last & has_after)
    def _():
        signal(barrier, (v + 1, a))

    signal(barrier, partner)

    @pl.when(has_before)
    def _():
        signal(barrier, (v - 1, 6 + ((y + 1) % CHIPS) // 2))

        @pl.when(is_first)
        def _():
            for i in range(4):
                signal(barrier, (v - 1, 4 * c + i))

        @pl.when((is_first | is_last) & (c == 1))
        def _():
            signal(barrier, (v - 1, jnp.where(is_first, 0, a)))

    signal(barrier, (v, 2 * ((y + 3) % CHIPS)))
    signal(barrier, (v, 2 * ((y + 2) % CHIPS) + 1))
    signal(barrier, (v, 2 * ((y + 1) % CHIPS) + 1))

    low_copy = pltpu.make_async_copy(low_hbm, low_smem, win_sem.at[0])
    high_copy = pltpu.make_async_copy(high_hbm, high_smem, win_sem.at[1])
    delta_copy = pltpu.make_async_copy(delta_hbm, delta_buf.at[c], delta_sem)
    low_copy.start()
    high_copy.start()
    delta_copy.start()

    def lanes(k):
        return pl.ds(pl.multiple_of(k * GROUP, GROUP), GROUP)

    def row_copies(g):
        k = group_of(y, c, g)
        return [
            pltpu.make_async_copy(q_hbm.at[:, lanes(k)], q_buf.at[g, c], rows_sem.at[0, g]),
            pltpu.make_async_copy(og_hbm.at[:, lanes(k)], og_buf.at[g, c], rows_sem.at[1, g]),
        ]

    def audio_copies(g, do):
        k = group_of(y, c, g)
        for i, (source, target) in enumerate(((k_hbm, k_buf), (v_hbm, v_buf))):
            sem = audio_sem.at[i, g]

            @pl.when(is_first)
            def _():
                do(pltpu.make_async_copy(source.at[pl.ds(0, 96), lanes(k)], target.at[g, pl.ds(32, 96)], sem))

            @pl.when(is_last)
            def _():
                do(pltpu.make_async_copy(source.at[pl.ds(160, 96), lanes(k)], target.at[g, pl.ds(0, 96)], sem))

            @pl.when((y > 0) & (y < CHIPS - 1))
            def _():
                first = pl.multiple_of(64 * y - 32, 32)
                do(pltpu.make_async_copy(source.at[pl.ds(first, AROWS), lanes(k)], target.at[g], sem))

    for g in range(2):
        for copy in row_copies(g):
            copy.start()
        audio_copies(g, lambda copy: copy.start())

    @pl.when(jnp.logical_not(has_before))
    def _():
        landed[3, :, 96:128] = jnp.zeros((3, ABLOCK, HEAD_DIM), jnp.bfloat16)

        @pl.when(is_first)
        def _():
            for buf in (k_buf, v_buf):
                buf[:, 0:32] = jnp.zeros((2, ABLOCK, GROUP), jnp.bfloat16)

    @pl.when(jnp.logical_not(has_after))
    def _():
        landed[0, :, 0:32] = jnp.zeros((3, ABLOCK, HEAD_DIM), jnp.bfloat16)

        @pl.when(is_last)
        def _():
            for buf in (k_buf, v_buf):
                buf[:, 96:128] = jnp.zeros((2, ABLOCK, GROUP), jnp.bfloat16)

    from_after = 1 + jnp.where(is_last, 4 + c, 0) + jnp.where(is_first, other, 0)
    from_before = jnp.where(is_last, 1, 0)
    pl.semaphore_wait(barrier, 3 + 2 * c + jnp.where(has_after, from_after, 0) + jnp.where(has_before, from_before, 0))

    def halo_copies(span, core, source_row, target_row):
        return [
            pltpu.make_async_remote_copy(
                source.at[pl.ds(source_row, ABLOCK), lanes(group_of(y, core, g))],
                target.at[g, pl.ds(target_row, ABLOCK)],
                halo_send.at[i, g, core], halo_recv.at[i, g],
                device_id=(span, 2 * y + core), device_id_type=MESH,
            )
            for g in range(2)
            for i, (source, target) in enumerate(((k_hbm, k_buf), (v_hbm, v_buf)))
        ]

    halo_down = halo_copies(v - 1, c, 0, 96)

    @pl.when(is_last & has_before)
    def _():
        for copy in halo_down:
            copy.start()

    @pl.when(has_after)
    def _():
        @pl.when(is_first & (c == 0))
        def _():
            for g in range(2):
                for core in range(2):
                    for copy in halo_copies(v + 1, core, 224, 0)[2 * g : 2 * g + 2]:
                        copy.start()

        signal(part_ready, (v + 1, y // 2))

    def swap_copies(g, slot):
        k = group_of(y, other, g)
        return [
            pltpu.make_async_remote_copy(
                source.at[:, lanes(k)], target.at[g, slot], swap_send.at[i, g], swap_recv.at[i, g],
                device_id=partner, device_id_type=MESH,
            )
            for i, (source, target) in enumerate(((q_hbm, q_buf), (og_hbm, og_buf)))
        ]

    for g in range(2):
        for copy in swap_copies(g, c):
            copy.start()

    low_copy.wait()
    high_copy.wait()
    lane = lax.broadcasted_iota(jnp.int32, (8, ROWS), 1)
    row = lax.broadcasted_iota(jnp.int32, (8, ROWS), 0)
    lows = jnp.where(lane < VBLOCK, low_smem[0], low_smem[1])
    highs = jnp.where(lane < VBLOCK, high_smem[0], high_smem[1])
    win_buf[c] = jnp.where(row == 0, lows, highs).astype(jnp.float32)

    def small_copies(slot):
        return [
            pltpu.make_async_remote_copy(
                buf.at[slot], buf.at[slot], small_send.at[i], small_recv.at[i], device_id=partner, device_id_type=MESH
            )
            for i, buf in enumerate((win_buf, delta_buf))
        ]

    small = small_copies(c)
    small[0].start()
    delta_copy.wait()
    small[1].start()
    for copy in small_copies(other):
        copy.wait_recv()

    first_block = (8 * v + 2 * y - 1).astype(jnp.float32)
    blocks = (lax.broadcasted_iota(jnp.int32, (REACH, ROWS), 0) // ABLOCK).astype(jnp.float32) + first_block
    for slot in range(2):
        inside = (blocks + slot >= win_buf[slot, 0:1, :]) & (blocks + slot < win_buf[slot, 1:2, :])
        bias_buf[slot] = jnp.where(inside, 0.0, masked_score)

    half = lax.broadcasted_iota(jnp.int32, (AROWS, HEAD_DIM), 1) < HEAD_DIM // 2

    def part_copies(p, do, do_local):
        start, size = PARTS[p]
        span, exists = v, True
        if p == 0:
            span, exists = jnp.where(is_first, v - 1, v), has_before | jnp.logical_not(is_first)
        if p == 2:
            span, exists = jnp.where(is_last, v + 1, v), has_after | jnp.logical_not(is_last)
        for g in range(2):
            k = group_of(y, c, g)
            for core in range(2):
                source = stage.at[g, core, :, pl.ds(start, size)]
                target = landed.at[y, :, pl.ds(start, size)]
                here = (span == v) & (2 * k + core == a)
                away = jnp.logical_not(here) if g == 1 and core == 0 else True

                @pl.when(away & exists)
                def _():
                    do(
                        pltpu.make_async_remote_copy(
                            source, target, part_send.at[g, core, p], part_recv.at[y, p],
                            device_id=(span, 2 * k + core), device_id_type=MESH,
                        )
                    )

                if g == 1 and core == 0:

                    @pl.when(here)
                    def _():
                        do_local(pltpu.make_async_copy(source, target, part_recv.at[y, p]))

    def dq_copies(g, slot):
        k = group_of(y, c, g)
        return (
            pltpu.make_async_copy(dq_buf.at[g, slot], dq_out.at[:, lanes(k)], out_sem.at[g]),
            pltpu.make_async_remote_copy(
                dq_buf.at[g, slot], dq_out.at[:, lanes(k)], dq_send.at[g], dq_recv.at[g],
                device_id=partner, device_id_type=MESH,
            ),
        )

    def work(last):
        slot = jnp.where(is_first, 1, 0)
        if last:
            slot = 1 - slot

        @pl.when(slot == c)
        def _():
            for g in range(2):
                for copy in row_copies(g):
                    copy.wait()

        @pl.when(slot != c)
        def _():
            for g in range(2):
                for copy in swap_copies(g, slot):
                    copy.wait_recv()

        if last:

            @pl.when((is_first & has_before) | (is_last & has_after))
            def _():
                for copy in halo_down:
                    copy.wait_recv()
        else:
            for g in range(2):
                audio_copies(g, lambda copy: copy.wait())

        bias = bias_buf[slot]
        reach = pl.ds(pl.multiple_of(ABLOCK * slot, ABLOCK), REACH)
        beyond = pl.ds(pl.multiple_of(REACH * (1 - slot), ABLOCK), ABLOCK)
        heads = [(g, i, slice(i * HEAD_DIM, (i + 1) * HEAD_DIM)) for g in range(2) for i in range(3)]
        scores = [nt(k_buf[g, reach, cols], q_buf[g, slot, :, cols]) for g, _, cols in heads]
        prob_grads = [nt(v_buf[g, reach, cols], og_buf[g, slot, :, cols]) for g, _, cols in heads]
        prob_halves, score_halves = [], []
        for (g, i, _), score, prob_grad in zip(heads, scores, prob_grads):
            delta = delta_buf[slot, pl.ds(3 * group_of(y, c, g) + i, 1), :]
            score = score + bias
            peak = jnp.max(score, axis=0, keepdims=True)
            weights = jnp.exp2((score - peak) * (logit_scale * math.log2(math.e)))
            probs = weights * (1.0 / jnp.sum(weights, axis=0, keepdims=True))
            prob_halves.append(probs.astype(jnp.bfloat16))
            score_halves.append((probs * (prob_grad - delta)).astype(jnp.bfloat16))
        for (g, i, cols), prob_half, score_half in zip(heads, prob_halves, score_halves):
            value_part = nn(prob_half, og_buf[g, slot, :, cols])
            key_part = nn(score_half, q_buf[g, slot, :, cols]) * logit_scale
            if not last:
                for total, part in ((key_sum, key_part), (value_sum, value_part)):
                    total[g, i, reach] = part
                    total[g, i, beyond] = jnp.zeros((ABLOCK, HEAD_DIM), jnp.float32)
                continue
            key_sum[g, i, reach] += key_part
            value_sum[g, i, reach] += value_part
        for g, i, cols in heads if last else []:
            key_part, value_part = key_sum[g, i], value_sum[g, i]
            if i == 1:
                stage[g, 0, 2] = jnp.where(half, key_part, pltpu.roll(value_part, 64, 1)).astype(jnp.bfloat16)
                stage[g, 1, 2] = jnp.where(half, pltpu.roll(key_part, 64, 1), value_part).astype(jnp.bfloat16)
            else:
                stage[g, i // 2, 0] = key_part.astype(jnp.bfloat16)
                stage[g, i // 2, 1] = value_part.astype(jnp.bfloat16)
        for (g, i, cols), score_half in zip(heads, score_halves):
            dq_buf[g, slot, :, cols] = (tn(score_half, k_buf[g, reach, cols]) * logit_scale).astype(jnp.bfloat16)
        if last:
            part_copies(2, lambda copy: copy.start(), lambda copy: copy.start())
            part_copies(1, lambda copy: copy.start(), lambda copy: copy.start())
        @pl.when(slot == c)
        def _():
            for g in range(2):
                dq_copies(g, slot)[0].start()

        @pl.when(slot != c)
        def _():
            for g in range(2):
                dq_copies(g, slot)[1].start()

        if last:

            @pl.when(is_first & has_before)
            def _():
                pl.semaphore_wait(part_ready, 4)

            part_copies(0, lambda copy: copy.start(), lambda copy: copy.start())

    work(False)

    work(True)

    @pl.when(is_last & has_before)
    def _():
        for copy in halo_down:
            copy.wait_send()

    @pl.when(is_first & has_after & (c == 0))
    def _():
        for core in range(2):
            for copy in halo_copies(v + 1, core, 224, 0):
                copy.wait_send()

    for copy in small:
        copy.wait_send()
    for g in range(2):
        for copy in swap_copies(g, c):
            copy.wait_send()
        dq_copies(g, c)[0].wait()
        dq_copies(g, other)[1].wait()
    for p in range(3):
        part_copies(p, lambda copy: copy.wait_send(), lambda copy: None)
    for chip in range(CHIPS):
        for p, (start, size) in enumerate(PARTS):
            part = landed.at[chip, :, pl.ds(start, size)]
            arrival = pltpu.make_async_copy(part, part, part_recv.at[chip, p])
            if p == 0 and chip == 0:
                pl.when(has_after)(arrival.wait)
            elif p == 2 and chip == CHIPS - 1:
                pl.when(has_before)(arrival.wait)
            else:
                arrival.wait()


def finish(dq_in, landed, dq_hbm, dk_hbm, dv_hbm, dk_buf, dv_buf, sem):
    c = lax.axis_index("audio") % 2
    dq_copy = pltpu.make_async_copy(dq_in, dq_hbm, sem.at[0])
    dq_copy.start()
    head_rows = pl.ds(pl.multiple_of(64 * c, 64), 128)
    middle_rows = pl.ds(pl.multiple_of(128 - 128 * c, 64), 64)
    for pair in range(2):
        rows = slice(pair * 128, (pair + 1) * 128)
        tiles = []
        for t in range(3):
            blocks = []
            for chip in (2 * pair, 2 * pair + 1):
                for own, far_chip, far in ((32, (chip + 3) % CHIPS, 96), (64, (chip + 1) % CHIPS, 0)):
                    own_term = landed[chip, t, own : own + ABLOCK].astype(jnp.float32)
                    blocks.append(own_term + landed[far_chip, t, far : far + ABLOCK].astype(jnp.float32))
            tiles.append(jnp.concatenate(blocks, axis=0).T.astype(jnp.bfloat16))
        dk_buf[head_rows, rows] = tiles[0]
        dv_buf[head_rows, rows] = tiles[1]
        dk_buf[middle_rows, rows] = tiles[2][0:64]
        dv_buf[middle_rows, rows] = tiles[2][64:128]
    copies = [pltpu.make_async_copy(dk_buf, dk_hbm, sem.at[1]), pltpu.make_async_copy(dv_buf, dv_hbm, sem.at[2])]
    for copy in copies:
        copy.start()
    for copy in [dq_copy] + copies:
        copy.wait()


def on_device(queries, keys, values, out_grad, delta, window_low, window_high):
    bf16, f32 = jnp.bfloat16, jnp.float32
    hbm, vmem = pl.BlockSpec(memory_space=pltpu.HBM), pl.BlockSpec(memory_space=pltpu.VMEM)
    dma = pltpu.SemaphoreType.DMA
    arrays = (queries, keys, values, out_grad, delta, window_low, window_high)
    arrays = [pltpu.with_memory_space_constraint(array, pltpu.HBM) for array in arrays]
    query_grad, landed = pl.pallas_call(
        kernel,
        out_shape=(pltpu.VMEM((ROWS, 1536), bf16), pltpu.VMEM((CHIPS, 3, AROWS, HEAD_DIM), bf16)),
        in_specs=[hbm] * 7,
        out_specs=(vmem, vmem),
        scratch_shapes=[
            pltpu.VMEM((2, 2, ROWS, GROUP), bf16),
            pltpu.VMEM((2, 2, ROWS, GROUP), bf16),
            pltpu.VMEM((2, AROWS, GROUP), bf16),
            pltpu.VMEM((2, AROWS, GROUP), bf16),
            pltpu.VMEM((2, 12, ROWS), f32),
            pltpu.VMEM((2, 8, ROWS), f32),
            pltpu.VMEM((2, REACH, ROWS), f32),
            pltpu.VMEM((2, 2, ROWS, GROUP), bf16),
            pltpu.VMEM((2, 3, AROWS, HEAD_DIM), f32),
            pltpu.VMEM((2, 3, AROWS, HEAD_DIM), f32),
            pltpu.VMEM((2, 2, 3, AROWS, HEAD_DIM), bf16),
            pltpu.SMEM((2,), jnp.int32),
            pltpu.SMEM((2,), jnp.int32),
            dma((2,)),
            dma(()),
            dma((2, 2)),
            dma((2, 2)),
            dma((2,)),
            dma((2, 2)),
            dma((2, 2)),
            dma((2,)),
            dma((2,)),
            dma((2, 2, 2)),
            dma((2, 2)),
            dma((2, 2, 3)),
            dma((CHIPS, 3)),
            dma((2,)),
            dma((2,)),
            pltpu.SemaphoreType.REGULAR,
        ],
        compiler_params=pltpu.CompilerParams(
            collective_id=0, has_side_effects=True, vmem_limit_bytes=32 << 20
        ),
        name="attention_backward",
    )(*arrays)
    query_grad, key_grad, value_grad = pl.pallas_call(
        finish,
        out_shape=(
            jax.ShapeDtypeStruct((ROWS, 1536), bf16),
            jax.ShapeDtypeStruct((192, 256), bf16),
            jax.ShapeDtypeStruct((192, 256), bf16),
        ),
        in_specs=[vmem, vmem],
        out_specs=(hbm, hbm, hbm),
        scratch_shapes=[pltpu.VMEM((192, 256), bf16), pltpu.VMEM((192, 256), bf16), dma((3,))],
        compiler_params=pltpu.CompilerParams(vmem_limit_bytes=32 << 20),
        name="sum_partials",
    )(query_grad, landed)
    return query_grad, key_grad.T, value_grad.T


def solution(mesh):
    return jax.shard_map(
        on_device,
        mesh=mesh,
        in_specs=(
            P(("video", "audio"), None),
            P("video", None),
            P("video", None),
            P(("video", "audio"), None),
            P(None, ("video", "audio")),
            P(("video", "audio")),
            P(("video", "audio")),
        ),
        out_specs=(P(("video", "audio"), None), P("video", "audio"), P("video", "audio")),
        check_vma=False,
    )
```

```python
import math

import jax
import jax.numpy as jnp
from jax import lax
from jax.experimental import pallas as pl
from jax.experimental.pallas import tpu as pltpu
from jax.sharding import PartitionSpec as P

HEAD_DIM = 128
VBLOCK = 64
ABLOCK = 32
SPANS = 64
CHIPS = 4
ROWS = 128
AROWS = 128
REACH = 96
GROUP = 384
PARTS = ((0, 32), (32, 64), (96, 32))

MESH = pl.DeviceIdType.MESH
masked_score = -1e30
logit_scale = 1.0 / math.sqrt(HEAD_DIM)


def nt(a, b):
    return lax.dot_general(a, b, (((1,), (1,)), ((), ())), preferred_element_type=jnp.float32)


def nn(a, b):
    return lax.dot_general(a, b, (((1,), (0,)), ((), ())), preferred_element_type=jnp.float32)


def tn(a, b):
    return lax.dot_general(a, b, (((0,), (0,)), ((), ())), preferred_element_type=jnp.float32)


def kernel(
    q_hbm, k_hbm, v_hbm, og_hbm, delta_hbm, low_hbm, high_hbm,
    dq_out, landed,
    q_buf, og_buf, k_buf, v_buf, edge_buf, delta_buf, win_buf, bias_buf, dq_buf, key_sum, value_sum, stage,
    low_smem, high_smem,
    win_sem, delta_sem, rows_sem, audio_sem, edge_sem, out_sem,
    swap_send, swap_recv, small_send, small_recv, halo_send, halo_recv,
    part_send, part_recv, dq_send, dq_recv, part_ready,
):
    v = lax.axis_index("video")
    a = lax.axis_index("audio")
    y, c = a // 2, a % 2
    other = 1 - c
    partner = (v, 2 * y + other)
    has_before, has_after = v > 0, v < SPANS - 1
    is_first, is_last = y == 0, y == CHIPS - 1

    def group_of(chip, core, g):
        return (chip + jnp.where(core == 0, 1 - g, 2 + g)) % CHIPS

    def signal(semaphore, device):
        pl.semaphore_signal(semaphore, inc=1, device_id=device, device_id_type=MESH)

    barrier = pltpu.get_barrier_semaphore()

    @pl.when(is_last & has_after)
    def _():
        signal(barrier, (v + 1, a))

    signal(barrier, partner)

    @pl.when(has_before)
    def _():
        signal(barrier, (v - 1, 6 + ((y + 1) % CHIPS) // 2))

        @pl.when(is_first)
        def _():
            for i in range(4):
                signal(barrier, (v - 1, 4 * c + i))

        @pl.when((is_first | is_last) & (c == 1))
        def _():
            signal(barrier, (v - 1, jnp.where(is_first, 0, a)))

    signal(barrier, (v, 2 * ((y + 3) % CHIPS)))
    signal(barrier, (v, 2 * ((y + 2) % CHIPS) + 1))
    signal(barrier, (v, 2 * ((y + 1) % CHIPS) + 1))

    low_copy = pltpu.make_async_copy(low_hbm, low_smem, win_sem.at[0])
    high_copy = pltpu.make_async_copy(high_hbm, high_smem, win_sem.at[1])
    delta_copy = pltpu.make_async_copy(delta_hbm, delta_buf.at[c], delta_sem)
    low_copy.start()
    high_copy.start()
    delta_copy.start()

    def lanes(k):
        return pl.ds(pl.multiple_of(k * GROUP, GROUP), GROUP)

    def row_copies(g):
        k = group_of(y, c, g)
        return [
            pltpu.make_async_copy(q_hbm.at[:, lanes(k)], q_buf.at[g, c], rows_sem.at[0, g]),
            pltpu.make_async_copy(og_hbm.at[:, lanes(k)], og_buf.at[g, c], rows_sem.at[1, g]),
        ]

    def audio_copies(g, do):
        k = group_of(y, c, g)
        for i, (source, target) in enumerate(((k_hbm, k_buf), (v_hbm, v_buf))):
            sem = audio_sem.at[i, g]

            @pl.when(is_first)
            def _():
                do(pltpu.make_async_copy(source.at[pl.ds(0, 96), lanes(k)], target.at[g, pl.ds(32, 96)], sem))

            @pl.when(is_last)
            def _():
                do(pltpu.make_async_copy(source.at[pl.ds(160, 96), lanes(k)], target.at[g, pl.ds(0, 96)], sem))

            @pl.when((y > 0) & (y < CHIPS - 1))
            def _():
                first = pl.multiple_of(64 * y - 32, 32)
                do(pltpu.make_async_copy(source.at[pl.ds(first, AROWS), lanes(k)], target.at[g], sem))

    edge_copies = [
        pltpu.make_async_copy(
            source.at[pl.ds(0, ABLOCK), lanes(group_of(y, c, g))], edge_buf.at[i, g], edge_sem.at[i, g]
        )
        for i, source in enumerate((k_hbm, v_hbm))
        for g in range(2)
    ]
    sends_down = is_last & has_before

    @pl.when(sends_down)
    def _():
        for copy in edge_copies:
            copy.start()

    for g in range(2):
        for copy in row_copies(g):
            copy.start()
        audio_copies(g, lambda copy: copy.start())

    @pl.when(sends_down)
    def _():
        for copy in edge_copies:
            copy.wait()

    @pl.when(jnp.logical_not(has_before))
    def _():
        landed[3, :, 96:128] = jnp.zeros((3, ABLOCK, HEAD_DIM), jnp.bfloat16)

        @pl.when(is_first)
        def _():
            for buf in (k_buf, v_buf):
                buf[:, 0:32] = jnp.zeros((2, ABLOCK, GROUP), jnp.bfloat16)

    @pl.when(jnp.logical_not(has_after))
    def _():
        landed[0, :, 0:32] = jnp.zeros((3, ABLOCK, HEAD_DIM), jnp.bfloat16)

        @pl.when(is_last)
        def _():
            for buf in (k_buf, v_buf):
                buf[:, 96:128] = jnp.zeros((2, ABLOCK, GROUP), jnp.bfloat16)

    from_after = 1 + jnp.where(is_last, 4 + c, 0) + jnp.where(is_first, other, 0)
    from_before = jnp.where(is_last, 1, 0)
    pl.semaphore_wait(barrier, 3 + 2 * c + jnp.where(has_after, from_after, 0) + jnp.where(has_before, from_before, 0))

    def up_copies(i, core):
        return [
            pltpu.make_async_remote_copy(
                (k_hbm, v_hbm)[i].at[pl.ds(224, ABLOCK), lanes(group_of(0, core, g))],
                (k_buf, v_buf)[i].at[g, pl.ds(0, ABLOCK)],
                halo_send.at[i, g, core], halo_recv.at[i, g], device_id=(v + 1, core), device_id_type=MESH,
            )
            for g in range(2)
        ]

    halo_up = (
        (0, [copy for pair in zip(up_copies(0, 0), up_copies(0, 1)) for copy in pair]),
        (1, up_copies(1, 0)),
        (CHIPS - 1, up_copies(1, 1)),
    )
    halo_down = [
        pltpu.make_async_remote_copy(
            edge_buf.at[i, g], buf.at[g, pl.ds(96, ABLOCK)], halo_send.at[i, g, c], halo_recv.at[i, g],
            device_id=(v - 1, a), device_id_type=MESH,
        )
        for g in range(2)
        for i, buf in enumerate((k_buf, v_buf))
    ]

    @pl.when(sends_down)
    def _():
        for copy in halo_down:
            copy.start()

    @pl.when(has_after)
    def _():
        for chip, copies in halo_up:

            @pl.when((y == chip) & (c == 0))
            def _():
                for copy in copies:
                    copy.start()

        signal(part_ready, (v + 1, y // 2))

    def swap_copies(g, slot):
        k = group_of(y, other, g)
        return [
            pltpu.make_async_remote_copy(
                source.at[:, lanes(k)], target.at[g, slot], swap_send.at[i, g], swap_recv.at[i, g],
                device_id=partner, device_id_type=MESH,
            )
            for i, (source, target) in enumerate(((q_hbm, q_buf), (og_hbm, og_buf)))
        ]

    for g in range(2):
        for copy in swap_copies(g, c):
            copy.start()

    low_copy.wait()
    high_copy.wait()
    lane = lax.broadcasted_iota(jnp.int32, (8, ROWS), 1)
    row = lax.broadcasted_iota(jnp.int32, (8, ROWS), 0)
    lows = jnp.where(lane < VBLOCK, low_smem[0], low_smem[1])
    highs = jnp.where(lane < VBLOCK, high_smem[0], high_smem[1])
    win_buf[c] = jnp.where(row == 0, lows, highs).astype(jnp.float32)

    def small_copies(slot):
        return [
            pltpu.make_async_remote_copy(
                buf.at[slot], buf.at[slot], small_send.at[i], small_recv.at[i], device_id=partner, device_id_type=MESH
            )
            for i, buf in enumerate((win_buf, delta_buf))
        ]

    small = small_copies(c)
    small[0].start()
    delta_copy.wait()
    small[1].start()
    for copy in small_copies(other):
        copy.wait_recv()

    row = lax.broadcasted_iota(jnp.int32, (REACH, ROWS), 0)
    for slot in range(2):
        blocks = 8 * v + 2 * y + jnp.where(row < 2 * ABLOCK, row // ABLOCK, 3 * slot - 1)
        blocks = blocks.astype(jnp.float32)
        inside = (blocks >= win_buf[slot, 0:1, :]) & (blocks < win_buf[slot, 1:2, :])
        bias_buf[slot] = jnp.where(inside, 0.0, masked_score)

    def part_copies(slot, groups, do, do_local):
        if slot is None:
            p, start, size, span, exists = 1, ABLOCK, 2 * ABLOCK, v, True
        else:
            p, start, size = 2 * slot, pl.multiple_of(REACH * slot, ABLOCK), ABLOCK
            down, up = is_first & (slot == 0), is_last & (slot == 1)
            span = v - jnp.where(down, 1, 0) + jnp.where(up, 1, 0)
            exists = jnp.logical_not(down & jnp.logical_not(has_before)) & jnp.logical_not(up & jnp.logical_not(has_after))
        for g in groups:
            k = group_of(y, c, g)
            for core in range(2):
                source = stage.at[g, core, :, pl.ds(start, size)]
                target = landed.at[y, :, pl.ds(start, size)]
                here = (span == v) & (2 * k + core == a)
                away = jnp.logical_not(here) if g == 1 and core == 0 else True

                @pl.when(away & exists)
                def _():
                    do(
                        pltpu.make_async_remote_copy(
                            source, target, part_send.at[g, core, p], part_recv.at[y, p],
                            device_id=(span, 2 * k + core), device_id_type=MESH,
                        )
                    )

                if g == 1 and core == 0:

                    @pl.when(here)
                    def _():
                        do_local(pltpu.make_async_copy(source, target, part_recv.at[y, p]))

    def dq_copies(g, slot):
        k = group_of(y, c, g)
        return (
            pltpu.make_async_copy(dq_buf.at[g, slot], dq_out.at[:, lanes(k)], out_sem.at[g]),
            pltpu.make_async_remote_copy(
                dq_buf.at[g, slot], dq_out.at[:, lanes(k)], dq_send.at[g], dq_recv.at[g],
                device_id=partner, device_id_type=MESH,
            ),
        )

    def work(last):
        slot = jnp.where(is_first, 1, 0)
        if last:
            slot = 1 - slot

        @pl.when(slot == c)
        def _():
            for g in range(2):
                for copy in row_copies(g):
                    copy.wait()

        @pl.when(slot != c)
        def _():
            for g in range(2):
                for copy in swap_copies(g, slot):
                    copy.wait_recv()

        def halo_wait(i, buf, groups):
            if last:

                @pl.when((is_first & has_before) | (is_last & has_after))
                def _():
                    for g in groups:
                        part = buf.at[g, pl.ds(0, ABLOCK)]
                        pltpu.make_async_remote_copy(
                            part, part, halo_send.at[i, g, 0], halo_recv.at[i, g], device_id=partner, device_id_type=MESH
                        ).wait_recv()

        def start(copy):
            copy.start()

        def put(heads, rows, key_parts, value_parts):
            for (g, i, _), key_part, value_part in zip(heads, key_parts, value_parts):
                if i == 1:
                    half = lax.broadcasted_iota(jnp.int32, key_part.shape, 1) < HEAD_DIM // 2
                    stage[g, 0, 2, rows] = jnp.where(half, key_part, pltpu.roll(value_part, 64, 1)).astype(jnp.bfloat16)
                    stage[g, 1, 2, rows] = jnp.where(half, pltpu.roll(key_part, 64, 1), value_part).astype(jnp.bfloat16)
                else:
                    stage[g, i // 2, 0, rows] = key_part.astype(jnp.bfloat16)
                    stage[g, i // 2, 1, rows] = value_part.astype(jnp.bfloat16)

        if not last:
            for g in range(2):
                audio_copies(g, lambda copy: copy.wait())
        middle = pl.ds(ABLOCK, 2 * ABLOCK)
        alone = pl.ds(pl.multiple_of(REACH * slot, ABLOCK), ABLOCK)
        bias = bias_buf[slot]

        def gradients(groups):
            heads = [(g, i, slice(i * HEAD_DIM, (i + 1) * HEAD_DIM)) for g in groups for i in range(3)]
            deltas = [delta_buf[slot, pl.ds(3 * group_of(y, c, g) + i, 1), :] for g, i, _ in heads]

            halo_wait(0, k_buf, groups)
            keys = [jnp.concatenate([k_buf[g, middle, cols], k_buf[g, alone, cols]], axis=0) for g, _, cols in heads]
            scores = [nt(key, q_buf[g, slot, :, cols]) for key, (g, _, cols) in zip(keys, heads)]
            prob_grads = [nt(v_buf[g, middle, cols], og_buf[g, slot, :, cols]) for g, _, cols in heads]
            probs, prob_halves, middle_halves = [], [], []
            for score, prob_grad, delta in zip(scores, prob_grads, deltas):
                score = score + bias
                peak = jnp.max(score, axis=0, keepdims=True)
                weights = jnp.exp2((score - peak) * (logit_scale * math.log2(math.e)))
                prob = weights * (1.0 / jnp.sum(weights, axis=0, keepdims=True))
                probs.append(prob[64:96])
                prob_halves.append(prob.astype(jnp.bfloat16))
                middle_halves.append((prob[0:64] * (prob_grad - delta)).astype(jnp.bfloat16))
            value_parts = [nn(prob, og_buf[g, slot, :, cols]) for prob, (g, _, cols) in zip(prob_halves, heads)]
            key_parts = [nn(score, q_buf[g, slot, :, cols]) * logit_scale for score, (g, _, cols) in zip(middle_halves, heads)]
            if last:
                key_parts = [part + key_sum[g, i] for part, (g, i, _) in zip(key_parts, heads)]
                middle_values = [part[0:64] + value_sum[g, i] for part, (g, i, _) in zip(value_parts, heads)]
                put(heads, middle, key_parts, middle_values)

                @pl.when(jnp.logical_not(is_last))
                def _():
                    part_copies(None, groups, start, start)
            else:
                for key_part, value_part, (g, i, _) in zip(key_parts, value_parts, heads):
                    key_sum[g, i] = key_part
                    value_sum[g, i] = value_part[0:64]

            halo_wait(1, v_buf, groups)
            prob_grads = [nt(v_buf[g, alone, cols], og_buf[g, slot, :, cols]) for g, _, cols in heads]
            alone_halves = [
                (prob * (prob_grad - delta)).astype(jnp.bfloat16) for prob, prob_grad, delta in zip(probs, prob_grads, deltas)
            ]
            key_parts = [nn(score, q_buf[g, slot, :, cols]) * logit_scale for score, (g, _, cols) in zip(alone_halves, heads)]
            put(heads, alone, key_parts, [part[64:96] for part in value_parts])
            if last:

                @pl.when(is_first & has_before & (0 in groups))
                def _():
                    pl.semaphore_wait(part_ready, 4)

            part_copies(slot, groups, start, start)
            if last:

                @pl.when(is_last)
                def _():
                    part_copies(None, groups, start, start)
            return list(zip(heads, keys, middle_halves, alone_halves))

        done = gradients((0,)) + gradients((1,)) if last else gradients((0, 1))
        for (g, _, cols), key, first, second in done:
            score_half = jnp.concatenate([first, second], axis=0)
            dq_buf[g, slot, :, cols] = (tn(score_half, key) * logit_scale).astype(jnp.bfloat16)

        @pl.when(slot == c)
        def _():
            for g in range(2):
                dq_copies(g, slot)[0].start()

        @pl.when(slot != c)
        def _():
            for g in range(2):
                dq_copies(g, slot)[1].start()

    work(False)

    work(True)

    @pl.when(sends_down)
    def _():
        for copy in halo_down:
            copy.wait_send()

    for chip, copies in halo_up:

        @pl.when((y == chip) & (c == 0) & has_after)
        def _():
            for copy in copies:
                copy.wait_send()

    for copy in small:
        copy.wait_send()
    for g in range(2):
        for copy in swap_copies(g, c):
            copy.wait_send()
        dq_copies(g, c)[0].wait()
        dq_copies(g, other)[1].wait()
    for p in (None, 0, 1):
        part_copies(p, (0, 1), lambda copy: copy.wait_send(), lambda copy: None)
    for chip in range(CHIPS):
        for p, (start, size) in enumerate(PARTS):
            part = landed.at[chip, :, pl.ds(start, size)]
            arrival = pltpu.make_async_copy(part, part, part_recv.at[chip, p])
            if p == 0 and chip == 0:
                pl.when(has_after)(arrival.wait)
            elif p == 2 and chip == CHIPS - 1:
                pl.when(has_before)(arrival.wait)
            else:
                arrival.wait()


def finish(dq_in, landed, dq_hbm, dk_hbm, dv_hbm, dk_buf, dv_buf, sem):
    c = lax.axis_index("audio") % 2
    dq_copy = pltpu.make_async_copy(dq_in, dq_hbm, sem.at[0])
    dq_copy.start()
    head_rows = pl.ds(pl.multiple_of(64 * c, 64), 128)
    middle_rows = pl.ds(pl.multiple_of(128 - 128 * c, 64), 64)
    for pair in range(2):
        rows = slice(pair * 128, (pair + 1) * 128)
        tiles = []
        for t in range(3):
            blocks = []
            for chip in (2 * pair, 2 * pair + 1):
                for own, far_chip, far in ((32, (chip + 3) % CHIPS, 96), (64, (chip + 1) % CHIPS, 0)):
                    own_term = landed[chip, t, own : own + ABLOCK].astype(jnp.float32)
                    blocks.append(own_term + landed[far_chip, t, far : far + ABLOCK].astype(jnp.float32))
            tiles.append(jnp.concatenate(blocks, axis=0).T.astype(jnp.bfloat16))
        dk_buf[head_rows, rows] = tiles[0]
        dv_buf[head_rows, rows] = tiles[1]
        dk_buf[middle_rows, rows] = tiles[2][0:64]
        dv_buf[middle_rows, rows] = tiles[2][64:128]
    copies = [pltpu.make_async_copy(dk_buf, dk_hbm, sem.at[1]), pltpu.make_async_copy(dv_buf, dv_hbm, sem.at[2])]
    for copy in copies:
        copy.start()
    for copy in [dq_copy] + copies:
        copy.wait()


def on_device(queries, keys, values, out_grad, delta, window_low, window_high):
    bf16, f32 = jnp.bfloat16, jnp.float32
    hbm, vmem = pl.BlockSpec(memory_space=pltpu.HBM), pl.BlockSpec(memory_space=pltpu.VMEM)
    dma = pltpu.SemaphoreType.DMA
    arrays = (queries, keys, values, out_grad, delta, window_low, window_high)
    arrays = [pltpu.with_memory_space_constraint(array, pltpu.HBM) for array in arrays]
    query_grad, landed = pl.pallas_call(
        kernel,
        out_shape=(pltpu.VMEM((ROWS, 1536), bf16), pltpu.VMEM((CHIPS, 3, AROWS, HEAD_DIM), bf16)),
        in_specs=[hbm] * 7,
        out_specs=(vmem, vmem),
        scratch_shapes=[
            pltpu.VMEM((2, 2, ROWS, GROUP), bf16),
            pltpu.VMEM((2, 2, ROWS, GROUP), bf16),
            pltpu.VMEM((2, AROWS, GROUP), bf16),
            pltpu.VMEM((2, AROWS, GROUP), bf16),
            pltpu.VMEM((2, 2, ABLOCK, GROUP), bf16),
            pltpu.VMEM((2, 12, ROWS), f32),
            pltpu.VMEM((2, 8, ROWS), f32),
            pltpu.VMEM((2, REACH, ROWS), f32),
            pltpu.VMEM((2, 2, ROWS, GROUP), bf16),
            pltpu.VMEM((2, 3, 2 * ABLOCK, HEAD_DIM), f32),
            pltpu.VMEM((2, 3, 2 * ABLOCK, HEAD_DIM), f32),
            pltpu.VMEM((2, 2, 3, AROWS, HEAD_DIM), bf16),
            pltpu.SMEM((2,), jnp.int32),
            pltpu.SMEM((2,), jnp.int32),
            dma((2,)),
            dma(()),
            dma((2, 2)),
            dma((2, 2)),
            dma((2, 2)),
            dma((2,)),
            dma((2, 2)),
            dma((2, 2)),
            dma((2,)),
            dma((2,)),
            dma((2, 2, 2)),
            dma((2, 2)),
            dma((2, 2, 3)),
            dma((CHIPS, 3)),
            dma((2,)),
            dma((2,)),
            pltpu.SemaphoreType.REGULAR,
        ],
        compiler_params=pltpu.CompilerParams(
            collective_id=0, has_side_effects=True, vmem_limit_bytes=32 << 20
        ),
        name="attention_backward",
    )(*arrays)
    query_grad, key_grad, value_grad = pl.pallas_call(
        finish,
        out_shape=(
            jax.ShapeDtypeStruct((ROWS, 1536), bf16),
            jax.ShapeDtypeStruct((192, 256), bf16),
            jax.ShapeDtypeStruct((192, 256), bf16),
        ),
        in_specs=[vmem, vmem],
        out_specs=(hbm, hbm, hbm),
        scratch_shapes=[pltpu.VMEM((192, 256), bf16), pltpu.VMEM((192, 256), bf16), dma((3,))],
        compiler_params=pltpu.CompilerParams(vmem_limit_bytes=32 << 20),
        name="sum_partials",
    )(query_grad, landed)
    return query_grad, key_grad.T, value_grad.T


def solution(mesh):
    return jax.shard_map(
        on_device,
        mesh=mesh,
        in_specs=(
            P(("video", "audio"), None),
            P("video", None),
            P("video", None),
            P(("video", "audio"), None),
            P(None, ("video", "audio")),
            P(("video", "audio")),
            P(("video", "audio")),
        ),
        out_specs=(P(("video", "audio"), None), P("video", "audio"), P("video", "audio")),
        check_vma=False,
    )
```

```python
import math

import jax
import jax.numpy as jnp
from jax import lax
from jax.experimental import pallas as pl
from jax.experimental.pallas import tpu as pltpu
from jax.sharding import PartitionSpec as P

HEAD_DIM = 128
VBLOCK = 64
ABLOCK = 32
SPANS = 64
CHIPS = 4
ROWS = 128
AROWS = 128
REACH = 96
GROUP = 384
ORDER = (1, 0, 2, 3)
PARTS = ((0, 32), (32, 64), (96, 32))

MESH = pl.DeviceIdType.MESH
masked_score = -1e30
logit_scale = 1.0 / math.sqrt(HEAD_DIM)


def nt(a, b):
    return lax.dot_general(a, b, (((1,), (1,)), ((), ())), preferred_element_type=jnp.float32)


def nn(a, b):
    return lax.dot_general(a, b, (((1,), (0,)), ((), ())), preferred_element_type=jnp.float32)


def tn(a, b):
    return lax.dot_general(a, b, (((0,), (0,)), ((), ())), preferred_element_type=jnp.float32)


def kernel(
    q_hbm, k_hbm, v_hbm, og_hbm, delta_hbm, low_hbm, high_hbm,
    dq_out, landed,
    q_buf, og_buf, k_buf, v_buf, edge_buf, q_own, og_own, k_own, k_edge, v_edge, edge_stage, delta_buf, win_buf, bias_buf, dq_buf, key_sum, value_sum, stage,
    low_smem, high_smem,
    win_sem, delta_sem, rows_sem, audio_sem, edge_sem, own_sem, out_sem,
    swap_send, swap_recv, small_send, small_recv, halo_send, halo_recv, edge_send, edge_recv, edge_part_send,
    part_send, part_recv, dq_send, dq_recv, part_ready,
):
    v = lax.axis_index("video")
    a = lax.axis_index("audio")
    y, c = a // 2, a % 2
    other = 1 - c
    partner = (v, 2 * y + other)
    has_before, has_after = v > 0, v < SPANS - 1
    is_first, is_last = y == 0, y == CHIPS - 1

    def group_of(chip, core, g):
        return (chip + jnp.where(core == 0, 1 - g, 2 + g)) % CHIPS

    def signal(semaphore, device):
        pl.semaphore_signal(semaphore, inc=1, device_id=device, device_id_type=MESH)

    barrier = pltpu.get_barrier_semaphore()

    @pl.when(is_last & has_after)
    def _():
        signal(barrier, (v + 1, a))

    signal(barrier, partner)

    @pl.when(has_before)
    def _():
        signal(barrier, (v - 1, 7))

        @pl.when(is_first)
        def _():
            for i in range(4):
                signal(barrier, (v - 1, 4 * c + i))

        @pl.when(is_first & (c == 1))
        def _():
            signal(barrier, (v - 1, 0))

    signal(barrier, (v, 2 * ((y + 3) % CHIPS)))
    signal(barrier, (v, 2 * ((y + 2) % CHIPS) + 1))
    signal(barrier, (v, 2 * ((y + 1) % CHIPS) + 1))

    low_copy = pltpu.make_async_copy(low_hbm, low_smem, win_sem.at[0])
    high_copy = pltpu.make_async_copy(high_hbm, high_smem, win_sem.at[1])
    delta_copy = pltpu.make_async_copy(delta_hbm, delta_buf.at[c], delta_sem)
    low_copy.start()
    high_copy.start()
    delta_copy.start()

    def lanes(k):
        return pl.ds(pl.multiple_of(k * GROUP, GROUP), GROUP)

    def row_copies(g):
        k = group_of(y, c, g)
        return [
            pltpu.make_async_copy(q_hbm.at[:, lanes(k)], q_buf.at[g, c], rows_sem.at[0, g]),
            pltpu.make_async_copy(og_hbm.at[:, lanes(k)], og_buf.at[g, c], rows_sem.at[1, g]),
        ]

    def audio_copies(g, do):
        k = group_of(y, c, g)
        for i, (source, target) in enumerate(((k_hbm, k_buf), (v_hbm, v_buf))):
            sem = audio_sem.at[i, g]

            @pl.when(is_first)
            def _():
                do(pltpu.make_async_copy(source.at[pl.ds(0, 96), lanes(k)], target.at[g, pl.ds(32, 96)], sem))

            @pl.when(is_last)
            def _():
                do(pltpu.make_async_copy(source.at[pl.ds(160, 96), lanes(k)], target.at[g, pl.ds(0, 96)], sem))

            @pl.when((y > 0) & (y < CHIPS - 1))
            def _():
                first = pl.multiple_of(64 * y - 32, 32)
                do(pltpu.make_async_copy(source.at[pl.ds(first, AROWS), lanes(k)], target.at[g], sem))

    def edge_copies(chips):
        return [
            pltpu.make_async_copy(source.at[pl.ds(0, ABLOCK), lanes(k)], edge_buf.at[i, j], edge_sem.at[i, j])
            for j, k in enumerate(chips)
            for i, source in enumerate((k_hbm, v_hbm))
        ]

    core_0_edges, core_1_edges = edge_copies((0, 3)), edge_copies(ORDER)
    sends_down = is_last & has_before
    works_up = is_last & has_after & (c == 1)
    edge_first = v % 16 == 15

    def when_down(do):
        for core, copies in ((0, core_0_edges), (1, core_1_edges)):

            @pl.when(sends_down & (c == core))
            def _():
                for copy in copies:
                    do(copy)

    when_down(lambda copy: copy.start())

    own_copies = []
    for j, k in enumerate(ORDER):
        own_copies += [
            pltpu.make_async_copy(q_hbm.at[:, lanes(k)], q_own.at[j], own_sem.at[0, j]),
            pltpu.make_async_copy(og_hbm.at[:, lanes(k)], og_own.at[j], own_sem.at[1, j]),
            pltpu.make_async_copy(k_hbm.at[pl.ds(192, 2 * ABLOCK), lanes(k)], k_own.at[j], own_sem.at[2, j]),
        ]

    for g in range(2):
        for copy in row_copies(g):
            copy.start()
        audio_copies(g, lambda copy: copy.start())

    @pl.when(works_up)
    def _():
        for copy in own_copies:
            copy.start()

    when_down(lambda copy: copy.wait())

    @pl.when(jnp.logical_not(has_before))
    def _():
        landed[3, :, 96:128] = jnp.zeros((3, ABLOCK, HEAD_DIM), jnp.bfloat16)

        @pl.when(is_first)
        def _():
            for buf in (k_buf, v_buf):
                buf[:, 0:32] = jnp.zeros((2, ABLOCK, GROUP), jnp.bfloat16)

    @pl.when(jnp.logical_not(has_after))
    def _():
        landed[0, :, 0:32] = jnp.zeros((3, ABLOCK, HEAD_DIM), jnp.bfloat16)

        @pl.when(is_last)
        def _():
            for buf in (k_buf, v_buf):
                buf[:, 96:128] = jnp.zeros((2, ABLOCK, GROUP), jnp.bfloat16)

    from_after = 1 + jnp.where(is_last, 8 * c, 0) + jnp.where(is_first, other, 0)
    from_before = jnp.where(is_last, 1, 0)
    pl.semaphore_wait(barrier, 3 + 2 * c + jnp.where(has_after, from_after, 0) + jnp.where(has_before, from_before, 0))

    def up_copies(i, core):
        return [
            pltpu.make_async_remote_copy(
                (k_hbm, v_hbm)[i].at[pl.ds(224, ABLOCK), lanes(group_of(0, core, g))],
                (k_buf, v_buf)[i].at[g, pl.ds(0, ABLOCK)],
                halo_send.at[i, g, core], halo_recv.at[i, g], device_id=(v + 1, core), device_id_type=MESH,
            )
            for g in range(2)
        ]

    halo_up = (
        (0, [copy for pair in zip(up_copies(0, 0), up_copies(0, 1)) for copy in pair]),
        (1, up_copies(1, 0)),
        (CHIPS - 1, up_copies(1, 1)),
    )
    def down_copies(core):
        targets, sends, receives = (k_edge, v_edge), edge_send, edge_recv
        if core == 0:
            targets, sends, receives = [buf.at[:, pl.ds(96, ABLOCK)] for buf in (k_buf, v_buf)], halo_send, halo_recv
        return [
            pltpu.make_async_remote_copy(
                edge_buf.at[i, j], target.at[j], sends.at[i, j, 0] if core == 0 else sends.at[i, j], receives.at[i, j],
                device_id=(v - 1, 6 + core), device_id_type=MESH,
            )
            for j in range(CHIPS if core else 2)
            for i, target in enumerate(targets)
        ]

    halo_down = ((0, down_copies(0)), (1, down_copies(1)))
    for core, copies in halo_down:

        @pl.when(sends_down & (c == core))
        def _():
            for copy in copies:
                copy.start()

    @pl.when(has_after)
    def _():
        for chip, copies in halo_up:

            @pl.when((y == chip) & (c == 0))
            def _():
                for copy in copies:
                    copy.start()

        signal(part_ready, (v + 1, y // 2))

    def swap_copies(g, slot):
        k = group_of(y, other, g)
        return [
            pltpu.make_async_remote_copy(
                source.at[:, lanes(k)], target.at[g, slot], swap_send.at[i, g], swap_recv.at[i, g],
                device_id=partner, device_id_type=MESH,
            )
            for i, (source, target) in enumerate(((q_hbm, q_buf), (og_hbm, og_buf)))
        ]

    for g in range(2):
        for copy in swap_copies(g, c):
            copy.start()

    low_copy.wait()
    high_copy.wait()
    lane = lax.broadcasted_iota(jnp.int32, (8, ROWS), 1)
    row = lax.broadcasted_iota(jnp.int32, (8, ROWS), 0)
    lows = jnp.where(lane < VBLOCK, low_smem[0], low_smem[1])
    highs = jnp.where(lane < VBLOCK, high_smem[0], high_smem[1])
    win_buf[c] = jnp.where(row == 0, lows, highs).astype(jnp.float32)

    def small_copies(slot):
        return [
            pltpu.make_async_remote_copy(
                buf.at[slot], buf.at[slot], small_send.at[i], small_recv.at[i], device_id=partner, device_id_type=MESH
            )
            for i, buf in enumerate((win_buf, delta_buf))
        ]

    small = small_copies(c)
    small[0].start()
    delta_copy.wait()
    small[1].start()
    for copy in small_copies(other):
        copy.wait_recv()

    row = lax.broadcasted_iota(jnp.int32, (REACH, ROWS), 0)
    for slot in range(2):
        blocks = 8 * v + 2 * y + jnp.where(row < 2 * ABLOCK, row // ABLOCK, 3 * slot - 1)
        blocks = blocks.astype(jnp.float32)
        inside = (blocks >= win_buf[slot, 0:1, :]) & (blocks < win_buf[slot, 1:2, :])
        bias_buf[slot] = jnp.where(inside, 0.0, masked_score)

    def part_copies(slot, groups, do, do_local):
        if slot is None:
            p, start, size, span, exists = 1, ABLOCK, 2 * ABLOCK, v, True
        else:
            p, start, size = 2 * slot, pl.multiple_of(REACH * slot, ABLOCK), ABLOCK
            down, up = is_first & (slot == 0), is_last & (slot == 1)
            span = v - jnp.where(down, 1, 0)
            exists = jnp.logical_not(down & jnp.logical_not(has_before)) & jnp.logical_not(up)
        for g in groups:
            k = group_of(y, c, g)
            for core in range(2):
                source = stage.at[g, core, :, pl.ds(start, size)]
                target = landed.at[y, :, pl.ds(start, size)]
                here = (span == v) & (2 * k + core == a) & exists
                away = jnp.logical_not(here) if g == 1 and core == 0 else True

                @pl.when(away & exists)
                def _():
                    do(
                        pltpu.make_async_remote_copy(
                            source, target, part_send.at[g, core, p], part_recv.at[y, p],
                            device_id=(span, 2 * k + core), device_id_type=MESH,
                        )
                    )

                if g == 1 and core == 0:

                    @pl.when(here)
                    def _():
                        do_local(pltpu.make_async_copy(source, target, part_recv.at[y, p]))

    def dq_copies(g, slot):
        k = group_of(y, c, g)
        return (
            pltpu.make_async_copy(dq_buf.at[g, slot], dq_out.at[:, lanes(k)], out_sem.at[g]),
            pltpu.make_async_remote_copy(
                dq_buf.at[g, slot], dq_out.at[:, lanes(k)], dq_send.at[g], dq_recv.at[g],
                device_id=partner, device_id_type=MESH,
            ),
        )

    def work(last):
        slot = jnp.where(is_first, 1, 0)
        if last:
            slot = 1 - slot

        @pl.when(slot == c)
        def _():
            for g in range(2):
                for copy in row_copies(g):
                    copy.wait()

        @pl.when(slot != c)
        def _():
            for g in range(2):
                for copy in swap_copies(g, slot):
                    copy.wait_recv()

        def halo_wait(i, buf, groups):
            if last:

                @pl.when((is_first & has_before) | (is_last & has_after & (c == 0)))
                def _():
                    for g in groups:
                        part = buf.at[g, pl.ds(0, ABLOCK)]
                        pltpu.make_async_remote_copy(
                            part, part, halo_send.at[i, g, 0], halo_recv.at[i, g], device_id=partner, device_id_type=MESH
                        ).wait_recv()

        def start(copy):
            copy.start()

        def put(heads, rows, key_parts, value_parts):
            for (g, i, _), key_part, value_part in zip(heads, key_parts, value_parts):
                if i == 1:
                    half = lax.broadcasted_iota(jnp.int32, key_part.shape, 1) < HEAD_DIM // 2
                    stage[g, 0, 2, rows] = jnp.where(half, key_part, pltpu.roll(value_part, 64, 1)).astype(jnp.bfloat16)
                    stage[g, 1, 2, rows] = jnp.where(half, pltpu.roll(key_part, 64, 1), value_part).astype(jnp.bfloat16)
                else:
                    stage[g, i // 2, 0, rows] = key_part.astype(jnp.bfloat16)
                    stage[g, i // 2, 1, rows] = value_part.astype(jnp.bfloat16)

        if not last:
            for g in range(2):
                audio_copies(g, lambda copy: copy.wait())
        middle = pl.ds(ABLOCK, 2 * ABLOCK)
        alone = pl.ds(pl.multiple_of(REACH * slot, ABLOCK), ABLOCK)
        bias = bias_buf[slot]

        def gradients(groups):
            heads = [(g, i, slice(i * HEAD_DIM, (i + 1) * HEAD_DIM)) for g in groups for i in range(3)]
            deltas = [delta_buf[slot, pl.ds(3 * group_of(y, c, g) + i, 1), :] for g, i, _ in heads]

            halo_wait(0, k_buf, groups)
            keys = [jnp.concatenate([k_buf[g, middle, cols], k_buf[g, alone, cols]], axis=0) for g, _, cols in heads]
            scores = [nt(key, q_buf[g, slot, :, cols]) for key, (g, _, cols) in zip(keys, heads)]
            prob_grads = [nt(v_buf[g, middle, cols], og_buf[g, slot, :, cols]) for g, _, cols in heads]
            probs, prob_halves, middle_halves = [], [], []
            for score, prob_grad, delta in zip(scores, prob_grads, deltas):
                score = score + bias
                peak = jnp.max(score, axis=0, keepdims=True)
                weights = jnp.exp2((score - peak) * (logit_scale * math.log2(math.e)))
                prob = weights * (1.0 / jnp.sum(weights, axis=0, keepdims=True))
                probs.append(prob[64:96])
                prob_halves.append(prob.astype(jnp.bfloat16))
                middle_halves.append((prob[0:64] * (prob_grad - delta)).astype(jnp.bfloat16))
            value_parts = [nn(prob, og_buf[g, slot, :, cols]) for prob, (g, _, cols) in zip(prob_halves, heads)]
            key_parts = [nn(score, q_buf[g, slot, :, cols]) * logit_scale for score, (g, _, cols) in zip(middle_halves, heads)]
            if last:
                key_parts = [part + key_sum[g, i] for part, (g, i, _) in zip(key_parts, heads)]
                middle_values = [part[0:64] + value_sum[g, i] for part, (g, i, _) in zip(value_parts, heads)]
                put(heads, middle, key_parts, middle_values)

                part_copies(None, groups, start, start)
            else:
                for key_part, value_part, (g, i, _) in zip(key_parts, value_parts, heads):
                    key_sum[g, i] = key_part
                    value_sum[g, i] = value_part[0:64]

            halo_wait(1, v_buf, groups)
            prob_grads = [nt(v_buf[g, alone, cols], og_buf[g, slot, :, cols]) for g, _, cols in heads]
            alone_halves = [
                (prob * (prob_grad - delta)).astype(jnp.bfloat16) for prob, prob_grad, delta in zip(probs, prob_grads, deltas)
            ]
            key_parts = [nn(score, q_buf[g, slot, :, cols]) * logit_scale for score, (g, _, cols) in zip(alone_halves, heads)]
            put(heads, alone, key_parts, [part[64:96] for part in value_parts])
            if last:

                @pl.when(is_first & has_before & (0 in groups))
                def _():
                    pl.semaphore_wait(part_ready, 4)

            part_copies(slot, groups, start, start)
            return list(zip(heads, keys, middle_halves, alone_halves))

        done = gradients((0,)) + gradients((1,)) if last else gradients((0, 1))
        for (g, _, cols), key, first, second in done:
            score_half = jnp.concatenate([first, second], axis=0)
            dq_buf[g, slot, :, cols] = (tn(score_half, key) * logit_scale).astype(jnp.bfloat16)

        @pl.when(slot == c)
        def _():
            for g in range(2):
                dq_copies(g, slot)[0].start()

        @pl.when(slot != c)
        def _():
            for g in range(2):
                dq_copies(g, slot)[1].start()

    def edge_part_copies(j):
        k = jnp.where(j < 2, 1 - j, j)
        return [
            pltpu.make_async_remote_copy(
                edge_stage.at[j, core], landed.at[CHIPS - 1, :, pl.ds(96, ABLOCK)],
                edge_part_send.at[j, core], part_recv.at[CHIPS - 1, 2],
                device_id=(v + 1, 2 * k + core), device_id_type=MESH,
            )
            for core in range(2)
        ]

    def arrived(i, j):
        part = (k_edge, v_edge)[i].at[j]
        pltpu.make_async_remote_copy(
            part, part, edge_send.at[i, j], edge_recv.at[i, j], device_id=partner, device_id_type=MESH
        ).wait_recv()

    def edge_work(j, wait):
        k = jnp.where(j < 2, 1 - j, j)
        heads = [slice(i * HEAD_DIM, (i + 1) * HEAD_DIM) for i in range(3)]
        bias = bias_buf[1]
        deltas = [delta_buf[1, pl.ds(3 * k + i, 1), :] for i in range(3)]
        wait(0, j)
        keys = [jnp.concatenate([k_own[j, :, cols], k_edge[j, :, cols]], axis=0) for cols in heads]
        scores = [nt(key, q_own[j, :, cols]) + bias for key, cols in zip(keys, heads)]
        probs = []
        for score in scores:
            weights = jnp.exp2((score - jnp.max(score, axis=0, keepdims=True)) * (logit_scale * math.log2(math.e)))
            probs.append(weights[64:96] * (1.0 / jnp.sum(weights, axis=0, keepdims=True)))
        value_parts = [nn(prob.astype(jnp.bfloat16), og_own[j, :, cols]) for prob, cols in zip(probs, heads)]
        wait(1, j)
        prob_grads = [nt(v_edge[j, :, cols], og_own[j, :, cols]) for cols in heads]
        halves = [(p * (grad - delta)).astype(jnp.bfloat16) for p, grad, delta in zip(probs, prob_grads, deltas)]
        key_parts = [nn(score, q_own[j, :, cols]) * logit_scale for score, cols in zip(halves, heads)]
        half = lax.broadcasted_iota(jnp.int32, (ABLOCK, HEAD_DIM), 1) < HEAD_DIM // 2
        for core in range(2):
            edge_stage[j, core, 0] = key_parts[2 * core].astype(jnp.bfloat16)
            edge_stage[j, core, 1] = value_parts[2 * core].astype(jnp.bfloat16)
        edge_stage[j, 0, 2] = jnp.where(half, key_parts[1], pltpu.roll(value_parts[1], 64, 1)).astype(jnp.bfloat16)
        edge_stage[j, 1, 2] = jnp.where(half, pltpu.roll(key_parts[1], 64, 1), value_parts[1]).astype(jnp.bfloat16)
        for copy in edge_part_copies(j):
            copy.start()

    work(False)

    @pl.when(works_up)
    def _():
        for copy in own_copies:
            copy.wait()

        @pl.when(edge_first)
        def _():
            lax.fori_loop(0, CHIPS, lambda j, carry: (edge_work(j, arrived), carry)[1], 0)

        @pl.when(jnp.logical_not(edge_first))
        def _():
            for j in range(CHIPS):
                for i in range(2):
                    arrived(i, j)

        for g in range(2):
            k_buf[g, pl.ds(96, ABLOCK)] = k_edge[2 * g]
            v_buf[g, pl.ds(96, ABLOCK)] = v_edge[2 * g]

    work(True)

    @pl.when(works_up & jnp.logical_not(edge_first))
    def _():
        lax.fori_loop(0, CHIPS, lambda j, carry: (edge_work(j, lambda i, j: None), carry)[1], 0)

    for core, copies in halo_down:

        @pl.when(sends_down & (c == core))
        def _():
            for copy in copies:
                copy.wait_send()

    @pl.when(works_up)
    def _():
        for j in range(CHIPS):
            for copy in edge_part_copies(j):
                copy.wait_send()

    for chip, copies in halo_up:

        @pl.when((y == chip) & (c == 0) & has_after)
        def _():
            for copy in copies:
                copy.wait_send()

    for copy in small:
        copy.wait_send()
    for g in range(2):
        for copy in swap_copies(g, c):
            copy.wait_send()
        dq_copies(g, c)[0].wait()
        dq_copies(g, other)[1].wait()
    for p in (None, 0, 1):
        part_copies(p, (0, 1), lambda copy: copy.wait_send(), lambda copy: None)
    for chip in range(CHIPS):
        for p, (start, size) in enumerate(PARTS):
            part = landed.at[chip, :, pl.ds(start, size)]
            arrival = pltpu.make_async_copy(part, part, part_recv.at[chip, p])
            if p == 0 and chip == 0:
                pl.when(has_after)(arrival.wait)
            elif p == 2 and chip == CHIPS - 1:
                pl.when(has_before)(arrival.wait)
            else:
                arrival.wait()


def finish(dq_in, landed, dq_hbm, dk_hbm, dv_hbm, dk_buf, dv_buf, sem):
    c = lax.axis_index("audio") % 2
    dq_copy = pltpu.make_async_copy(dq_in, dq_hbm, sem.at[0])
    dq_copy.start()
    head_rows = pl.ds(pl.multiple_of(64 * c, 64), 128)
    middle_rows = pl.ds(pl.multiple_of(128 - 128 * c, 64), 64)
    for pair in range(2):
        rows = slice(pair * 128, (pair + 1) * 128)
        tiles = []
        for t in range(3):
            blocks = []
            for chip in (2 * pair, 2 * pair + 1):
                for own, far_chip, far in ((32, (chip + 3) % CHIPS, 96), (64, (chip + 1) % CHIPS, 0)):
                    own_term = landed[chip, t, own : own + ABLOCK].astype(jnp.float32)
                    blocks.append(own_term + landed[far_chip, t, far : far + ABLOCK].astype(jnp.float32))
            tiles.append(jnp.concatenate(blocks, axis=0).T.astype(jnp.bfloat16))
        dk_buf[head_rows, rows] = tiles[0]
        dv_buf[head_rows, rows] = tiles[1]
        dk_buf[middle_rows, rows] = tiles[2][0:64]
        dv_buf[middle_rows, rows] = tiles[2][64:128]
    copies = [pltpu.make_async_copy(dk_buf, dk_hbm, sem.at[1]), pltpu.make_async_copy(dv_buf, dv_hbm, sem.at[2])]
    for copy in copies:
        copy.start()
    for copy in [dq_copy] + copies:
        copy.wait()


def on_device(queries, keys, values, out_grad, delta, window_low, window_high):
    bf16, f32 = jnp.bfloat16, jnp.float32
    hbm, vmem = pl.BlockSpec(memory_space=pltpu.HBM), pl.BlockSpec(memory_space=pltpu.VMEM)
    dma = pltpu.SemaphoreType.DMA
    arrays = (queries, keys, values, out_grad, delta, window_low, window_high)
    arrays = [pltpu.with_memory_space_constraint(array, pltpu.HBM) for array in arrays]
    query_grad, landed = pl.pallas_call(
        kernel,
        out_shape=(pltpu.VMEM((ROWS, 1536), bf16), pltpu.VMEM((CHIPS, 3, AROWS, HEAD_DIM), bf16)),
        in_specs=[hbm] * 7,
        out_specs=(vmem, vmem),
        scratch_shapes=[
            pltpu.VMEM((2, 2, ROWS, GROUP), bf16),
            pltpu.VMEM((2, 2, ROWS, GROUP), bf16),
            pltpu.VMEM((2, AROWS, GROUP), bf16),
            pltpu.VMEM((2, AROWS, GROUP), bf16),
            pltpu.VMEM((2, CHIPS, ABLOCK, GROUP), bf16),
            pltpu.VMEM((CHIPS, ROWS, GROUP), bf16),
            pltpu.VMEM((CHIPS, ROWS, GROUP), bf16),
            pltpu.VMEM((CHIPS, 2 * ABLOCK, GROUP), bf16),
            pltpu.VMEM((CHIPS, ABLOCK, GROUP), bf16),
            pltpu.VMEM((CHIPS, ABLOCK, GROUP), bf16),
            pltpu.VMEM((CHIPS, 2, 3, ABLOCK, HEAD_DIM), bf16),
            pltpu.VMEM((2, 12, ROWS), f32),
            pltpu.VMEM((2, 8, ROWS), f32),
            pltpu.VMEM((2, REACH, ROWS), f32),
            pltpu.VMEM((2, 2, ROWS, GROUP), bf16),
            pltpu.VMEM((2, 3, 2 * ABLOCK, HEAD_DIM), f32),
            pltpu.VMEM((2, 3, 2 * ABLOCK, HEAD_DIM), f32),
            pltpu.VMEM((2, 2, 3, AROWS, HEAD_DIM), bf16),
            pltpu.SMEM((2,), jnp.int32),
            pltpu.SMEM((2,), jnp.int32),
            dma((2,)),
            dma(()),
            dma((2, 2)),
            dma((2, 2)),
            dma((2, CHIPS)),
            dma((3, CHIPS)),
            dma((2,)),
            dma((2, 2)),
            dma((2, 2)),
            dma((2,)),
            dma((2,)),
            dma((2, 2, 2)),
            dma((2, 2)),
            dma((2, CHIPS)),
            dma((2, CHIPS)),
            dma((CHIPS, 2)),
            dma((2, 2, 3)),
            dma((CHIPS, 3)),
            dma((2,)),
            dma((2,)),
            pltpu.SemaphoreType.REGULAR,
        ],
        compiler_params=pltpu.CompilerParams(
            collective_id=0, has_side_effects=True, vmem_limit_bytes=32 << 20
        ),
        name="attention_backward",
    )(*arrays)
    query_grad, key_grad, value_grad = pl.pallas_call(
        finish,
        out_shape=(
            jax.ShapeDtypeStruct((ROWS, 1536), bf16),
            jax.ShapeDtypeStruct((192, 256), bf16),
            jax.ShapeDtypeStruct((192, 256), bf16),
        ),
        in_specs=[vmem, vmem],
        out_specs=(hbm, hbm, hbm),
        scratch_shapes=[pltpu.VMEM((192, 256), bf16), pltpu.VMEM((192, 256), bf16), dma((3,))],
        compiler_params=pltpu.CompilerParams(vmem_limit_bytes=32 << 20),
        name="sum_partials",
    )(query_grad, landed)
    return query_grad, key_grad.T, value_grad.T


def solution(mesh):
    return jax.shard_map(
        on_device,
        mesh=mesh,
        in_specs=(
            P(("video", "audio"), None),
            P("video", None),
            P("video", None),
            P(("video", "audio"), None),
            P(None, ("video", "audio")),
            P(("video", "audio")),
            P(("video", "audio")),
        ),
        out_specs=(P(("video", "audio"), None), P("video", "audio"), P("video", "audio")),
        check_vma=False,
    )
```

```python
import math

import jax
import jax.numpy as jnp
from jax import lax
from jax.experimental import pallas as pl
from jax.experimental.pallas import tpu as pltpu
from jax.sharding import PartitionSpec as P

HEAD_DIM = 128
VBLOCK = 64
ABLOCK = 32
SPANS = 64
CHIPS = 4
ROWS = 128
AROWS = 128
REACH = 96
GROUP = 384
PARTS = ((0, 32), (32, 64), (96, 32))

MESH = pl.DeviceIdType.MESH
masked_score = -1e30
logit_scale = 1.0 / math.sqrt(HEAD_DIM)


def nt(a, b):
    return lax.dot_general(a, b, (((1,), (1,)), ((), ())), preferred_element_type=jnp.float32)


def nn(a, b):
    return lax.dot_general(a, b, (((1,), (0,)), ((), ())), preferred_element_type=jnp.float32)


def tn(a, b):
    return lax.dot_general(a, b, (((0,), (0,)), ((), ())), preferred_element_type=jnp.float32)


def kernel(
    q_hbm, k_hbm, v_hbm, og_hbm, delta_hbm, low_hbm, high_hbm,
    dq_out, landed,
    q_buf, og_buf, k_buf, v_buf, edge_buf, q_own, og_own, k_own, k_edge, v_edge, edge_stage, delta_buf, win_buf, bias_buf, dq_buf, key_sum, value_sum, stage,
    low_smem, high_smem,
    win_sem, delta_sem, rows_sem, audio_sem, edge_sem, own_sem, out_sem,
    swap_send, swap_recv, small_send, small_recv, halo_send, halo_recv, edge_send, edge_recv, edge_part_send,
    part_send, part_recv, dq_send, dq_recv, part_ready,
):
    v = lax.axis_index("video")
    a = lax.axis_index("audio")
    y, c = a // 2, a % 2
    other = 1 - c
    partner = (v, 2 * y + other)
    has_before, has_after = v > 0, v < SPANS - 1
    is_first, is_last = y == 0, y == CHIPS - 1

    def group_of(chip, core, g):
        return (chip + jnp.where(core == 0, 1 - g, 2 + g)) % CHIPS

    def signal(semaphore, device):
        pl.semaphore_signal(semaphore, inc=1, device_id=device, device_id_type=MESH)

    barrier = pltpu.get_barrier_semaphore()

    @pl.when(is_last & has_after)
    def _():
        signal(barrier, (v + 1, a))

        @pl.when(c == 1)
        def _():
            signal(barrier, (v + 1, 6))

    signal(barrier, partner)

    @pl.when(has_before)
    def _():
        signal(barrier, (v - 1, 7))

        @pl.when(is_first)
        def _():
            for i in range(4):
                signal(barrier, (v - 1, 4 * c + i))

        @pl.when(is_first & (c == 1))
        def _():
            signal(barrier, (v - 1, 0))

    signal(barrier, (v, 2 * ((y + 3) % CHIPS)))
    signal(barrier, (v, 2 * ((y + 2) % CHIPS) + 1))
    signal(barrier, (v, 2 * ((y + 1) % CHIPS) + 1))

    low_copy = pltpu.make_async_copy(low_hbm, low_smem, win_sem.at[0])
    high_copy = pltpu.make_async_copy(high_hbm, high_smem, win_sem.at[1])
    delta_copy = pltpu.make_async_copy(delta_hbm, delta_buf.at[c], delta_sem)
    low_copy.start()
    high_copy.start()
    delta_copy.start()

    def lanes(k):
        return pl.ds(pl.multiple_of(k * GROUP, GROUP), GROUP)

    def row_copies(g):
        k = group_of(y, c, g)
        return [
            pltpu.make_async_copy(q_hbm.at[:, lanes(k)], q_buf.at[g, c], rows_sem.at[0, g]),
            pltpu.make_async_copy(og_hbm.at[:, lanes(k)], og_buf.at[g, c], rows_sem.at[1, g]),
        ]

    def audio_copies(g, do):
        k = group_of(y, c, g)
        for i, (source, target) in enumerate(((k_hbm, k_buf), (v_hbm, v_buf))):
            sem = audio_sem.at[i, g]

            @pl.when(is_first)
            def _():
                do(pltpu.make_async_copy(source.at[pl.ds(0, 96), lanes(k)], target.at[g, pl.ds(32, 96)], sem))

            @pl.when(is_last)
            def _():
                do(pltpu.make_async_copy(source.at[pl.ds(160, 96), lanes(k)], target.at[g, pl.ds(0, 96)], sem))

            @pl.when((y > 0) & (y < CHIPS - 1))
            def _():
                first = pl.multiple_of(64 * y - 32, 32)
                do(pltpu.make_async_copy(source.at[pl.ds(first, AROWS), lanes(k)], target.at[g], sem))

    def edge_copies(chips):
        return [
            pltpu.make_async_copy(source.at[pl.ds(0, ABLOCK), lanes(k)], edge_buf.at[i, j], edge_sem.at[i, j])
            for j, k in enumerate(chips)
            for i, source in enumerate((k_hbm, v_hbm))
        ]

    core_0_edges, core_1_edges = edge_copies((2, 3, 0)), edge_copies((0, 1))
    sends_down = is_last & has_before
    works_up = is_last & has_after & (c == 1)
    edge_first = v % 16 == 15

    def when_down(do):
        for core, copies in ((0, core_0_edges), (1, core_1_edges)):

            @pl.when(sends_down & (c == core))
            def _():
                for copy in copies:
                    do(copy)

    when_down(lambda copy: copy.start())

    own_copies = []
    for j in range(CHIPS):
        k = j
        own_copies += [
            pltpu.make_async_copy(q_hbm.at[:, lanes(k)], q_own.at[j], own_sem.at[0, j]),
            pltpu.make_async_copy(og_hbm.at[:, lanes(k)], og_own.at[j], own_sem.at[1, j]),
            pltpu.make_async_copy(k_hbm.at[pl.ds(192, 2 * ABLOCK), lanes(k)], k_own.at[j], own_sem.at[2, j]),
        ]

    for g in range(2):
        for copy in row_copies(g):
            copy.start()
        audio_copies(g, lambda copy: copy.start())

    @pl.when(works_up)
    def _():
        for copy in own_copies:
            copy.start()

    when_down(lambda copy: copy.wait())

    @pl.when(jnp.logical_not(has_before))
    def _():
        landed[3, :, 96:128] = jnp.zeros((3, ABLOCK, HEAD_DIM), jnp.bfloat16)

        @pl.when(is_first)
        def _():
            for buf in (k_buf, v_buf):
                buf[:, 0:32] = jnp.zeros((2, ABLOCK, GROUP), jnp.bfloat16)

    @pl.when(jnp.logical_not(has_after))
    def _():
        landed[0, :, 0:32] = jnp.zeros((3, ABLOCK, HEAD_DIM), jnp.bfloat16)

        @pl.when(is_last)
        def _():
            for buf in (k_buf, v_buf):
                buf[:, 96:128] = jnp.zeros((2, ABLOCK, GROUP), jnp.bfloat16)

    from_after = 1 + jnp.where(is_last, 8 * c, 0) + jnp.where(is_first, other, 0)
    from_before = jnp.where(is_last, 2 - c, 0)
    pl.semaphore_wait(barrier, 3 + 2 * c + jnp.where(has_after, from_after, 0) + jnp.where(has_before, from_before, 0))

    def up_copies(i, core):
        return [
            pltpu.make_async_remote_copy(
                (k_hbm, v_hbm)[i].at[pl.ds(224, ABLOCK), lanes(group_of(0, core, g))],
                (k_buf, v_buf)[i].at[g, pl.ds(0, ABLOCK)],
                halo_send.at[i, g, core], halo_recv.at[i, g], device_id=(v + 1, core), device_id_type=MESH,
            )
            for g in range(2)
        ]

    halo_up = (
        (0, [copy for pair in zip(up_copies(0, 0), up_copies(0, 1)) for copy in pair]),
        (1, up_copies(1, 0)),
        (CHIPS - 1, up_copies(1, 1)),
    )
    def down_copies(core):
        blocks = [
            pltpu.make_async_remote_copy(
                edge_buf.at[i, n], target.at[2 - 2 * core + n], edge_send.at[i, n], edge_recv.at[i, 2 - 2 * core + n],
                device_id=(v - 1, 7), device_id_type=MESH,
            )
            for n in range(2)
            for i, target in enumerate((k_edge, v_edge))
        ]
        if core == 0:
            blocks += [
                pltpu.make_async_remote_copy(
                    edge_buf.at[i, 2 - g], target.at[g, pl.ds(96, ABLOCK)], halo_send.at[i, g, 0], halo_recv.at[i, g],
                    device_id=(v - 1, 6), device_id_type=MESH,
                )
                for g in range(2)
                for i, target in enumerate((k_buf, v_buf))
            ]
        return blocks

    halo_down = ((0, down_copies(0)), (1, down_copies(1)))
    for core, copies in halo_down:

        @pl.when(sends_down & (c == core))
        def _():
            for copy in copies:
                copy.start()

    @pl.when(has_after)
    def _():
        for chip, copies in halo_up:

            @pl.when((y == chip) & (c == 0))
            def _():
                for copy in copies:
                    copy.start()

        signal(part_ready, (v + 1, y // 2))

    def swap_copies(g, slot):
        k = group_of(y, other, g)
        return [
            pltpu.make_async_remote_copy(
                source.at[:, lanes(k)], target.at[g, slot], swap_send.at[i, g], swap_recv.at[i, g],
                device_id=partner, device_id_type=MESH,
            )
            for i, (source, target) in enumerate(((q_hbm, q_buf), (og_hbm, og_buf)))
        ]

    for g in range(2):
        for copy in swap_copies(g, c):
            copy.start()

    low_copy.wait()
    high_copy.wait()
    lane = lax.broadcasted_iota(jnp.int32, (8, ROWS), 1)
    row = lax.broadcasted_iota(jnp.int32, (8, ROWS), 0)
    lows = jnp.where(lane < VBLOCK, low_smem[0], low_smem[1])
    highs = jnp.where(lane < VBLOCK, high_smem[0], high_smem[1])
    win_buf[c] = jnp.where(row == 0, lows, highs).astype(jnp.float32)

    def small_copies(slot):
        return [
            pltpu.make_async_remote_copy(
                buf.at[slot], buf.at[slot], small_send.at[i], small_recv.at[i], device_id=partner, device_id_type=MESH
            )
            for i, buf in enumerate((win_buf, delta_buf))
        ]

    small = small_copies(c)
    small[0].start()
    delta_copy.wait()
    small[1].start()
    for copy in small_copies(other):
        copy.wait_recv()

    row = lax.broadcasted_iota(jnp.int32, (REACH, ROWS), 0)
    for slot in range(2):
        blocks = 8 * v + 2 * y + jnp.where(row < 2 * ABLOCK, row // ABLOCK, 3 * slot - 1)
        blocks = blocks.astype(jnp.float32)
        inside = (blocks >= win_buf[slot, 0:1, :]) & (blocks < win_buf[slot, 1:2, :])
        bias_buf[slot] = jnp.where(inside, 0.0, masked_score)

    def part_copies(slot, groups, do, do_local):
        if slot is None:
            p, start, size, span, exists = 1, ABLOCK, 2 * ABLOCK, v, True
        else:
            p, start, size = 2 * slot, pl.multiple_of(REACH * slot, ABLOCK), ABLOCK
            down, up = is_first & (slot == 0), is_last & (slot == 1)
            span = v - jnp.where(down, 1, 0)
            exists = jnp.logical_not(down & jnp.logical_not(has_before)) & jnp.logical_not(up)
        for g in groups:
            k = group_of(y, c, g)
            for core in range(2):
                source = stage.at[g, core, :, pl.ds(start, size)]
                target = landed.at[y, :, pl.ds(start, size)]
                here = (span == v) & (2 * k + core == a) & exists
                away = jnp.logical_not(here) if g == 1 and core == 0 else True

                @pl.when(away & exists)
                def _():
                    do(
                        pltpu.make_async_remote_copy(
                            source, target, part_send.at[g, core, p], part_recv.at[y, p],
                            device_id=(span, 2 * k + core), device_id_type=MESH,
                        )
                    )

                if g == 1 and core == 0:

                    @pl.when(here)
                    def _():
                        do_local(pltpu.make_async_copy(source, target, part_recv.at[y, p]))

    def dq_copies(g, slot):
        k = group_of(y, c, g)
        return (
            pltpu.make_async_copy(dq_buf.at[g, slot], dq_out.at[:, lanes(k)], out_sem.at[g]),
            pltpu.make_async_remote_copy(
                dq_buf.at[g, slot], dq_out.at[:, lanes(k)], dq_send.at[g], dq_recv.at[g],
                device_id=partner, device_id_type=MESH,
            ),
        )

    def work(last):
        slot = jnp.where(is_first, 1, 0)
        if last:
            slot = 1 - slot

        @pl.when(slot == c)
        def _():
            for g in range(2):
                for copy in row_copies(g):
                    copy.wait()

        @pl.when(slot != c)
        def _():
            for g in range(2):
                for copy in swap_copies(g, slot):
                    copy.wait_recv()

        def halo_wait(i, buf, groups):
            if last:

                @pl.when((is_first & has_before) | (is_last & has_after & (c == 0)))
                def _():
                    for g in groups:
                        part = buf.at[g, pl.ds(0, ABLOCK)]
                        pltpu.make_async_remote_copy(
                            part, part, halo_send.at[i, g, 0], halo_recv.at[i, g], device_id=partner, device_id_type=MESH
                        ).wait_recv()

        def start(copy):
            copy.start()

        def put(heads, rows, key_parts, value_parts):
            for (g, i, _), key_part, value_part in zip(heads, key_parts, value_parts):
                if i == 1:
                    half = lax.broadcasted_iota(jnp.int32, key_part.shape, 1) < HEAD_DIM // 2
                    stage[g, 0, 2, rows] = jnp.where(half, key_part, pltpu.roll(value_part, 64, 1)).astype(jnp.bfloat16)
                    stage[g, 1, 2, rows] = jnp.where(half, pltpu.roll(key_part, 64, 1), value_part).astype(jnp.bfloat16)
                else:
                    stage[g, i // 2, 0, rows] = key_part.astype(jnp.bfloat16)
                    stage[g, i // 2, 1, rows] = value_part.astype(jnp.bfloat16)

        if not last:
            for g in range(2):
                audio_copies(g, lambda copy: copy.wait())
        middle = pl.ds(ABLOCK, 2 * ABLOCK)
        alone = pl.ds(pl.multiple_of(REACH * slot, ABLOCK), ABLOCK)
        bias = bias_buf[slot]

        def gradients(groups):
            heads = [(g, i, slice(i * HEAD_DIM, (i + 1) * HEAD_DIM)) for g in groups for i in range(3)]
            deltas = [delta_buf[slot, pl.ds(3 * group_of(y, c, g) + i, 1), :] for g, i, _ in heads]

            halo_wait(0, k_buf, groups)
            keys = [jnp.concatenate([k_buf[g, middle, cols], k_buf[g, alone, cols]], axis=0) for g, _, cols in heads]
            scores = [nt(key, q_buf[g, slot, :, cols]) for key, (g, _, cols) in zip(keys, heads)]
            prob_grads = [nt(v_buf[g, middle, cols], og_buf[g, slot, :, cols]) for g, _, cols in heads]
            probs, prob_halves, middle_halves = [], [], []
            for score, prob_grad, delta in zip(scores, prob_grads, deltas):
                score = score + bias
                peak = jnp.max(score, axis=0, keepdims=True)
                weights = jnp.exp2((score - peak) * (logit_scale * math.log2(math.e)))
                prob = weights * (1.0 / jnp.sum(weights, axis=0, keepdims=True))
                probs.append(prob[64:96])
                prob_halves.append(prob.astype(jnp.bfloat16))
                middle_halves.append((prob[0:64] * (prob_grad - delta)).astype(jnp.bfloat16))
            value_parts = [nn(prob, og_buf[g, slot, :, cols]) for prob, (g, _, cols) in zip(prob_halves, heads)]
            key_parts = [nn(score, q_buf[g, slot, :, cols]) * logit_scale for score, (g, _, cols) in zip(middle_halves, heads)]
            if last:
                key_parts = [part + key_sum[g, i] for part, (g, i, _) in zip(key_parts, heads)]
                middle_values = [part[0:64] + value_sum[g, i] for part, (g, i, _) in zip(value_parts, heads)]
                put(heads, middle, key_parts, middle_values)

                part_copies(None, groups, start, start)
            else:
                for key_part, value_part, (g, i, _) in zip(key_parts, value_parts, heads):
                    key_sum[g, i] = key_part
                    value_sum[g, i] = value_part[0:64]

            halo_wait(1, v_buf, groups)
            prob_grads = [nt(v_buf[g, alone, cols], og_buf[g, slot, :, cols]) for g, _, cols in heads]
            alone_halves = [
                (prob * (prob_grad - delta)).astype(jnp.bfloat16) for prob, prob_grad, delta in zip(probs, prob_grads, deltas)
            ]
            key_parts = [nn(score, q_buf[g, slot, :, cols]) * logit_scale for score, (g, _, cols) in zip(alone_halves, heads)]
            put(heads, alone, key_parts, [part[64:96] for part in value_parts])
            if last:

                @pl.when(is_first & has_before & (0 in groups))
                def _():
                    pl.semaphore_wait(part_ready, 4)

            part_copies(slot, groups, start, start)
            return list(zip(heads, keys, middle_halves, alone_halves))

        done = gradients((0,)) + gradients((1,)) if last else gradients((0, 1))
        for (g, _, cols), key, first, second in done:
            score_half = jnp.concatenate([first, second], axis=0)
            dq_buf[g, slot, :, cols] = (tn(score_half, key) * logit_scale).astype(jnp.bfloat16)

        @pl.when(slot == c)
        def _():
            for g in range(2):
                dq_copies(g, slot)[0].start()

        @pl.when(slot != c)
        def _():
            for g in range(2):
                dq_copies(g, slot)[1].start()

    def edge_part_copies(j):
        return [
            pltpu.make_async_remote_copy(
                edge_stage.at[j, core], landed.at[CHIPS - 1, :, pl.ds(96, ABLOCK)],
                edge_part_send.at[j, core], part_recv.at[CHIPS - 1, 2],
                device_id=(v + 1, 2 * j + core), device_id_type=MESH,
            )
            for core in range(2)
        ]

    def arrived(i, j):
        part = (k_edge, v_edge)[i].at[j]
        pltpu.make_async_remote_copy(
            part, part, edge_send.at[i, 0], edge_recv.at[i, j], device_id=partner, device_id_type=MESH
        ).wait_recv()

    def edge_work(j, wait):
        heads = [slice(i * HEAD_DIM, (i + 1) * HEAD_DIM) for i in range(3)]
        bias = bias_buf[1]
        deltas = [delta_buf[1, pl.ds(3 * j + i, 1), :] for i in range(3)]
        wait(0, j)
        keys = [jnp.concatenate([k_own[j, :, cols], k_edge[j, :, cols]], axis=0) for cols in heads]
        scores = [nt(key, q_own[j, :, cols]) + bias for key, cols in zip(keys, heads)]
        probs = []
        for score in scores:
            weights = jnp.exp2((score - jnp.max(score, axis=0, keepdims=True)) * (logit_scale * math.log2(math.e)))
            probs.append(weights[64:96] * (1.0 / jnp.sum(weights, axis=0, keepdims=True)))
        value_parts = [nn(prob.astype(jnp.bfloat16), og_own[j, :, cols]) for prob, cols in zip(probs, heads)]
        wait(1, j)
        prob_grads = [nt(v_edge[j, :, cols], og_own[j, :, cols]) for cols in heads]
        halves = [(p * (grad - delta)).astype(jnp.bfloat16) for p, grad, delta in zip(probs, prob_grads, deltas)]
        key_parts = [nn(score, q_own[j, :, cols]) * logit_scale for score, cols in zip(halves, heads)]
        half = lax.broadcasted_iota(jnp.int32, (ABLOCK, HEAD_DIM), 1) < HEAD_DIM // 2
        for core in range(2):
            edge_stage[j, core, 0] = key_parts[2 * core].astype(jnp.bfloat16)
            edge_stage[j, core, 1] = value_parts[2 * core].astype(jnp.bfloat16)
        edge_stage[j, 0, 2] = jnp.where(half, key_parts[1], pltpu.roll(value_parts[1], 64, 1)).astype(jnp.bfloat16)
        edge_stage[j, 1, 2] = jnp.where(half, pltpu.roll(key_parts[1], 64, 1), value_parts[1]).astype(jnp.bfloat16)
        for copy in edge_part_copies(j):
            copy.start()

    work(False)

    @pl.when(works_up)
    def _():
        for copy in own_copies:
            copy.wait()

        @pl.when(edge_first)
        def _():
            lax.fori_loop(0, CHIPS, lambda j, carry: (edge_work(j, arrived), carry)[1], 0)

        @pl.when(jnp.logical_not(edge_first))
        def _():
            for j in range(CHIPS):
                for i in range(2):
                    arrived(i, j)

        for g in range(2):
            k_buf[g, pl.ds(96, ABLOCK)] = k_edge[g + 1]
            v_buf[g, pl.ds(96, ABLOCK)] = v_edge[g + 1]

    work(True)

    @pl.when(works_up & jnp.logical_not(edge_first))
    def _():
        lax.fori_loop(0, CHIPS, lambda j, carry: (edge_work(j, lambda i, j: None), carry)[1], 0)

    for core, copies in halo_down:

        @pl.when(sends_down & (c == core))
        def _():
            for copy in copies:
                copy.wait_send()

    @pl.when(works_up)
    def _():
        for j in range(CHIPS):
            for copy in edge_part_copies(j):
                copy.wait_send()

    for chip, copies in halo_up:

        @pl.when((y == chip) & (c == 0) & has_after)
        def _():
            for copy in copies:
                copy.wait_send()

    for copy in small:
        copy.wait_send()
    for g in range(2):
        for copy in swap_copies(g, c):
            copy.wait_send()
        dq_copies(g, c)[0].wait()
        dq_copies(g, other)[1].wait()
    for p in (None, 0, 1):
        part_copies(p, (0, 1), lambda copy: copy.wait_send(), lambda copy: None)
    for chip in range(CHIPS):
        for p, (start, size) in enumerate(PARTS):
            part = landed.at[chip, :, pl.ds(start, size)]
            arrival = pltpu.make_async_copy(part, part, part_recv.at[chip, p])
            if p == 0 and chip == 0:
                pl.when(has_after)(arrival.wait)
            elif p == 2 and chip == CHIPS - 1:
                pl.when(has_before)(arrival.wait)
            else:
                arrival.wait()


def finish(dq_in, landed, dq_hbm, dk_hbm, dv_hbm, dk_buf, dv_buf, sem):
    c = lax.axis_index("audio") % 2
    dq_copy = pltpu.make_async_copy(dq_in, dq_hbm, sem.at[0])
    dq_copy.start()
    head_rows = pl.ds(pl.multiple_of(64 * c, 64), 128)
    middle_rows = pl.ds(pl.multiple_of(128 - 128 * c, 64), 64)
    for pair in range(2):
        rows = slice(pair * 128, (pair + 1) * 128)
        tiles = []
        for t in range(3):
            blocks = []
            for chip in (2 * pair, 2 * pair + 1):
                for own, far_chip, far in ((32, (chip + 3) % CHIPS, 96), (64, (chip + 1) % CHIPS, 0)):
                    own_term = landed[chip, t, own : own + ABLOCK].astype(jnp.float32)
                    blocks.append(own_term + landed[far_chip, t, far : far + ABLOCK].astype(jnp.float32))
            tiles.append(jnp.concatenate(blocks, axis=0).T.astype(jnp.bfloat16))
        dk_buf[head_rows, rows] = tiles[0]
        dv_buf[head_rows, rows] = tiles[1]
        dk_buf[middle_rows, rows] = tiles[2][0:64]
        dv_buf[middle_rows, rows] = tiles[2][64:128]
    copies = [pltpu.make_async_copy(dk_buf, dk_hbm, sem.at[1]), pltpu.make_async_copy(dv_buf, dv_hbm, sem.at[2])]
    for copy in copies:
        copy.start()
    for copy in [dq_copy] + copies:
        copy.wait()


def on_device(queries, keys, values, out_grad, delta, window_low, window_high):
    bf16, f32 = jnp.bfloat16, jnp.float32
    hbm, vmem = pl.BlockSpec(memory_space=pltpu.HBM), pl.BlockSpec(memory_space=pltpu.VMEM)
    dma = pltpu.SemaphoreType.DMA
    arrays = (queries, keys, values, out_grad, delta, window_low, window_high)
    arrays = [pltpu.with_memory_space_constraint(array, pltpu.HBM) for array in arrays]
    query_grad, landed = pl.pallas_call(
        kernel,
        out_shape=(pltpu.VMEM((ROWS, 1536), bf16), pltpu.VMEM((CHIPS, 3, AROWS, HEAD_DIM), bf16)),
        in_specs=[hbm] * 7,
        out_specs=(vmem, vmem),
        scratch_shapes=[
            pltpu.VMEM((2, 2, ROWS, GROUP), bf16),
            pltpu.VMEM((2, 2, ROWS, GROUP), bf16),
            pltpu.VMEM((2, AROWS, GROUP), bf16),
            pltpu.VMEM((2, AROWS, GROUP), bf16),
            pltpu.VMEM((2, 3, ABLOCK, GROUP), bf16),
            pltpu.VMEM((CHIPS, ROWS, GROUP), bf16),
            pltpu.VMEM((CHIPS, ROWS, GROUP), bf16),
            pltpu.VMEM((CHIPS, 2 * ABLOCK, GROUP), bf16),
            pltpu.VMEM((CHIPS, ABLOCK, GROUP), bf16),
            pltpu.VMEM((CHIPS, ABLOCK, GROUP), bf16),
            pltpu.VMEM((CHIPS, 2, 3, ABLOCK, HEAD_DIM), bf16),
            pltpu.VMEM((2, 12, ROWS), f32),
            pltpu.VMEM((2, 8, ROWS), f32),
            pltpu.VMEM((2, REACH, ROWS), f32),
            pltpu.VMEM((2, 2, ROWS, GROUP), bf16),
            pltpu.VMEM((2, 3, 2 * ABLOCK, HEAD_DIM), f32),
            pltpu.VMEM((2, 3, 2 * ABLOCK, HEAD_DIM), f32),
            pltpu.VMEM((2, 2, 3, AROWS, HEAD_DIM), bf16),
            pltpu.SMEM((2,), jnp.int32),
            pltpu.SMEM((2,), jnp.int32),
            dma((2,)),
            dma(()),
            dma((2, 2)),
            dma((2, 2)),
            dma((2, 3)),
            dma((3, CHIPS)),
            dma((2,)),
            dma((2, 2)),
            dma((2, 2)),
            dma((2,)),
            dma((2,)),
            dma((2, 2, 2)),
            dma((2, 2)),
            dma((2, 2)),
            dma((2, CHIPS)),
            dma((CHIPS, 2)),
            dma((2, 2, 3)),
            dma((CHIPS, 3)),
            dma((2,)),
            dma((2,)),
            pltpu.SemaphoreType.REGULAR,
        ],
        compiler_params=pltpu.CompilerParams(
            collective_id=0, has_side_effects=True, vmem_limit_bytes=32 << 20
        ),
        name="attention_backward",
    )(*arrays)
    query_grad, key_grad, value_grad = pl.pallas_call(
        finish,
        out_shape=(
            jax.ShapeDtypeStruct((ROWS, 1536), bf16),
            jax.ShapeDtypeStruct((192, 256), bf16),
            jax.ShapeDtypeStruct((192, 256), bf16),
        ),
        in_specs=[vmem, vmem],
        out_specs=(hbm, hbm, hbm),
        scratch_shapes=[pltpu.VMEM((192, 256), bf16), pltpu.VMEM((192, 256), bf16), dma((3,))],
        compiler_params=pltpu.CompilerParams(vmem_limit_bytes=32 << 20),
        name="sum_partials",
    )(query_grad, landed)
    return query_grad, key_grad.T, value_grad.T


def solution(mesh):
    return jax.shard_map(
        on_device,
        mesh=mesh,
        in_specs=(
            P(("video", "audio"), None),
            P("video", None),
            P("video", None),
            P(("video", "audio"), None),
            P(None, ("video", "audio")),
            P(("video", "audio")),
            P(("video", "audio")),
        ),
        out_specs=(P(("video", "audio"), None), P("video", "audio"), P("video", "audio")),
        check_vma=False,
    )
```

```python
import math

import jax
import jax.numpy as jnp
from jax import lax
from jax.experimental import pallas as pl
from jax.experimental.pallas import tpu as pltpu
from jax.sharding import PartitionSpec as P

HEAD_DIM = 128
VBLOCK = 64
ABLOCK = 32
SPANS = 64
CHIPS = 4
ROWS = 128
AROWS = 128
REACH = 96
GROUP = 384

MESH = pl.DeviceIdType.MESH
masked_score = -1e30
logit_scale = 1.0 / math.sqrt(HEAD_DIM)


def nt(a, b):
    return lax.dot_general(a, b, (((1,), (1,)), ((), ())), preferred_element_type=jnp.float32)


def nn(a, b):
    return lax.dot_general(a, b, (((1,), (0,)), ((), ())), preferred_element_type=jnp.float32)


def tn(a, b):
    return lax.dot_general(a, b, (((0,), (0,)), ((), ())), preferred_element_type=jnp.float32)


def kernel(
    q_hbm, k_hbm, v_hbm, og_hbm, delta_hbm, low_hbm, high_hbm,
    dq_out, landed,
    rows_buf, audio_buf, edge_buf, own_rows, k_own, edge_kv, edge_stage, delta_own, small_buf, bias_buf, dq_buf,
    key_sum, value_sum, stage, gauge,
    low_smem, high_smem,
    win_sem, delta_sem, rows_sem, audio_sem, edge_sem, own_sem, out_sem,
    swap_send, swap_recv, small_send, small_recv, halo_send, halo_recv, edge_send, edge_recv, edge_part_send,
    part_send, part_recv, dq_send, dq_recv, part_ready,
):
    v = lax.axis_index("video")
    a = lax.axis_index("audio")
    y, c = a // 2, a % 2
    other = 1 - c
    partner = (v, 2 * y + other)
    q_buf, og_buf = rows_buf.at[0], rows_buf.at[1]
    k_buf, v_buf = audio_buf.at[0], audio_buf.at[1]
    q_own, og_own = own_rows.at[0], own_rows.at[1]
    has_before, has_after = v > 0, v < SPANS - 1
    is_first, is_last = y == 0, y == CHIPS - 1

    def role(chip, core):
        return jnp.where(chip == CHIPS - 1, 1 - core, core)

    def group_of(chip, core, g):
        return (chip + jnp.where(role(chip, core) == 0, 1 - g, 2 + g)) % CHIPS

    def signal(semaphore, device):
        pl.semaphore_signal(semaphore, inc=1, device_id=device, device_id_type=MESH)

    barrier = pltpu.get_barrier_semaphore()

    @pl.when(is_last & has_after & (c == 1))
    def _():
        signal(barrier, (v + 1, 7))
        signal(barrier, (v + 1, 6))

    signal(barrier, partner)

    @pl.when(has_before)
    def _():
        signal(barrier, (v - 1, 7))

        @pl.when(is_first)
        def _():
            for i in range(4):
                signal(barrier, (v - 1, 4 * c + i))

        @pl.when(is_first & (c == 1))
        def _():
            signal(barrier, (v - 1, 0))

    for ahead, part in ((3, 0), (2, 1), (1, 1)):
        chip = (y + ahead) % CHIPS
        signal(barrier, (v, 2 * chip + role(chip, part)))

    low_copy = pltpu.make_async_copy(low_hbm, low_smem, win_sem.at[0])
    high_copy = pltpu.make_async_copy(high_hbm, high_smem, win_sem.at[1])
    delta_copy = pltpu.make_async_copy(delta_hbm, delta_own, delta_sem)
    low_copy.start()
    high_copy.start()
    delta_copy.start()

    def lanes(k):
        return pl.ds(pl.multiple_of(k * GROUP, GROUP), GROUP)

    def landed_wait(ref, sem):
        pltpu.make_async_copy(ref, ref, sem).wait()

    def sent_wait(ref, sem):
        pltpu.make_async_remote_copy(
            ref, ref, sem, dq_recv, device_id=partner, device_id_type=MESH
        ).wait_send()

    def row_copies(g):
        k = group_of(y, c, g)
        return [
            pltpu.make_async_copy(q_hbm.at[:, lanes(k)], q_buf.at[g, c], rows_sem),
            pltpu.make_async_copy(og_hbm.at[:, lanes(k)], og_buf.at[g, c], rows_sem),
        ]

    reaches = ((is_first, 0, 32, 96), (is_last, 160, 0, 96), ((y > 0) & (y < CHIPS - 1), 64 * y - 32, 0, AROWS))

    def audio_start(g):
        k = group_of(y, c, g)
        for chosen, first, target, count in reaches:

            @pl.when(chosen)
            def _():
                for source, buf in ((k_hbm, k_buf), (v_hbm, v_buf)):
                    rows = pl.ds(first if isinstance(first, int) else pl.multiple_of(first, 32), count)
                    pltpu.make_async_copy(source.at[rows, lanes(k)], buf.at[g, pl.ds(target, count)], audio_sem).start()

    def audio_wait():
        for chosen, _, target, count in reaches:

            @pl.when(chosen)
            def _():
                landed_wait(audio_buf.at[:, :, pl.ds(target, count)], audio_sem)

    sends_down = is_last & has_before
    works_up = is_last & has_after & (c == 1)
    edge_first, edge_early = v % 16 == 15, v % 16 == 0

    @pl.when(sends_down)
    def _():
        for n in range(2):
            for i, source in enumerate((k_hbm, v_hbm)):
                pltpu.make_async_copy(
                    source.at[pl.ds(0, ABLOCK), lanes(2 - 2 * c + n)], edge_buf.at[n, i], edge_sem
                ).start()

    own_copies = []
    for j in range(CHIPS):
        k = j
        own_copies += [
            pltpu.make_async_copy(q_hbm.at[:, lanes(k)], q_own.at[j], own_sem.at[0]),
            pltpu.make_async_copy(og_hbm.at[:, lanes(k)], og_own.at[j], own_sem.at[0]),
            pltpu.make_async_copy(k_hbm.at[pl.ds(192, 2 * ABLOCK), lanes(k)], k_own.at[j], own_sem.at[1]),
        ]

    for g in range(2):
        for copy in row_copies(g):
            copy.start()
        audio_start(g)

    @pl.when(works_up)
    def _():
        for copy in own_copies:
            copy.start()

    @pl.when(sends_down)
    def _():
        landed_wait(edge_buf, edge_sem)

    @pl.when(jnp.logical_not(has_before))
    def _():
        landed[3, :, 96:128] = jnp.zeros((3, ABLOCK, HEAD_DIM), jnp.bfloat16)

        @pl.when(is_first)
        def _():
            audio_buf[:, :, 0:32] = jnp.zeros((2, 2, ABLOCK, GROUP), jnp.bfloat16)

    @pl.when(jnp.logical_not(has_after))
    def _():
        landed[0, :, 0:32] = jnp.zeros((3, ABLOCK, HEAD_DIM), jnp.bfloat16)

        @pl.when(is_last)
        def _():
            audio_buf[:, :, 96:128] = jnp.zeros((2, 2, ABLOCK, GROUP), jnp.bfloat16)

    from_after = 1 + jnp.where(is_last, 8 * c, 0) + jnp.where(is_first, other, 0)
    from_before = jnp.where(is_last, 1, 0)
    pl.semaphore_wait(barrier, 3 + 2 * role(y, c) + jnp.where(has_after, from_after, 0) + jnp.where(has_before, from_before, 0))

    def up_copies(i, core):
        return [
            pltpu.make_async_remote_copy(
                (k_hbm, v_hbm)[i].at[pl.ds(224, ABLOCK), lanes(group_of(0, core, g))],
                (k_buf, v_buf)[i].at[g, pl.ds(0, ABLOCK)],
                halo_send, halo_recv.at[i], device_id=(v + 1, core), device_id_type=MESH,
            )
            for g in range(2)
        ]

    halo_up = (
        (0, [copy for pair in zip(up_copies(0, 0), up_copies(0, 1)) for copy in pair]),
        (1, up_copies(1, 0)),
        (CHIPS - 1, up_copies(1, 1)),
    )
    @pl.when(sends_down)
    def _():
        for n in range(2):
            j = 2 - 2 * c + n
            pltpu.make_async_remote_copy(
                edge_buf.at[n], edge_kv.at[j], edge_send, edge_recv.at[j], device_id=(v - 1, 7), device_id_type=MESH
            ).start()

    @pl.when(has_after)
    def _():
        for chip, copies in halo_up:

            @pl.when((y == chip) & (c == 0))
            def _():
                for copy in copies:
                    copy.start()

        signal(part_ready, (v + 1, y // 2))

    def swap_copies(g, slot):
        k = group_of(y, other, g)
        return [
            pltpu.make_async_remote_copy(
                source.at[:, lanes(k)], target.at[g, slot], swap_send, swap_recv,
                device_id=partner, device_id_type=MESH,
            )
            for source, target in ((q_hbm, q_buf), (og_hbm, og_buf))
        ]

    for g in range(2):
        for copy in swap_copies(g, c):
            copy.start()

    def arrived(j):
        landed_wait(edge_kv.at[j], edge_recv.at[j])

    hand_on = [
        pltpu.make_async_remote_copy(
            edge_kv.at[1 + g, i], buf.at[g, pl.ds(96, ABLOCK)], halo_send, halo_recv.at[i],
            device_id=partner, device_id_type=MESH,
        )
        for g in range(2)
        for i, buf in enumerate((k_buf, v_buf))
    ]

    @pl.when(works_up & edge_early)
    def _():
        for j in range(CHIPS):
            arrived(j)
        for copy in hand_on:
            copy.start()

    low_copy.wait()
    high_copy.wait()
    lane = lax.broadcasted_iota(jnp.int32, (8, ROWS), 1)
    row = lax.broadcasted_iota(jnp.int32, (8, ROWS), 0)
    lows = jnp.where(lane < VBLOCK, low_smem[0], low_smem[1])
    highs = jnp.where(lane < VBLOCK, high_smem[0], high_smem[1])
    delta_copy.wait()
    small_buf[c, 0:8] = jnp.where(row == 0, lows, highs).astype(jnp.float32)
    small_buf[c, 8:20] = delta_own[...]
    small_buf[c, 20:24] = jnp.zeros((4, ROWS), jnp.float32)
    small = pltpu.make_async_remote_copy(
        small_buf.at[c], small_buf.at[c], small_send, small_recv, device_id=partner, device_id_type=MESH
    )
    small.start()
    small.wait_recv()

    row = lax.broadcasted_iota(jnp.int32, (REACH, ROWS), 0)
    for slot in range(2):
        blocks = 8 * v + 2 * y + jnp.where(row < 2 * ABLOCK, row // ABLOCK, 3 * slot - 1)
        blocks = blocks.astype(jnp.float32)
        inside = (blocks >= small_buf[slot, 0:1, :]) & (blocks < small_buf[slot, 1:2, :])
        bias_buf[slot] = jnp.where(inside, 0.0, masked_score)

    def part_copies(slot, groups, do, do_local):
        if slot is None:
            start, size, span, exists = ABLOCK, 2 * ABLOCK, v, True
        else:
            start, size = pl.multiple_of(REACH * slot, ABLOCK), ABLOCK
            down, up = is_first & (slot == 0), is_last & (slot == 1)
            span = v - jnp.where(down, 1, 0)
            exists = jnp.logical_not(down & jnp.logical_not(has_before)) & jnp.logical_not(up)
        for g in groups:
            k = group_of(y, c, g)
            for core in range(2):
                source = stage.at[g, core, :, pl.ds(start, size)]
                target = landed.at[y, :, pl.ds(start, size)]
                here = (span == v) & (2 * k + core == a) & exists
                away = jnp.logical_not(here) if g == 1 else True

                @pl.when(away & exists)
                def _():
                    do(
                        pltpu.make_async_remote_copy(
                            source, target, part_send, part_recv,
                            device_id=(span, 2 * k + core), device_id_type=MESH,
                        )
                    )

                if g == 1:

                    @pl.when(here)
                    def _():
                        do_local(pltpu.make_async_copy(source, target, part_recv))

    def dq_copies(g, slot):
        k = group_of(y, c, g)
        return (
            pltpu.make_async_copy(dq_buf.at[g, slot], dq_out.at[:, lanes(k)], out_sem),
            pltpu.make_async_remote_copy(
                dq_buf.at[g, slot], dq_out.at[:, lanes(k)], dq_send, dq_recv,
                device_id=partner, device_id_type=MESH,
            ),
        )

    def work(last):
        slot = jnp.where(is_first, 1, 0)
        if last:
            slot = 1 - slot

        @pl.when(slot == c)
        def _():
            landed_wait(rows_buf.at[:, :, slot], rows_sem)

        @pl.when(slot != c)
        def _():
            landed_wait(rows_buf.at[:, :, slot], swap_recv)

        def halo_wait(i):
            if last:

                @pl.when((is_first & has_before) | (is_last & has_after & (c == 0)))
                def _():
                    landed_wait(audio_buf.at[i, :, pl.ds(0, ABLOCK)], halo_recv.at[i])

        def start(copy):
            copy.start()

        def put(heads, rows, key_parts, value_parts):
            for (g, i, _), key_part, value_part in zip(heads, key_parts, value_parts):
                if i == 1:
                    half = lax.broadcasted_iota(jnp.int32, key_part.shape, 1) < HEAD_DIM // 2
                    stage[g, 0, 2, rows] = jnp.where(half, key_part, pltpu.roll(value_part, 64, 1)).astype(jnp.bfloat16)
                    stage[g, 1, 2, rows] = jnp.where(half, pltpu.roll(key_part, 64, 1), value_part).astype(jnp.bfloat16)
                else:
                    stage[g, i // 2, 0, rows] = key_part.astype(jnp.bfloat16)
                    stage[g, i // 2, 1, rows] = value_part.astype(jnp.bfloat16)

        if not last:
            audio_wait()
        middle = pl.ds(ABLOCK, 2 * ABLOCK)
        alone = pl.ds(pl.multiple_of(REACH * slot, ABLOCK), ABLOCK)
        bias = bias_buf[slot]

        def gradients(groups):
            heads = [(g, i, slice(i * HEAD_DIM, (i + 1) * HEAD_DIM)) for g in groups for i in range(3)]
            deltas = [small_buf[slot, pl.ds(8 + 3 * group_of(y, c, g) + i, 1), :] for g, i, _ in heads]

            if 0 in groups:
                halo_wait(0)
            keys = [jnp.concatenate([k_buf[g, middle, cols], k_buf[g, alone, cols]], axis=0) for g, _, cols in heads]
            scores = [nt(key, q_buf[g, slot, :, cols]) for key, (g, _, cols) in zip(keys, heads)]
            prob_grads = [nt(v_buf[g, middle, cols], og_buf[g, slot, :, cols]) for g, _, cols in heads]
            probs, prob_halves, middle_halves = [], [], []
            for score, prob_grad, delta in zip(scores, prob_grads, deltas):
                score = score + bias
                peak = jnp.max(score, axis=0, keepdims=True)
                weights = jnp.exp2((score - peak) * (logit_scale * math.log2(math.e)))
                prob = weights * (1.0 / jnp.sum(weights, axis=0, keepdims=True))
                probs.append(prob[64:96])
                prob_halves.append(prob.astype(jnp.bfloat16))
                middle_halves.append((prob[0:64] * (prob_grad - delta)).astype(jnp.bfloat16))
            value_parts = [nn(prob, og_buf[g, slot, :, cols]) for prob, (g, _, cols) in zip(prob_halves, heads)]
            key_parts = [nn(score, q_buf[g, slot, :, cols]) * logit_scale for score, (g, _, cols) in zip(middle_halves, heads)]
            if last:
                key_parts = [part + key_sum[g, i] for part, (g, i, _) in zip(key_parts, heads)]
                middle_values = [part[0:64] + value_sum[g, i] for part, (g, i, _) in zip(value_parts, heads)]
                put(heads, middle, key_parts, middle_values)

                part_copies(None, groups, start, start)
            else:
                for key_part, value_part, (g, i, _) in zip(key_parts, value_parts, heads):
                    key_sum[g, i] = key_part
                    value_sum[g, i] = value_part[0:64]

            return heads, deltas, keys, probs, middle_halves, value_parts

        def edge_gradients(groups, heads, deltas, keys, probs, middle_halves, value_parts):
            halo_wait(1)
            prob_grads = [nt(v_buf[g, alone, cols], og_buf[g, slot, :, cols]) for g, _, cols in heads]
            alone_halves = [
                (prob * (prob_grad - delta)).astype(jnp.bfloat16) for prob, prob_grad, delta in zip(probs, prob_grads, deltas)
            ]
            key_parts = [nn(score, q_buf[g, slot, :, cols]) * logit_scale for score, (g, _, cols) in zip(alone_halves, heads)]
            put(heads, alone, key_parts, [part[64:96] for part in value_parts])
            if last:

                @pl.when(is_first & has_before & (0 in groups))
                def _():
                    pl.semaphore_wait(part_ready, 4)

            part_copies(slot, groups if last else (0,), start, start)
            return list(zip(heads, keys, middle_halves, alone_halves))

        if last:
            first = gradients((0,))
            part_copies(1 - slot, (1,), start, start)
            second = gradients((1,))
            done = edge_gradients((0, 1), *[one + other for one, other in zip(first, second)])
        else:
            done = edge_gradients((0, 1), *gradients((0, 1)))
        for (g, _, cols), key, first, second in done:
            score_half = jnp.concatenate([first, second], axis=0)
            dq_buf[g, slot, :, cols] = (tn(score_half, key) * logit_scale).astype(jnp.bfloat16)

        @pl.when(slot == c)
        def _():
            for g in range(2):
                dq_copies(g, slot)[0].start()

        @pl.when(slot != c)
        def _():
            for g in range(2):
                dq_copies(g, slot)[1].start()

    def edge_part_copies(j):
        return [
            pltpu.make_async_remote_copy(
                edge_stage.at[j, core], landed.at[CHIPS - 1, :, pl.ds(96, ABLOCK)],
                edge_part_send, part_recv,
                device_id=(v + 1, 2 * j + core), device_id_type=MESH,
            )
            for core in range(2)
        ]

    def edge_work(j, wait):
        heads = [slice(i * HEAD_DIM, (i + 1) * HEAD_DIM) for i in range(3)]
        bias = bias_buf[1]
        deltas = [small_buf[1, pl.ds(8 + 3 * j + i, 1), :] for i in range(3)]
        wait(j)
        keys = [jnp.concatenate([k_own[j, :, cols], edge_kv[j, 0, :, cols]], axis=0) for cols in heads]
        scores = [nt(key, q_own[j, :, cols]) + bias for key, cols in zip(keys, heads)]
        probs = []
        for score in scores:
            weights = jnp.exp2((score - jnp.max(score, axis=0, keepdims=True)) * (logit_scale * math.log2(math.e)))
            probs.append(weights[64:96] * (1.0 / jnp.sum(weights, axis=0, keepdims=True)))
        value_parts = [nn(prob.astype(jnp.bfloat16), og_own[j, :, cols]) for prob, cols in zip(probs, heads)]
        prob_grads = [nt(edge_kv[j, 1, :, cols], og_own[j, :, cols]) for cols in heads]
        halves = [(p * (grad - delta)).astype(jnp.bfloat16) for p, grad, delta in zip(probs, prob_grads, deltas)]
        key_parts = [nn(score, q_own[j, :, cols]) * logit_scale for score, cols in zip(halves, heads)]
        half = lax.broadcasted_iota(jnp.int32, (ABLOCK, HEAD_DIM), 1) < HEAD_DIM // 2
        for core in range(2):
            edge_stage[j, core, 0] = key_parts[2 * core].astype(jnp.bfloat16)
            edge_stage[j, core, 1] = value_parts[2 * core].astype(jnp.bfloat16)
        edge_stage[j, 0, 2] = jnp.where(half, key_parts[1], pltpu.roll(value_parts[1], 64, 1)).astype(jnp.bfloat16)
        edge_stage[j, 1, 2] = jnp.where(half, pltpu.roll(key_parts[1], 64, 1), value_parts[1]).astype(jnp.bfloat16)
        for copy in edge_part_copies(j):
            copy.start()

    work(False)

    @pl.when(works_up)
    def _():
        landed_wait(own_rows, own_sem.at[0])
        landed_wait(k_own, own_sem.at[1])

        @pl.when(edge_first)
        def _():
            lax.fori_loop(0, CHIPS, lambda j, carry: (edge_work(j, arrived), carry)[1], 0)

        @pl.when(jnp.logical_not(edge_first | edge_early))
        def _():
            for j in range(CHIPS):
                arrived(j)

        @pl.when(jnp.logical_not(edge_early))
        def _():
            for copy in hand_on:
                copy.start()

        for g in range(2):
            for i in range(2):
                audio_buf[i, g, pl.ds(96, ABLOCK)] = edge_kv[3 * g, i]

    work(True)

    @pl.when(works_up & jnp.logical_not(edge_first))
    def _():
        lax.fori_loop(0, CHIPS, lambda j, carry: (edge_work(j, lambda j: None), carry)[1], 0)

    @pl.when(sends_down)
    def _():
        sent_wait(edge_buf, edge_send)

    @pl.when(works_up)
    def _():
        sent_wait(gauge.at[pl.ds(0, 4)], halo_send)
        sent_wait(edge_stage, edge_part_send)

    for chip, copies in halo_up:

        @pl.when((y == chip) & (c == 0) & has_after)
        def _():
            sent_wait(gauge.at[pl.ds(0, len(copies))], halo_send)

    small.wait_send()
    sent_wait(rows_buf.at[:, :, c], swap_send)
    landed_wait(dq_buf.at[:, c], out_sem)
    sent_wait(dq_buf.at[:, other], dq_send)
    landed_wait(dq_buf.at[:, other], dq_recv)

    copies = 4 - (1 - role(y, c))
    to_before = jnp.where(has_before, 4, 0)
    units = 3 * copies + jnp.where(is_first, to_before, jnp.where(is_last, 0, copies))
    for count in (9, 12, 13, 16):

        @pl.when(units == count)
        def _():
            sent_wait(gauge.at[pl.ds(0, count)], part_send)

    @pl.when(has_before & has_after)
    def _():
        landed_wait(gauge, part_recv)

    @pl.when(jnp.logical_not(has_before & has_after))
    def _():
        landed_wait(gauge.at[pl.ds(0, 15)], part_recv)


def finish(dq_in, landed, dq_hbm, dk_hbm, dv_hbm, dk_buf, dv_buf, sem):
    c = lax.axis_index("audio") % 2
    dq_copy = pltpu.make_async_copy(dq_in, dq_hbm, sem.at[0])
    dq_copy.start()
    head_rows = pl.ds(pl.multiple_of(64 * c, 64), 128)
    middle_rows = pl.ds(pl.multiple_of(128 - 128 * c, 64), 64)
    for pair in range(2):
        rows = slice(pair * 128, (pair + 1) * 128)
        tiles = []
        for t in range(3):
            blocks = []
            for chip in (2 * pair, 2 * pair + 1):
                for own, far_chip, far in ((32, (chip + 3) % CHIPS, 96), (64, (chip + 1) % CHIPS, 0)):
                    own_term = landed[chip, t, own : own + ABLOCK].astype(jnp.float32)
                    blocks.append(own_term + landed[far_chip, t, far : far + ABLOCK].astype(jnp.float32))
            tiles.append(jnp.concatenate(blocks, axis=0).T.astype(jnp.bfloat16))
        dk_buf[head_rows, rows] = tiles[0]
        dv_buf[head_rows, rows] = tiles[1]
        dk_buf[middle_rows, rows] = tiles[2][0:64]
        dv_buf[middle_rows, rows] = tiles[2][64:128]
    copies = [pltpu.make_async_copy(dk_buf, dk_hbm, sem.at[1]), pltpu.make_async_copy(dv_buf, dv_hbm, sem.at[2])]
    for copy in copies:
        copy.start()
    for copy in [dq_copy] + copies:
        copy.wait()


def on_device(queries, keys, values, out_grad, delta, window_low, window_high):
    bf16, f32 = jnp.bfloat16, jnp.float32
    hbm, vmem = pl.BlockSpec(memory_space=pltpu.HBM), pl.BlockSpec(memory_space=pltpu.VMEM)
    dma = pltpu.SemaphoreType.DMA
    arrays = (queries, keys, values, out_grad, delta, window_low, window_high)
    arrays = [pltpu.with_memory_space_constraint(array, pltpu.HBM) for array in arrays]
    query_grad, landed = pl.pallas_call(
        kernel,
        out_shape=(pltpu.VMEM((ROWS, 1536), bf16), pltpu.VMEM((CHIPS, 3, AROWS, HEAD_DIM), bf16)),
        in_specs=[hbm] * 7,
        out_specs=(vmem, vmem),
        scratch_shapes=[
            pltpu.VMEM((2, 2, 2, ROWS, GROUP), bf16),
            pltpu.VMEM((2, 2, AROWS, GROUP), bf16),
            pltpu.VMEM((2, 2, ABLOCK, GROUP), bf16),
            pltpu.VMEM((2, CHIPS, ROWS, GROUP), bf16),
            pltpu.VMEM((CHIPS, 2 * ABLOCK, GROUP), bf16),
            pltpu.VMEM((CHIPS, 2, ABLOCK, GROUP), bf16),
            pltpu.VMEM((CHIPS, 2, 3, ABLOCK, HEAD_DIM), bf16),
            pltpu.VMEM((12, ROWS), f32),
            pltpu.VMEM((2, 24, ROWS), f32),
            pltpu.VMEM((2, REACH, ROWS), f32),
            pltpu.VMEM((2, 2, ROWS, GROUP), bf16),
            pltpu.VMEM((2, 3, 2 * ABLOCK, HEAD_DIM), f32),
            pltpu.VMEM((2, 3, 2 * ABLOCK, HEAD_DIM), f32),
            pltpu.VMEM((2, 2, 3, AROWS, HEAD_DIM), bf16),
            pltpu.VMEM((16, ABLOCK, GROUP), bf16),
            pltpu.SMEM((2,), jnp.int32),
            pltpu.SMEM((2,), jnp.int32),
            dma((2,)),
            dma(()),
            dma(()),
            dma(()),
            dma(()),
            dma((2,)),
            dma(()),
            dma(()),
            dma(()),
            dma(()),
            dma(()),
            dma(()),
            dma((2,)),
            dma(()),
            dma((CHIPS,)),
            dma(()),
            dma(()),
            dma(()),
            dma(()),
            dma(()),
            pltpu.SemaphoreType.REGULAR,
        ],
        compiler_params=pltpu.CompilerParams(
            collective_id=0, has_side_effects=True, vmem_limit_bytes=32 << 20
        ),
        name="attention_backward",
    )(*arrays)
    query_grad, key_grad, value_grad = pl.pallas_call(
        finish,
        out_shape=(
            jax.ShapeDtypeStruct((ROWS, 1536), bf16),
            jax.ShapeDtypeStruct((192, 256), bf16),
            jax.ShapeDtypeStruct((192, 256), bf16),
        ),
        in_specs=[vmem, vmem],
        out_specs=(hbm, hbm, hbm),
        scratch_shapes=[pltpu.VMEM((192, 256), bf16), pltpu.VMEM((192, 256), bf16), dma((3,))],
        compiler_params=pltpu.CompilerParams(vmem_limit_bytes=32 << 20),
        name="sum_partials",
    )(query_grad, landed)
    return query_grad, key_grad.T, value_grad.T


def solution(mesh):
    return jax.shard_map(
        on_device,
        mesh=mesh,
        in_specs=(
            P(("video", "audio"), None),
            P("video", None),
            P("video", None),
            P(("video", "audio"), None),
            P(None, ("video", "audio")),
            P(("video", "audio")),
            P(("video", "audio")),
        ),
        out_specs=(P(("video", "audio"), None), P("video", "audio"), P("video", "audio")),
        check_vma=False,
    )
```

```python
import math

import jax
import jax.numpy as jnp
from jax import lax
from jax.experimental import pallas as pl
from jax.experimental.pallas import tpu as pltpu
from jax.sharding import PartitionSpec as P

HEAD_DIM = 128
VBLOCK = 64
ABLOCK = 32
SPANS = 64
CHIPS = 4
ROWS = 128
AROWS = 128
REACH = 96
GROUP = 384

MESH = pl.DeviceIdType.MESH
masked_score = -1e30
logit_scale = 1.0 / math.sqrt(HEAD_DIM)


def nt(a, b):
    return lax.dot_general(a, b, (((1,), (1,)), ((), ())), preferred_element_type=jnp.float32)


def nn(a, b):
    return lax.dot_general(a, b, (((1,), (0,)), ((), ())), preferred_element_type=jnp.float32)


def tn(a, b):
    return lax.dot_general(a, b, (((0,), (0,)), ((), ())), preferred_element_type=jnp.float32)


def kernel(
    q_hbm, k_hbm, v_hbm, og_hbm, delta_hbm, low_hbm, high_hbm,
    dq_out, landed,
    rows_buf, audio_buf, edge_buf, own_rows, k_own, edge_kv, edge_stage, delta_own, small_buf, bias_buf, dq_buf,
    key_sum, value_sum, stage, gauge,
    low_smem, high_smem,
    win_sem, delta_sem, rows_sem, audio_sem, edge_sem, own_sem, out_sem,
    swap_send, swap_recv, small_send, small_recv, halo_send, halo_recv, edge_send, edge_recv, edge_part_send,
    part_send, part_recv, dq_send, dq_recv, part_ready,
):
    v = lax.axis_index("video")
    a = lax.axis_index("audio")
    y, c = a // 2, a % 2
    other = 1 - c
    partner = (v, 2 * y + other)
    q_buf, og_buf = rows_buf.at[0], rows_buf.at[1]
    k_buf, v_buf = audio_buf.at[0], audio_buf.at[1]
    q_own, og_own = own_rows.at[0], own_rows.at[1]
    has_before, has_after = v > 0, v < SPANS - 1
    is_first, is_last = y == 0, y == CHIPS - 1

    def role(chip, core):
        return jnp.where(chip == CHIPS - 1, 1 - core, core)

    def group_of(chip, core, g):
        return (chip + jnp.where(role(chip, core) == 0, 1 - g, 2 + g)) % CHIPS

    def signal(semaphore, device):
        pl.semaphore_signal(semaphore, inc=1, device_id=device, device_id_type=MESH)

    barrier = pltpu.get_barrier_semaphore()

    @pl.when(is_last & has_after & (c == 1))
    def _():
        signal(barrier, (v + 1, 7))
        signal(barrier, (v + 1, 6))

    signal(barrier, partner)

    @pl.when(has_before)
    def _():
        signal(barrier, (v - 1, 7))

        @pl.when(is_first)
        def _():
            for i in range(4):
                signal(barrier, (v - 1, 4 * c + i))

        @pl.when(is_first & (c == 1))
        def _():
            signal(barrier, (v - 1, 0))

    for ahead, part in ((3, 0), (2, 1), (1, 1)):
        chip = (y + ahead) % CHIPS
        signal(barrier, (v, 2 * chip + role(chip, part)))

    low_copy = pltpu.make_async_copy(low_hbm, low_smem, win_sem.at[0])
    high_copy = pltpu.make_async_copy(high_hbm, high_smem, win_sem.at[1])
    delta_copy = pltpu.make_async_copy(delta_hbm, delta_own, delta_sem)
    low_copy.start()
    high_copy.start()
    delta_copy.start()

    def lanes(k):
        return pl.ds(pl.multiple_of(k * GROUP, GROUP), GROUP)

    def landed_wait(ref, sem):
        pltpu.make_async_copy(ref, ref, sem).wait()

    def sent_wait(ref, sem):
        pltpu.make_async_remote_copy(
            ref, ref, sem, dq_recv, device_id=partner, device_id_type=MESH
        ).wait_send()

    def row_copies(g):
        k = group_of(y, c, g)
        return [
            pltpu.make_async_copy(q_hbm.at[:, lanes(k)], q_buf.at[g, c], rows_sem),
            pltpu.make_async_copy(og_hbm.at[:, lanes(k)], og_buf.at[g, c], rows_sem),
        ]

    reaches = ((is_first, 0, 32, 96), (is_last, 160, 0, 96), ((y > 0) & (y < CHIPS - 1), 64 * y - 32, 0, AROWS))

    def audio_start(g):
        k = group_of(y, c, g)
        for chosen, first, target, count in reaches:

            @pl.when(chosen)
            def _():
                for source, buf in ((k_hbm, k_buf), (v_hbm, v_buf)):
                    rows = pl.ds(first if isinstance(first, int) else pl.multiple_of(first, 32), count)
                    pltpu.make_async_copy(source.at[rows, lanes(k)], buf.at[g, pl.ds(target, count)], audio_sem).start()

    def audio_wait():
        for chosen, _, target, count in reaches:

            @pl.when(chosen)
            def _():
                landed_wait(audio_buf.at[:, :, pl.ds(target, count)], audio_sem)

    sends_down = is_last & has_before
    works_up = is_last & has_after & (c == 1)
    edge_first, edge_early = v % 16 == 15, v % 16 == 0

    @pl.when(sends_down)
    def _():
        for n in range(2):
            for i, source in enumerate((k_hbm, v_hbm)):
                pltpu.make_async_copy(
                    source.at[pl.ds(0, ABLOCK), lanes(2 - 2 * c + n)], edge_buf.at[n, i], edge_sem
                ).start()

    own_copies = []
    for j in range(CHIPS):
        k = j
        own_copies += [
            pltpu.make_async_copy(q_hbm.at[:, lanes(k)], q_own.at[j], own_sem.at[0]),
            pltpu.make_async_copy(og_hbm.at[:, lanes(k)], og_own.at[j], own_sem.at[0]),
            pltpu.make_async_copy(k_hbm.at[pl.ds(192, 2 * ABLOCK), lanes(k)], k_own.at[j], own_sem.at[1]),
        ]

    for g in range(2):
        for copy in row_copies(g):
            copy.start()
        audio_start(g)

    @pl.when(works_up)
    def _():
        for copy in own_copies:
            copy.start()

    @pl.when(sends_down)
    def _():
        landed_wait(edge_buf, edge_sem)

    @pl.when(jnp.logical_not(has_before))
    def _():
        landed[3, :, 96:128] = jnp.zeros((3, ABLOCK, HEAD_DIM), jnp.bfloat16)

        @pl.when(is_first)
        def _():
            audio_buf[:, :, 0:32] = jnp.zeros((2, 2, ABLOCK, GROUP), jnp.bfloat16)

    @pl.when(jnp.logical_not(has_after))
    def _():
        landed[0, :, 0:32] = jnp.zeros((3, ABLOCK, HEAD_DIM), jnp.bfloat16)

        @pl.when(is_last)
        def _():
            audio_buf[:, :, 96:128] = jnp.zeros((2, 2, ABLOCK, GROUP), jnp.bfloat16)

    from_after = 1 + jnp.where(is_last, 8 * c, 0) + jnp.where(is_first, other, 0)
    from_before = jnp.where(is_last, 1, 0)
    pl.semaphore_wait(barrier, 3 + 2 * role(y, c) + jnp.where(has_after, from_after, 0) + jnp.where(has_before, from_before, 0))

    def up_copies(i, core):
        return [
            pltpu.make_async_remote_copy(
                (k_hbm, v_hbm)[i].at[pl.ds(224, ABLOCK), lanes(group_of(0, core, g))],
                (k_buf, v_buf)[i].at[g, pl.ds(0, ABLOCK)],
                halo_send, halo_recv.at[g if i == 0 else 2], device_id=(v + 1, core), device_id_type=MESH,
            )
            for g in range(2)
        ]

    halo_up = (
        (0, [copy for pair in zip(up_copies(0, 0), up_copies(0, 1)) for copy in pair]),
        (1, up_copies(1, 0)),
        (CHIPS - 1, up_copies(1, 1)),
    )
    @pl.when(sends_down)
    def _():
        for n in range(2):
            j = 2 - 2 * c + n
            for i in range(2):
                pltpu.make_async_remote_copy(
                    edge_buf.at[n, i], edge_kv.at[j, i], edge_send, edge_recv.at[j, i],
                    device_id=(v - 1, 7), device_id_type=MESH,
                ).start()

    @pl.when(has_after)
    def _():
        for chip, copies in halo_up:

            @pl.when((y == chip) & (c == 0))
            def _():
                for copy in copies:
                    copy.start()

        signal(part_ready, (v + 1, y // 2))

    def swap_copies(g, slot):
        k = group_of(y, other, g)
        return [
            pltpu.make_async_remote_copy(
                source.at[:, lanes(k)], target.at[g, slot], swap_send, swap_recv,
                device_id=partner, device_id_type=MESH,
            )
            for source, target in ((q_hbm, q_buf), (og_hbm, og_buf))
        ]

    for g in range(2):
        for copy in swap_copies(g, c):
            copy.start()

    def arrived(j, i):
        landed_wait(edge_kv.at[j, i], edge_recv.at[j, i])

    hand_on = [
        pltpu.make_async_remote_copy(
            edge_kv.at[1 + g, i], buf.at[g, pl.ds(96, ABLOCK)], halo_send, halo_recv.at[g if i == 0 else 2],
            device_id=partner, device_id_type=MESH,
        )
        for g in range(2)
        for i, buf in enumerate((k_buf, v_buf))
    ]

    @pl.when(works_up & edge_early)
    def _():
        for j in range(CHIPS):
            arrived(j, 0)
            arrived(j, 1)
        for copy in hand_on:
            copy.start()

    low_copy.wait()
    high_copy.wait()
    lane = lax.broadcasted_iota(jnp.int32, (8, ROWS), 1)
    row = lax.broadcasted_iota(jnp.int32, (8, ROWS), 0)
    lows = jnp.where(lane < VBLOCK, low_smem[0], low_smem[1])
    highs = jnp.where(lane < VBLOCK, high_smem[0], high_smem[1])
    delta_copy.wait()
    small_buf[c, 0:8] = jnp.where(row == 0, lows, highs).astype(jnp.float32)
    small_buf[c, 8:20] = delta_own[...]
    small_buf[c, 20:24] = jnp.zeros((4, ROWS), jnp.float32)
    small = pltpu.make_async_remote_copy(
        small_buf.at[c], small_buf.at[c], small_send, small_recv, device_id=partner, device_id_type=MESH
    )
    small.start()
    small.wait_recv()

    row = lax.broadcasted_iota(jnp.int32, (REACH, ROWS), 0)
    for slot in range(2):
        blocks = 8 * v + 2 * y + jnp.where(row < 2 * ABLOCK, row // ABLOCK, 3 * slot - 1)
        blocks = blocks.astype(jnp.float32)
        inside = (blocks >= small_buf[slot, 0:1, :]) & (blocks < small_buf[slot, 1:2, :])
        bias_buf[slot] = jnp.where(inside, 0.0, masked_score)

    def part_copies(slot, groups, do, do_local):
        if slot is None:
            start, size, span, exists = ABLOCK, 2 * ABLOCK, v, True
        else:
            start, size = pl.multiple_of(REACH * slot, ABLOCK), ABLOCK
            down, up = is_first & (slot == 0), is_last & (slot == 1)
            span = v - jnp.where(down, 1, 0)
            exists = jnp.logical_not(down & jnp.logical_not(has_before)) & jnp.logical_not(up)
        for g in groups:
            k = group_of(y, c, g)
            for core in range(2):
                source = stage.at[g, core, :, pl.ds(start, size)]
                target = landed.at[y, :, pl.ds(start, size)]
                here = (span == v) & (2 * k + core == a) & exists
                away = jnp.logical_not(here) if g == 1 else True

                @pl.when(away & exists)
                def _():
                    do(
                        pltpu.make_async_remote_copy(
                            source, target, part_send, part_recv,
                            device_id=(span, 2 * k + core), device_id_type=MESH,
                        )
                    )

                if g == 1:

                    @pl.when(here)
                    def _():
                        do_local(pltpu.make_async_copy(source, target, part_recv))

    def dq_copies(g, slot):
        k = group_of(y, c, g)
        return (
            pltpu.make_async_copy(dq_buf.at[g, slot], dq_out.at[:, lanes(k)], out_sem),
            pltpu.make_async_remote_copy(
                dq_buf.at[g, slot], dq_out.at[:, lanes(k)], dq_send, dq_recv,
                device_id=partner, device_id_type=MESH,
            ),
        )

    def work(last):
        slot = jnp.where(is_first, 1, 0)
        if last:
            slot = 1 - slot

        @pl.when(slot == c)
        def _():
            landed_wait(rows_buf.at[:, :, slot], rows_sem)

        @pl.when(slot != c)
        def _():
            landed_wait(rows_buf.at[:, :, slot], swap_recv)

        def halo_wait(ref, sem):
            if last:

                @pl.when((is_first & has_before) | (is_last & has_after & (c == 0)))
                def _():
                    landed_wait(ref, sem)

        def start(copy):
            copy.start()

        def put(heads, rows, key_parts, value_parts):
            for (g, i, _), key_part, value_part in zip(heads, key_parts, value_parts):
                if i == 1:
                    half = lax.broadcasted_iota(jnp.int32, key_part.shape, 1) < HEAD_DIM // 2
                    stage[g, 0, 2, rows] = jnp.where(half, key_part, pltpu.roll(value_part, 64, 1)).astype(jnp.bfloat16)
                    stage[g, 1, 2, rows] = jnp.where(half, pltpu.roll(key_part, 64, 1), value_part).astype(jnp.bfloat16)
                else:
                    stage[g, i // 2, 0, rows] = key_part.astype(jnp.bfloat16)
                    stage[g, i // 2, 1, rows] = value_part.astype(jnp.bfloat16)

        if not last:
            audio_wait()
        middle = pl.ds(ABLOCK, 2 * ABLOCK)
        alone = pl.ds(pl.multiple_of(REACH * slot, ABLOCK), ABLOCK)
        bias = bias_buf[slot]

        def gradients(groups):
            heads = [(g, i, slice(i * HEAD_DIM, (i + 1) * HEAD_DIM)) for g in groups for i in range(3)]
            deltas = [small_buf[slot, pl.ds(8 + 3 * group_of(y, c, g) + i, 1), :] for g, i, _ in heads]

            for g in groups:
                halo_wait(k_buf.at[g, pl.ds(0, ABLOCK)], halo_recv.at[g])
            keys = [jnp.concatenate([k_buf[g, middle, cols], k_buf[g, alone, cols]], axis=0) for g, _, cols in heads]
            scores = [nt(key, q_buf[g, slot, :, cols]) for key, (g, _, cols) in zip(keys, heads)]
            prob_grads = [nt(v_buf[g, middle, cols], og_buf[g, slot, :, cols]) for g, _, cols in heads]
            probs, prob_halves, middle_halves = [], [], []
            for score, prob_grad, delta in zip(scores, prob_grads, deltas):
                score = score + bias
                peak = jnp.max(score, axis=0, keepdims=True)
                weights = jnp.exp2((score - peak) * (logit_scale * math.log2(math.e)))
                prob = weights * (1.0 / jnp.sum(weights, axis=0, keepdims=True))
                probs.append(prob[64:96])
                prob_halves.append(prob.astype(jnp.bfloat16))
                middle_halves.append((prob[0:64] * (prob_grad - delta)).astype(jnp.bfloat16))
            value_parts = [nn(prob, og_buf[g, slot, :, cols]) for prob, (g, _, cols) in zip(prob_halves, heads)]
            key_parts = [nn(score, q_buf[g, slot, :, cols]) * logit_scale for score, (g, _, cols) in zip(middle_halves, heads)]
            if last:
                key_parts = [part + key_sum[g, i] for part, (g, i, _) in zip(key_parts, heads)]
                middle_values = [part[0:64] + value_sum[g, i] for part, (g, i, _) in zip(value_parts, heads)]
                put(heads, middle, key_parts, middle_values)

                part_copies(None, groups, start, start)
            else:
                for key_part, value_part, (g, i, _) in zip(key_parts, value_parts, heads):
                    key_sum[g, i] = key_part
                    value_sum[g, i] = value_part[0:64]

            return heads, deltas, keys, probs, middle_halves, value_parts

        def edge_gradients(groups, heads, deltas, keys, probs, middle_halves, value_parts):
            halo_wait(v_buf.at[:, pl.ds(0, ABLOCK)], halo_recv.at[2])
            prob_grads = [nt(v_buf[g, alone, cols], og_buf[g, slot, :, cols]) for g, _, cols in heads]
            alone_halves = [
                (prob * (prob_grad - delta)).astype(jnp.bfloat16) for prob, prob_grad, delta in zip(probs, prob_grads, deltas)
            ]
            key_parts = [nn(score, q_buf[g, slot, :, cols]) * logit_scale for score, (g, _, cols) in zip(alone_halves, heads)]
            put(heads, alone, key_parts, [part[64:96] for part in value_parts])
            if last:

                @pl.when(is_first & has_before & (0 in groups))
                def _():
                    pl.semaphore_wait(part_ready, 4)

            part_copies(slot, groups if last else (0,), start, start)
            return list(zip(heads, keys, middle_halves, alone_halves))

        if last:
            first = gradients((0,))
            part_copies(1 - slot, (1,), start, start)
            second = gradients((1,))
            done = edge_gradients((0, 1), *[one + other for one, other in zip(first, second)])
        else:
            done = edge_gradients((0, 1), *gradients((0, 1)))
        for (g, _, cols), key, first, second in done:
            score_half = jnp.concatenate([first, second], axis=0)
            dq_buf[g, slot, :, cols] = (tn(score_half, key) * logit_scale).astype(jnp.bfloat16)

        @pl.when(slot == c)
        def _():
            for g in range(2):
                dq_copies(g, slot)[0].start()

        @pl.when(slot != c)
        def _():
            for g in range(2):
                dq_copies(g, slot)[1].start()

    def edge_part_copies(j):
        return [
            pltpu.make_async_remote_copy(
                edge_stage.at[j, core], landed.at[CHIPS - 1, :, pl.ds(96, ABLOCK)],
                edge_part_send, part_recv,
                device_id=(v + 1, 2 * j + core), device_id_type=MESH,
            )
            for core in range(2)
        ]

    def edge_work(j, wait):
        heads = [slice(i * HEAD_DIM, (i + 1) * HEAD_DIM) for i in range(3)]
        bias = bias_buf[1]
        deltas = [small_buf[1, pl.ds(8 + 3 * j + i, 1), :] for i in range(3)]
        wait(j, 0)
        keys = [jnp.concatenate([k_own[j, :, cols], edge_kv[j, 0, :, cols]], axis=0) for cols in heads]
        scores = [nt(key, q_own[j, :, cols]) + bias for key, cols in zip(keys, heads)]
        probs = []
        for score in scores:
            weights = jnp.exp2((score - jnp.max(score, axis=0, keepdims=True)) * (logit_scale * math.log2(math.e)))
            probs.append(weights[64:96] * (1.0 / jnp.sum(weights, axis=0, keepdims=True)))
        value_parts = [nn(prob.astype(jnp.bfloat16), og_own[j, :, cols]) for prob, cols in zip(probs, heads)]
        wait(j, 1)
        prob_grads = [nt(edge_kv[j, 1, :, cols], og_own[j, :, cols]) for cols in heads]
        halves = [(p * (grad - delta)).astype(jnp.bfloat16) for p, grad, delta in zip(probs, prob_grads, deltas)]
        key_parts = [nn(score, q_own[j, :, cols]) * logit_scale for score, cols in zip(halves, heads)]
        half = lax.broadcasted_iota(jnp.int32, (ABLOCK, HEAD_DIM), 1) < HEAD_DIM // 2
        for core in range(2):
            edge_stage[j, core, 0] = key_parts[2 * core].astype(jnp.bfloat16)
            edge_stage[j, core, 1] = value_parts[2 * core].astype(jnp.bfloat16)
        edge_stage[j, 0, 2] = jnp.where(half, key_parts[1], pltpu.roll(value_parts[1], 64, 1)).astype(jnp.bfloat16)
        edge_stage[j, 1, 2] = jnp.where(half, pltpu.roll(key_parts[1], 64, 1), value_parts[1]).astype(jnp.bfloat16)
        for copy in edge_part_copies(j):
            copy.start()

    work(False)

    @pl.when(works_up)
    def _():
        landed_wait(own_rows, own_sem.at[0])
        landed_wait(k_own, own_sem.at[1])

        @pl.when(edge_first)
        def _():
            lax.fori_loop(0, CHIPS, lambda j, carry: (edge_work(j, arrived), carry)[1], 0)

        @pl.when(jnp.logical_not(edge_first | edge_early))
        def _():
            for j in range(CHIPS):
                arrived(j, 0)
                arrived(j, 1)

        @pl.when(jnp.logical_not(edge_early))
        def _():
            for copy in hand_on:
                copy.start()

        for g in range(2):
            for i in range(2):
                audio_buf[i, g, pl.ds(96, ABLOCK)] = edge_kv[3 * g, i]

    work(True)

    @pl.when(works_up & jnp.logical_not(edge_first))
    def _():
        lax.fori_loop(0, CHIPS, lambda j, carry: (edge_work(j, lambda j, i: None), carry)[1], 0)

    @pl.when(sends_down)
    def _():
        sent_wait(edge_buf, edge_send)

    @pl.when(works_up)
    def _():
        sent_wait(gauge.at[pl.ds(0, 4)], halo_send)
        sent_wait(edge_stage, edge_part_send)

    for chip, copies in halo_up:

        @pl.when((y == chip) & (c == 0) & has_after)
        def _():
            sent_wait(gauge.at[pl.ds(0, len(copies))], halo_send)

    small.wait_send()
    sent_wait(rows_buf.at[:, :, c], swap_send)
    landed_wait(dq_buf.at[:, c], out_sem)
    sent_wait(dq_buf.at[:, other], dq_send)
    landed_wait(dq_buf.at[:, other], dq_recv)

    copies = 4 - (1 - role(y, c))
    to_before = jnp.where(has_before, 4, 0)
    units = 3 * copies + jnp.where(is_first, to_before, jnp.where(is_last, 0, copies))
    for count in (9, 12, 13, 16):

        @pl.when(units == count)
        def _():
            sent_wait(gauge.at[pl.ds(0, count)], part_send)

    @pl.when(has_before & has_after)
    def _():
        landed_wait(gauge, part_recv)

    @pl.when(jnp.logical_not(has_before & has_after))
    def _():
        landed_wait(gauge.at[pl.ds(0, 15)], part_recv)


def finish(dq_in, landed, dq_hbm, dk_hbm, dv_hbm, dk_buf, dv_buf, sem):
    c = lax.axis_index("audio") % 2
    dq_copy = pltpu.make_async_copy(dq_in, dq_hbm, sem.at[0])
    dq_copy.start()
    head_rows = pl.ds(pl.multiple_of(64 * c, 64), 128)
    middle_rows = pl.ds(pl.multiple_of(128 - 128 * c, 64), 64)
    for pair in range(2):
        rows = slice(pair * 128, (pair + 1) * 128)
        tiles = []
        for t in range(3):
            blocks = []
            for chip in (2 * pair, 2 * pair + 1):
                for own, far_chip, far in ((32, (chip + 3) % CHIPS, 96), (64, (chip + 1) % CHIPS, 0)):
                    own_term = landed[chip, t, own : own + ABLOCK].astype(jnp.float32)
                    blocks.append(own_term + landed[far_chip, t, far : far + ABLOCK].astype(jnp.float32))
            tiles.append(jnp.concatenate(blocks, axis=0).T.astype(jnp.bfloat16))
        dk_buf[head_rows, rows] = tiles[0]
        dv_buf[head_rows, rows] = tiles[1]
        dk_buf[middle_rows, rows] = tiles[2][0:64]
        dv_buf[middle_rows, rows] = tiles[2][64:128]
    copies = [pltpu.make_async_copy(dk_buf, dk_hbm, sem.at[1]), pltpu.make_async_copy(dv_buf, dv_hbm, sem.at[2])]
    for copy in copies:
        copy.start()
    for copy in [dq_copy] + copies:
        copy.wait()


def on_device(queries, keys, values, out_grad, delta, window_low, window_high):
    bf16, f32 = jnp.bfloat16, jnp.float32
    hbm, vmem = pl.BlockSpec(memory_space=pltpu.HBM), pl.BlockSpec(memory_space=pltpu.VMEM)
    dma = pltpu.SemaphoreType.DMA
    arrays = (queries, keys, values, out_grad, delta, window_low, window_high)
    arrays = [pltpu.with_memory_space_constraint(array, pltpu.HBM) for array in arrays]
    query_grad, landed = pl.pallas_call(
        kernel,
        out_shape=(pltpu.VMEM((ROWS, 1536), bf16), pltpu.VMEM((CHIPS, 3, AROWS, HEAD_DIM), bf16)),
        in_specs=[hbm] * 7,
        out_specs=(vmem, vmem),
        scratch_shapes=[
            pltpu.VMEM((2, 2, 2, ROWS, GROUP), bf16),
            pltpu.VMEM((2, 2, AROWS, GROUP), bf16),
            pltpu.VMEM((2, 2, ABLOCK, GROUP), bf16),
            pltpu.VMEM((2, CHIPS, ROWS, GROUP), bf16),
            pltpu.VMEM((CHIPS, 2 * ABLOCK, GROUP), bf16),
            pltpu.VMEM((CHIPS, 2, ABLOCK, GROUP), bf16),
            pltpu.VMEM((CHIPS, 2, 3, ABLOCK, HEAD_DIM), bf16),
            pltpu.VMEM((12, ROWS), f32),
            pltpu.VMEM((2, 24, ROWS), f32),
            pltpu.VMEM((2, REACH, ROWS), f32),
            pltpu.VMEM((2, 2, ROWS, GROUP), bf16),
            pltpu.VMEM((2, 3, 2 * ABLOCK, HEAD_DIM), f32),
            pltpu.VMEM((2, 3, 2 * ABLOCK, HEAD_DIM), f32),
            pltpu.VMEM((2, 2, 3, AROWS, HEAD_DIM), bf16),
            pltpu.VMEM((16, ABLOCK, GROUP), bf16),
            pltpu.SMEM((2,), jnp.int32),
            pltpu.SMEM((2,), jnp.int32),
            dma((2,)),
            dma(()),
            dma(()),
            dma(()),
            dma(()),
            dma((2,)),
            dma(()),
            dma(()),
            dma(()),
            dma(()),
            dma(()),
            dma(()),
            dma((3,)),
            dma(()),
            dma((CHIPS, 2)),
            dma(()),
            dma(()),
            dma(()),
            dma(()),
            dma(()),
            pltpu.SemaphoreType.REGULAR,
        ],
        compiler_params=pltpu.CompilerParams(
            collective_id=0, has_side_effects=True, vmem_limit_bytes=32 << 20
        ),
        name="attention_backward",
    )(*arrays)
    query_grad, key_grad, value_grad = pl.pallas_call(
        finish,
        out_shape=(
            jax.ShapeDtypeStruct((ROWS, 1536), bf16),
            jax.ShapeDtypeStruct((192, 256), bf16),
            jax.ShapeDtypeStruct((192, 256), bf16),
        ),
        in_specs=[vmem, vmem],
        out_specs=(hbm, hbm, hbm),
        scratch_shapes=[pltpu.VMEM((192, 256), bf16), pltpu.VMEM((192, 256), bf16), dma((3,))],
        compiler_params=pltpu.CompilerParams(vmem_limit_bytes=32 << 20),
        name="sum_partials",
    )(query_grad, landed)
    return query_grad, key_grad.T, value_grad.T


def solution(mesh):
    return jax.shard_map(
        on_device,
        mesh=mesh,
        in_specs=(
            P(("video", "audio"), None),
            P("video", None),
            P("video", None),
            P(("video", "audio"), None),
            P(None, ("video", "audio")),
            P(("video", "audio")),
            P(("video", "audio")),
        ),
        out_specs=(P(("video", "audio"), None), P("video", "audio"), P("video", "audio")),
        check_vma=False,
    )
```

```python
import math

import jax
import jax.numpy as jnp
from jax import lax
from jax.experimental import pallas as pl
from jax.experimental.pallas import tpu as pltpu
from jax.sharding import PartitionSpec as P

HEAD_DIM = 128
VBLOCK = 64
ABLOCK = 32
SPANS = 64
CHIPS = 4
ROWS = 128
AROWS = 128
REACH = 96
GROUP = 384

MESH = pl.DeviceIdType.MESH
masked_score = -1e30
logit_scale = 1.0 / math.sqrt(HEAD_DIM)


def nt(a, b):
    return lax.dot_general(a, b, (((1,), (1,)), ((), ())), preferred_element_type=jnp.float32)


def nn(a, b):
    return lax.dot_general(a, b, (((1,), (0,)), ((), ())), preferred_element_type=jnp.float32)


def tn(a, b):
    return lax.dot_general(a, b, (((0,), (0,)), ((), ())), preferred_element_type=jnp.float32)


def kernel(
    q_hbm, k_hbm, v_hbm, og_hbm, delta_hbm, low_hbm, high_hbm,
    dq_out, landed,
    rows_buf, audio_buf, edge_buf, own_rows, k_own, edge_kv, edge_stage, delta_own, small_buf, bias_buf, dq_buf,
    key_sum, value_sum, stage, gauge,
    low_smem, high_smem,
    win_sem, delta_sem, rows_sem, audio_sem, edge_sem, own_sem, out_sem,
    swap_send, swap_recv, small_send, small_recv, halo_send, halo_recv, edge_send, edge_recv, edge_part_send,
    part_send, part_recv, dq_send, dq_recv, part_ready,
):
    v = lax.axis_index("video")
    a = lax.axis_index("audio")
    y, c = a // 2, a % 2
    other = 1 - c
    partner = (v, 2 * y + other)
    q_buf, og_buf = rows_buf.at[0], rows_buf.at[1]
    k_buf, v_buf = audio_buf.at[0], audio_buf.at[1]
    q_own, og_own = own_rows.at[0], own_rows.at[1]
    has_before, has_after = v > 0, v < SPANS - 1
    is_first, is_last = y == 0, y == CHIPS - 1

    def role(chip, core):
        return jnp.where(chip == CHIPS - 1, 1 - core, core)

    def group_of(chip, core, g):
        return (chip + jnp.where(role(chip, core) == 0, 1 - g, 2 + g)) % CHIPS

    def signal(semaphore, device):
        pl.semaphore_signal(semaphore, inc=1, device_id=device, device_id_type=MESH)

    barrier = pltpu.get_barrier_semaphore()

    @pl.when(is_last & has_after & (c == 1))
    def _():
        signal(barrier, (v + 1, 7))
        signal(barrier, (v + 1, 6))

    signal(barrier, partner)

    @pl.when(has_before)
    def _():
        signal(barrier, (v - 1, 7))

        @pl.when(is_first)
        def _():
            for i in range(4):
                signal(barrier, (v - 1, 4 * c + i))

        @pl.when(is_first & (c == 1))
        def _():
            signal(barrier, (v - 1, 0))

    for ahead, part in ((3, 0), (2, 1), (1, 1)):
        chip = (y + ahead) % CHIPS
        signal(barrier, (v, 2 * chip + role(chip, part)))

    low_copy = pltpu.make_async_copy(low_hbm, low_smem, win_sem.at[0])
    high_copy = pltpu.make_async_copy(high_hbm, high_smem, win_sem.at[1])
    delta_copy = pltpu.make_async_copy(delta_hbm, delta_own, delta_sem)
    low_copy.start()
    high_copy.start()
    delta_copy.start()

    def lanes(k):
        return pl.ds(pl.multiple_of(k * GROUP, GROUP), GROUP)

    def landed_wait(ref, sem):
        pltpu.make_async_copy(ref, ref, sem).wait()

    def sent_wait(ref, sem):
        pltpu.make_async_remote_copy(
            ref, ref, sem, dq_recv, device_id=partner, device_id_type=MESH
        ).wait_send()

    def row_copies(g):
        k = group_of(y, c, g)
        return [
            pltpu.make_async_copy(q_hbm.at[:, lanes(k)], q_buf.at[g, c], rows_sem),
            pltpu.make_async_copy(og_hbm.at[:, lanes(k)], og_buf.at[g, c], rows_sem),
        ]

    reaches = ((is_first, 0, 32, 96), (is_last, 160, 0, 96), ((y > 0) & (y < CHIPS - 1), 64 * y - 32, 0, AROWS))

    def audio_start(g):
        k = group_of(y, c, g)
        for chosen, first, target, count in reaches:

            @pl.when(chosen)
            def _():
                for source, buf in ((k_hbm, k_buf), (v_hbm, v_buf)):
                    rows = pl.ds(first if isinstance(first, int) else pl.multiple_of(first, 32), count)
                    pltpu.make_async_copy(source.at[rows, lanes(k)], buf.at[g, pl.ds(target, count)], audio_sem).start()

    def audio_wait():
        for chosen, _, target, count in reaches:

            @pl.when(chosen)
            def _():
                landed_wait(audio_buf.at[:, :, pl.ds(target, count)], audio_sem)

    sends_down = is_last & has_before
    works_up = is_last & has_after & (c == 1)
    edge_first, edge_early = v % 16 == 15, v % 16 == 0

    @pl.when(sends_down)
    def _():
        for n in range(2):
            for i, source in enumerate((k_hbm, v_hbm)):
                pltpu.make_async_copy(
                    source.at[pl.ds(0, ABLOCK), lanes(2 - 2 * c + n)], edge_buf.at[n, i], edge_sem
                ).start()

    own_copies = []
    for j in range(CHIPS):
        k = j
        own_copies += [
            pltpu.make_async_copy(q_hbm.at[:, lanes(k)], q_own.at[j], own_sem.at[0]),
            pltpu.make_async_copy(og_hbm.at[:, lanes(k)], og_own.at[j], own_sem.at[0]),
            pltpu.make_async_copy(k_hbm.at[pl.ds(192, 2 * ABLOCK), lanes(k)], k_own.at[j], own_sem.at[1]),
        ]

    for g in range(2):
        for copy in row_copies(g):
            copy.start()
        audio_start(g)

    @pl.when(works_up)
    def _():
        for copy in own_copies:
            copy.start()

    @pl.when(sends_down)
    def _():
        landed_wait(edge_buf, edge_sem)

    @pl.when(jnp.logical_not(has_before))
    def _():
        landed[3, :, 96:128] = jnp.zeros((3, ABLOCK, HEAD_DIM), jnp.bfloat16)

        @pl.when(is_first)
        def _():
            audio_buf[:, :, 0:32] = jnp.zeros((2, 2, ABLOCK, GROUP), jnp.bfloat16)

    @pl.when(jnp.logical_not(has_after))
    def _():
        landed[0, :, 0:32] = jnp.zeros((3, ABLOCK, HEAD_DIM), jnp.bfloat16)

        @pl.when(is_last)
        def _():
            audio_buf[:, :, 96:128] = jnp.zeros((2, 2, ABLOCK, GROUP), jnp.bfloat16)

    from_after = 1 + jnp.where(is_last, 8 * c, 0) + jnp.where(is_first, other, 0)
    from_before = jnp.where(is_last, 1, 0)
    pl.semaphore_wait(barrier, 3 + 2 * role(y, c) + jnp.where(has_after, from_after, 0) + jnp.where(has_before, from_before, 0))

    def up_copies(i, core):
        return [
            pltpu.make_async_remote_copy(
                (k_hbm, v_hbm)[i].at[pl.ds(224, ABLOCK), lanes(group_of(0, core, g))],
                (k_buf, v_buf)[i].at[g, pl.ds(0, ABLOCK)],
                halo_send, halo_recv.at[g if i == 0 else 2], device_id=(v + 1, core), device_id_type=MESH,
            )
            for g in range(2)
        ]

    halo_up = (
        (0, [copy for pair in zip(up_copies(0, 0), up_copies(0, 1)) for copy in pair]),
        (1, up_copies(1, 0)),
        (CHIPS - 1, up_copies(1, 1)),
    )
    @pl.when(sends_down)
    def _():
        for n in range(2):
            j = 2 - 2 * c + n
            for i in range(2):
                pltpu.make_async_remote_copy(
                    edge_buf.at[n, i], edge_kv.at[j, i], edge_send, edge_recv.at[j, i],
                    device_id=(v - 1, 7), device_id_type=MESH,
                ).start()

    @pl.when(has_after)
    def _():
        for chip, copies in halo_up:

            @pl.when((y == chip) & (c == 0))
            def _():
                for copy in copies:
                    copy.start()

        signal(part_ready, (v + 1, y // 2))

    def swap_copies(g, slot):
        k = group_of(y, other, g)
        return [
            pltpu.make_async_remote_copy(
                source.at[:, lanes(k)], target.at[g, slot], swap_send, swap_recv,
                device_id=partner, device_id_type=MESH,
            )
            for source, target in ((q_hbm, q_buf), (og_hbm, og_buf))
        ]

    for g in range(2):
        for copy in swap_copies(g, c):
            copy.start()

    def arrived(j, i):
        landed_wait(edge_kv.at[j, i], edge_recv.at[j, i])

    hand_on = [
        pltpu.make_async_remote_copy(
            edge_kv.at[1 + g, i], buf.at[g, pl.ds(96, ABLOCK)], halo_send, halo_recv.at[g if i == 0 else 2],
            device_id=partner, device_id_type=MESH,
        )
        for g in range(2)
        for i, buf in enumerate((k_buf, v_buf))
    ]

    @pl.when(works_up & edge_early)
    def _():
        for j in range(CHIPS):
            arrived(j, 0)
            arrived(j, 1)
        for copy in hand_on:
            copy.start()

    low_copy.wait()
    high_copy.wait()
    lane = lax.broadcasted_iota(jnp.int32, (8, ROWS), 1)
    row = lax.broadcasted_iota(jnp.int32, (8, ROWS), 0)
    lows = jnp.where(lane < VBLOCK, low_smem[0], low_smem[1])
    highs = jnp.where(lane < VBLOCK, high_smem[0], high_smem[1])
    delta_copy.wait()
    small_buf[c, 0:8] = jnp.where(row == 0, lows, highs).astype(jnp.float32)
    small_buf[c, 8:20] = delta_own[...]
    small_buf[c, 20:24] = jnp.zeros((4, ROWS), jnp.float32)
    small = pltpu.make_async_remote_copy(
        small_buf.at[c], small_buf.at[c], small_send, small_recv, device_id=partner, device_id_type=MESH
    )
    small.start()
    small.wait_recv()

    row = lax.broadcasted_iota(jnp.int32, (REACH, ROWS), 0)
    for slot in range(2):
        blocks = 8 * v + 2 * y + jnp.where(row < 2 * ABLOCK, row // ABLOCK, 3 * slot - 1)
        blocks = blocks.astype(jnp.float32)
        inside = (blocks >= small_buf[slot, 0:1, :]) & (blocks < small_buf[slot, 1:2, :])
        bias_buf[slot] = jnp.where(inside, 0.0, masked_score)

    def part_copies(slot, groups, do, do_local):
        if slot is None:
            start, size, span, exists = ABLOCK, 2 * ABLOCK, v, True
        else:
            start, size = pl.multiple_of(REACH * slot, ABLOCK), ABLOCK
            down, up = is_first & (slot == 0), is_last & (slot == 1)
            span = v - jnp.where(down, 1, 0)
            exists = jnp.logical_not(down & jnp.logical_not(has_before)) & jnp.logical_not(up)
        for g in groups:
            k = group_of(y, c, g)
            for core in range(2):
                source = stage.at[g, core, :, pl.ds(start, size)]
                target = landed.at[y, :, pl.ds(start, size)]
                here = (span == v) & (2 * k + core == a) & exists
                away = jnp.logical_not(here) if g == 1 else True

                @pl.when(away & exists)
                def _():
                    do(
                        pltpu.make_async_remote_copy(
                            source, target, part_send, part_recv,
                            device_id=(span, 2 * k + core), device_id_type=MESH,
                        )
                    )

                if g == 1:

                    @pl.when(here)
                    def _():
                        do_local(pltpu.make_async_copy(source, target, part_recv))

    def dq_copies(g, slot):
        k = group_of(y, c, g)
        return (
            pltpu.make_async_copy(dq_buf.at[g, slot], dq_out.at[:, lanes(k)], out_sem),
            pltpu.make_async_remote_copy(
                dq_buf.at[g, slot], dq_out.at[:, lanes(k)], dq_send, dq_recv,
                device_id=partner, device_id_type=MESH,
            ),
        )

    def work(last):
        slot = jnp.where(is_first, 1, 0)
        if last:
            slot = 1 - slot

        @pl.when(slot == c)
        def _():
            landed_wait(rows_buf.at[:, :, slot], rows_sem)

        @pl.when(slot != c)
        def _():
            landed_wait(rows_buf.at[:, :, slot], swap_recv)

        def halo_wait(ref, sem):
            if last:

                @pl.when((is_first & has_before) | (is_last & has_after & (c == 0)))
                def _():
                    landed_wait(ref, sem)

        def start(copy):
            copy.start()

        def put(heads, rows, key_parts, value_parts):
            for (g, i, _), key_part, value_part in zip(heads, key_parts, value_parts):
                if i == 1:
                    half = lax.broadcasted_iota(jnp.int32, key_part.shape, 1) < HEAD_DIM // 2
                    stage[g, 0, 2, rows] = jnp.where(half, key_part, pltpu.roll(value_part, 64, 1)).astype(jnp.bfloat16)
                    stage[g, 1, 2, rows] = jnp.where(half, pltpu.roll(key_part, 64, 1), value_part).astype(jnp.bfloat16)
                else:
                    stage[g, i // 2, 0, rows] = key_part.astype(jnp.bfloat16)
                    stage[g, i // 2, 1, rows] = value_part.astype(jnp.bfloat16)

        if not last:
            audio_wait()
        middle = pl.ds(ABLOCK, 2 * ABLOCK)
        alone = pl.ds(pl.multiple_of(REACH * slot, ABLOCK), ABLOCK)
        bias = bias_buf[slot]

        def gradients(groups):
            heads = [(g, i, slice(i * HEAD_DIM, (i + 1) * HEAD_DIM)) for g in groups for i in range(3)]
            deltas = [small_buf[slot, pl.ds(8 + 3 * group_of(y, c, g) + i, 1), :] for g, i, _ in heads]

            for g in groups:
                halo_wait(k_buf.at[g, pl.ds(0, ABLOCK)], halo_recv.at[g])
            keys = [jnp.concatenate([k_buf[g, middle, cols], k_buf[g, alone, cols]], axis=0) for g, _, cols in heads]
            scores = [nt(key, q_buf[g, slot, :, cols]) for key, (g, _, cols) in zip(keys, heads)]
            prob_grads = [nt(v_buf[g, middle, cols], og_buf[g, slot, :, cols]) for g, _, cols in heads]
            probs, prob_halves, middle_halves = [], [], []
            for score, prob_grad, delta in zip(scores, prob_grads, deltas):
                score = score + bias
                peak = jnp.max(score, axis=0, keepdims=True)
                weights = jnp.exp2((score - peak) * (logit_scale * math.log2(math.e)))
                prob = weights * (1.0 / jnp.sum(weights, axis=0, keepdims=True))
                probs.append(prob[64:96])
                prob_halves.append(prob.astype(jnp.bfloat16))
                middle_halves.append((prob[0:64] * (prob_grad - delta)).astype(jnp.bfloat16))
            value_parts = [nn(prob, og_buf[g, slot, :, cols]) for prob, (g, _, cols) in zip(prob_halves, heads)]
            key_parts = [nn(score, q_buf[g, slot, :, cols]) * logit_scale for score, (g, _, cols) in zip(middle_halves, heads)]
            if last:
                key_parts = [part + key_sum[g, i] for part, (g, i, _) in zip(key_parts, heads)]
                middle_values = [part[0:64] + value_sum[g, i] for part, (g, i, _) in zip(value_parts, heads)]
                put(heads, middle, key_parts, middle_values)

                part_copies(None, groups, start, start)
            else:
                for key_part, value_part, (g, i, _) in zip(key_parts, value_parts, heads):
                    key_sum[g, i] = key_part
                    value_sum[g, i] = value_part[0:64]

            return heads, deltas, keys, probs, middle_halves, value_parts

        def edge_gradients(groups, heads, deltas, keys, probs, middle_halves, value_parts):
            halo_wait(v_buf.at[:, pl.ds(0, ABLOCK)], halo_recv.at[2])
            prob_grads = [nt(v_buf[g, alone, cols], og_buf[g, slot, :, cols]) for g, _, cols in heads]
            alone_halves = [
                (prob * (prob_grad - delta)).astype(jnp.bfloat16) for prob, prob_grad, delta in zip(probs, prob_grads, deltas)
            ]
            key_parts = [nn(score, q_buf[g, slot, :, cols]) * logit_scale for score, (g, _, cols) in zip(alone_halves, heads)]
            put(heads, alone, key_parts, [part[64:96] for part in value_parts])
            if last:

                @pl.when(is_first & has_before & (0 in groups))
                def _():
                    pl.semaphore_wait(part_ready, 4)

            part_copies(slot, groups if last else (0,), start, start)
            return list(zip(heads, keys, middle_halves, alone_halves))

        if last:
            first = gradients((0,))
            part_copies(1 - slot, (1,), start, start)
            second = gradients((1,))
            done = edge_gradients((0, 1), *[one + other for one, other in zip(first, second)])
        else:
            done = edge_gradients((0, 1), *gradients((0, 1)))
        for (g, _, cols), key, first, second in done:
            score_half = jnp.concatenate([first, second], axis=0)
            dq_buf[g, slot, :, cols] = (tn(score_half, key) * logit_scale).astype(jnp.bfloat16)

        @pl.when(slot == c)
        def _():
            for g in range(2):
                dq_copies(g, slot)[0].start()

        @pl.when(slot != c)
        def _():
            for g in range(2):
                dq_copies(g, slot)[1].start()

    def edge_part_copies(j):
        return [
            pltpu.make_async_remote_copy(
                edge_stage.at[j, core], landed.at[CHIPS - 1, :, pl.ds(96, ABLOCK)],
                edge_part_send, part_recv,
                device_id=(v + 1, 2 * j + core), device_id_type=MESH,
            )
            for core in range(2)
        ]

    def edge_work(j, wait):
        heads = [slice(i * HEAD_DIM, (i + 1) * HEAD_DIM) for i in range(3)]
        bias = bias_buf[1]
        deltas = [small_buf[1, pl.ds(8 + 3 * j + i, 1), :] for i in range(3)]
        wait(j, 0)
        keys = [jnp.concatenate([k_own[j, :, cols], edge_kv[j, 0, :, cols]], axis=0) for cols in heads]
        scores = [nt(key, q_own[j, :, cols]) + bias for key, cols in zip(keys, heads)]
        probs = []
        for score in scores:
            weights = jnp.exp2((score - jnp.max(score, axis=0, keepdims=True)) * (logit_scale * math.log2(math.e)))
            probs.append(weights[64:96] * (1.0 / jnp.sum(weights, axis=0, keepdims=True)))
        value_parts = [nn(prob.astype(jnp.bfloat16), og_own[j, :, cols]) for prob, cols in zip(probs, heads)]
        wait(j, 1)
        prob_grads = [nt(edge_kv[j, 1, :, cols], og_own[j, :, cols]) for cols in heads]
        halves = [(p * (grad - delta)).astype(jnp.bfloat16) for p, grad, delta in zip(probs, prob_grads, deltas)]
        key_parts = [nn(score, q_own[j, :, cols]) * logit_scale for score, cols in zip(halves, heads)]
        half = lax.broadcasted_iota(jnp.int32, (ABLOCK, HEAD_DIM), 1) < HEAD_DIM // 2
        for core in range(2):
            edge_stage[j, core, 0] = key_parts[2 * core].astype(jnp.bfloat16)
            edge_stage[j, core, 1] = value_parts[2 * core].astype(jnp.bfloat16)
        edge_stage[j, 0, 2] = jnp.where(half, key_parts[1], pltpu.roll(value_parts[1], 64, 1)).astype(jnp.bfloat16)
        edge_stage[j, 1, 2] = jnp.where(half, pltpu.roll(key_parts[1], 64, 1), value_parts[1]).astype(jnp.bfloat16)
        for copy in edge_part_copies(j):
            copy.start()

    @pl.when(works_up)
    def _():
        landed_wait(own_rows, own_sem.at[0])
        landed_wait(k_own, own_sem.at[1])

        @pl.when(edge_first)
        def _():
            lax.fori_loop(0, CHIPS, lambda j, carry: (edge_work(j, arrived), carry)[1], 0)

    work(False)

    @pl.when(works_up)
    def _():
        @pl.when(jnp.logical_not(edge_first | edge_early))
        def _():
            for j in range(CHIPS):
                arrived(j, 0)
                arrived(j, 1)

        @pl.when(jnp.logical_not(edge_early))
        def _():
            for copy in hand_on:
                copy.start()

        for g in range(2):
            for i in range(2):
                audio_buf[i, g, pl.ds(96, ABLOCK)] = edge_kv[3 * g, i]

    work(True)

    @pl.when(works_up & jnp.logical_not(edge_first))
    def _():
        lax.fori_loop(0, CHIPS, lambda j, carry: (edge_work(j, lambda j, i: None), carry)[1], 0)

    @pl.when(sends_down)
    def _():
        sent_wait(edge_buf, edge_send)

    @pl.when(works_up)
    def _():
        sent_wait(gauge.at[pl.ds(0, 4)], halo_send)
        sent_wait(edge_stage, edge_part_send)

    for chip, copies in halo_up:

        @pl.when((y == chip) & (c == 0) & has_after)
        def _():
            sent_wait(gauge.at[pl.ds(0, len(copies))], halo_send)

    small.wait_send()
    sent_wait(rows_buf.at[:, :, c], swap_send)
    landed_wait(dq_buf.at[:, c], out_sem)
    sent_wait(dq_buf.at[:, other], dq_send)
    landed_wait(dq_buf.at[:, other], dq_recv)

    copies = 4 - (1 - role(y, c))
    to_before = jnp.where(has_before, 4, 0)
    units = 3 * copies + jnp.where(is_first, to_before, jnp.where(is_last, 0, copies))
    for count in (9, 12, 13, 16):

        @pl.when(units == count)
        def _():
            sent_wait(gauge.at[pl.ds(0, count)], part_send)

    @pl.when(has_before & has_after)
    def _():
        landed_wait(gauge, part_recv)

    @pl.when(jnp.logical_not(has_before & has_after))
    def _():
        landed_wait(gauge.at[pl.ds(0, 15)], part_recv)


def finish(dq_in, landed, dq_hbm, dk_hbm, dv_hbm, dk_buf, dv_buf, sem):
    c = lax.axis_index("audio") % 2
    dq_copy = pltpu.make_async_copy(dq_in, dq_hbm, sem.at[0])
    dq_copy.start()
    head_rows = pl.ds(pl.multiple_of(64 * c, 64), 128)
    middle_rows = pl.ds(pl.multiple_of(128 - 128 * c, 64), 64)
    for pair in range(2):
        rows = slice(pair * 128, (pair + 1) * 128)
        tiles = []
        for t in range(3):
            blocks = []
            for chip in (2 * pair, 2 * pair + 1):
                for own, far_chip, far in ((32, (chip + 3) % CHIPS, 96), (64, (chip + 1) % CHIPS, 0)):
                    own_term = landed[chip, t, own : own + ABLOCK].astype(jnp.float32)
                    blocks.append(own_term + landed[far_chip, t, far : far + ABLOCK].astype(jnp.float32))
            tiles.append(jnp.concatenate(blocks, axis=0).T.astype(jnp.bfloat16))
        dk_buf[head_rows, rows] = tiles[0]
        dv_buf[head_rows, rows] = tiles[1]
        dk_buf[middle_rows, rows] = tiles[2][0:64]
        dv_buf[middle_rows, rows] = tiles[2][64:128]
    copies = [pltpu.make_async_copy(dk_buf, dk_hbm, sem.at[1]), pltpu.make_async_copy(dv_buf, dv_hbm, sem.at[2])]
    for copy in copies:
        copy.start()
    for copy in [dq_copy] + copies:
        copy.wait()


def on_device(queries, keys, values, out_grad, delta, window_low, window_high):
    bf16, f32 = jnp.bfloat16, jnp.float32
    hbm, vmem = pl.BlockSpec(memory_space=pltpu.HBM), pl.BlockSpec(memory_space=pltpu.VMEM)
    dma = pltpu.SemaphoreType.DMA
    arrays = (queries, keys, values, out_grad, delta, window_low, window_high)
    arrays = [pltpu.with_memory_space_constraint(array, pltpu.HBM) for array in arrays]
    query_grad, landed = pl.pallas_call(
        kernel,
        out_shape=(pltpu.VMEM((ROWS, 1536), bf16), pltpu.VMEM((CHIPS, 3, AROWS, HEAD_DIM), bf16)),
        in_specs=[hbm] * 7,
        out_specs=(vmem, vmem),
        scratch_shapes=[
            pltpu.VMEM((2, 2, 2, ROWS, GROUP), bf16),
            pltpu.VMEM((2, 2, AROWS, GROUP), bf16),
            pltpu.VMEM((2, 2, ABLOCK, GROUP), bf16),
            pltpu.VMEM((2, CHIPS, ROWS, GROUP), bf16),
            pltpu.VMEM((CHIPS, 2 * ABLOCK, GROUP), bf16),
            pltpu.VMEM((CHIPS, 2, ABLOCK, GROUP), bf16),
            pltpu.VMEM((CHIPS, 2, 3, ABLOCK, HEAD_DIM), bf16),
            pltpu.VMEM((12, ROWS), f32),
            pltpu.VMEM((2, 24, ROWS), f32),
            pltpu.VMEM((2, REACH, ROWS), f32),
            pltpu.VMEM((2, 2, ROWS, GROUP), bf16),
            pltpu.VMEM((2, 3, 2 * ABLOCK, HEAD_DIM), f32),
            pltpu.VMEM((2, 3, 2 * ABLOCK, HEAD_DIM), f32),
            pltpu.VMEM((2, 2, 3, AROWS, HEAD_DIM), bf16),
            pltpu.VMEM((16, ABLOCK, GROUP), bf16),
            pltpu.SMEM((2,), jnp.int32),
            pltpu.SMEM((2,), jnp.int32),
            dma((2,)),
            dma(()),
            dma(()),
            dma(()),
            dma(()),
            dma((2,)),
            dma(()),
            dma(()),
            dma(()),
            dma(()),
            dma(()),
            dma(()),
            dma((3,)),
            dma(()),
            dma((CHIPS, 2)),
            dma(()),
            dma(()),
            dma(()),
            dma(()),
            dma(()),
            pltpu.SemaphoreType.REGULAR,
        ],
        compiler_params=pltpu.CompilerParams(
            collective_id=0, has_side_effects=True, vmem_limit_bytes=32 << 20
        ),
        name="attention_backward",
    )(*arrays)
    query_grad, key_grad, value_grad = pl.pallas_call(
        finish,
        out_shape=(
            jax.ShapeDtypeStruct((ROWS, 1536), bf16),
            jax.ShapeDtypeStruct((192, 256), bf16),
            jax.ShapeDtypeStruct((192, 256), bf16),
        ),
        in_specs=[vmem, vmem],
        out_specs=(hbm, hbm, hbm),
        scratch_shapes=[pltpu.VMEM((192, 256), bf16), pltpu.VMEM((192, 256), bf16), dma((3,))],
        compiler_params=pltpu.CompilerParams(vmem_limit_bytes=32 << 20),
        name="sum_partials",
    )(query_grad, landed)
    return query_grad, key_grad.T, value_grad.T


def solution(mesh):
    return jax.shard_map(
        on_device,
        mesh=mesh,
        in_specs=(
            P(("video", "audio"), None),
            P("video", None),
            P("video", None),
            P(("video", "audio"), None),
            P(None, ("video", "audio")),
            P(("video", "audio")),
            P(("video", "audio")),
        ),
        out_specs=(P(("video", "audio"), None), P("video", "audio"), P("video", "audio")),
        check_vma=False,
    )
```

```python
import math

import jax
import jax.numpy as jnp
from jax import lax
from jax.experimental import pallas as pl
from jax.experimental.pallas import tpu as pltpu
from jax.sharding import PartitionSpec as P

HEAD_DIM = 128
VBLOCK = 64
ABLOCK = 32
SPANS = 64
CHIPS = 4
ROWS = 128
AROWS = 128
REACH = 96
GROUP = 384

MESH = pl.DeviceIdType.MESH
masked_score = -1e30
logit_scale = 1.0 / math.sqrt(HEAD_DIM)


def nt(a, b):
    return lax.dot_general(a, b, (((1,), (1,)), ((), ())), preferred_element_type=jnp.float32)


def nn(a, b):
    return lax.dot_general(a, b, (((1,), (0,)), ((), ())), preferred_element_type=jnp.float32)


def tn(a, b):
    return lax.dot_general(a, b, (((0,), (0,)), ((), ())), preferred_element_type=jnp.float32)


def kernel(
    q_hbm, k_hbm, v_hbm, og_hbm, delta_hbm, low_hbm, high_hbm,
    dq_out, landed,
    rows_buf, audio_buf, edge_buf, own_rows, k_own, edge_kv, edge_stage, delta_own, small_buf, bias_buf, dq_buf,
    key_sum, value_sum, stage, gauge,
    low_smem, high_smem,
    win_sem, delta_sem, rows_sem, audio_sem, edge_sem, own_sem, out_sem,
    swap_recv, small_send, small_recv, edge_send, halo_recv, edge_recv,
    part_send, part_recv, dq_send, dq_recv, part_ready,
):
    v = lax.axis_index("video")
    a = lax.axis_index("audio")
    y, c = a // 2, a % 2
    other = 1 - c
    partner = (v, 2 * y + other)
    q_buf, og_buf = rows_buf.at[0], rows_buf.at[1]
    k_buf, v_buf = audio_buf.at[0], audio_buf.at[1]
    q_own, og_own = own_rows.at[0], own_rows.at[1]
    has_before, has_after = v > 0, v < SPANS - 1
    is_first, is_last = y == 0, y == CHIPS - 1

    def role(chip, core):
        return jnp.where(chip == CHIPS - 1, 1 - core, core)

    def group_of(chip, core, g):
        return (chip + jnp.where(role(chip, core) == 0, 1 - g, 2 + g)) % CHIPS

    def signal(semaphore, device):
        pl.semaphore_signal(semaphore, inc=1, device_id=device, device_id_type=MESH)

    barrier = pltpu.get_barrier_semaphore()

    @pl.when(is_last & has_after & (c == 1))
    def _():
        signal(barrier, (v + 1, 7))
        signal(barrier, (v + 1, 6))

    signal(barrier, partner)

    @pl.when(has_before)
    def _():
        signal(barrier, (v - 1, 7))

        @pl.when(is_first)
        def _():
            for i in range(4):
                signal(barrier, (v - 1, 4 * c + i))

        @pl.when(is_first & (c == 1))
        def _():
            signal(barrier, (v - 1, 0))

    for ahead, part in ((3, 0), (2, 1), (1, 1)):
        chip = (y + ahead) % CHIPS
        signal(barrier, (v, 2 * chip + role(chip, part)))

    low_copy = pltpu.make_async_copy(low_hbm, low_smem, win_sem.at[0])
    high_copy = pltpu.make_async_copy(high_hbm, high_smem, win_sem.at[1])
    delta_copy = pltpu.make_async_copy(delta_hbm, delta_own, delta_sem)
    low_copy.start()
    high_copy.start()
    delta_copy.start()

    def lanes(k):
        return pl.ds(pl.multiple_of(k * GROUP, GROUP), GROUP)

    def landed_wait(ref, sem):
        pltpu.make_async_copy(ref, ref, sem).wait()

    def sent_wait(ref, sem):
        pltpu.make_async_remote_copy(
            ref, ref, sem, dq_recv, device_id=partner, device_id_type=MESH
        ).wait_send()

    def row_copies(g):
        k = group_of(y, c, g)
        return [
            pltpu.make_async_copy(q_hbm.at[:, lanes(k)], q_buf.at[g, c], rows_sem),
            pltpu.make_async_copy(og_hbm.at[:, lanes(k)], og_buf.at[g, c], rows_sem),
        ]

    reaches = ((is_first, 0, 32, 96), (is_last, 160, 0, 96), ((y > 0) & (y < CHIPS - 1), 64 * y - 32, 0, AROWS))

    def audio_start(g):
        k = group_of(y, c, g)
        for chosen, first, target, count in reaches:

            @pl.when(chosen)
            def _():
                for source, buf in ((k_hbm, k_buf), (v_hbm, v_buf)):
                    rows = pl.ds(first if isinstance(first, int) else pl.multiple_of(first, 32), count)
                    pltpu.make_async_copy(source.at[rows, lanes(k)], buf.at[g, pl.ds(target, count)], audio_sem).start()

    def audio_wait():
        for chosen, _, target, count in reaches:

            @pl.when(chosen)
            def _():
                landed_wait(audio_buf.at[:, :, pl.ds(target, count)], audio_sem)

    sends_down = is_last & has_before
    works_up = is_last & has_after & (c == 1)
    edge_first, edge_early = v % 16 == 15, v % 16 == 0

    @pl.when(sends_down)
    def _():
        for n in range(2):
            for i, source in enumerate((k_hbm, v_hbm)):
                pltpu.make_async_copy(
                    source.at[pl.ds(0, ABLOCK), lanes(2 - 2 * c + n)], edge_buf.at[n, i], edge_sem
                ).start()

    own_copies = []
    for j in range(CHIPS):
        k = j
        own_copies += [
            pltpu.make_async_copy(q_hbm.at[:, lanes(k)], q_own.at[j], own_sem),
            pltpu.make_async_copy(og_hbm.at[:, lanes(k)], og_own.at[j], own_sem),
            pltpu.make_async_copy(k_hbm.at[pl.ds(192, 2 * ABLOCK), lanes(k)], k_own.at[j], own_sem),
        ]

    for g in range(2):
        for copy in row_copies(g):
            copy.start()
        audio_start(g)

    @pl.when(works_up)
    def _():
        for copy in own_copies:
            copy.start()

    @pl.when(sends_down)
    def _():
        landed_wait(edge_buf, edge_sem)

    @pl.when(jnp.logical_not(has_before))
    def _():
        landed[3, :, 96:128] = jnp.zeros((3, ABLOCK, HEAD_DIM), jnp.bfloat16)

        @pl.when(is_first)
        def _():
            audio_buf[:, :, 0:32] = jnp.zeros((2, 2, ABLOCK, GROUP), jnp.bfloat16)

    @pl.when(jnp.logical_not(has_after))
    def _():
        landed[0, :, 0:32] = jnp.zeros((3, ABLOCK, HEAD_DIM), jnp.bfloat16)

        @pl.when(is_last)
        def _():
            audio_buf[:, :, 96:128] = jnp.zeros((2, 2, ABLOCK, GROUP), jnp.bfloat16)

    from_after = 1 + jnp.where(is_last, 8 * c, 0) + jnp.where(is_first, other, 0)
    from_before = jnp.where(is_last, 1, 0)
    pl.semaphore_wait(barrier, 3 + 2 * role(y, c) + jnp.where(has_after, from_after, 0) + jnp.where(has_before, from_before, 0))

    def up_copies(i, core):
        return [
            pltpu.make_async_remote_copy(
                (k_hbm, v_hbm)[i].at[pl.ds(224, ABLOCK), lanes(group_of(0, core, g))],
                (k_buf, v_buf)[i].at[g, pl.ds(0, ABLOCK)],
                edge_send, halo_recv.at[g if i == 0 else 2], device_id=(v + 1, core), device_id_type=MESH,
            )
            for g in range(2)
        ]

    halo_up = (
        (0, [copy for pair in zip(up_copies(0, 0), up_copies(0, 1)) for copy in pair]),
        (1, up_copies(1, 0)),
        (CHIPS - 1, up_copies(1, 1)),
    )
    @pl.when(sends_down)
    def _():
        for n in range(2):
            j = 2 - 2 * c + n
            for i in range(2):
                pltpu.make_async_remote_copy(
                    edge_buf.at[n, i], edge_kv.at[j, i], edge_send, edge_recv.at[j, i],
                    device_id=(v - 1, 7), device_id_type=MESH,
                ).start()

    @pl.when(has_after)
    def _():
        for chip, copies in halo_up:

            @pl.when((y == chip) & (c == 0))
            def _():
                for copy in copies:
                    copy.start()

        signal(part_ready, (v + 1, y // 2))

    def swap_copies(g, slot):
        k = group_of(y, other, g)
        return [
            pltpu.make_async_remote_copy(
                source.at[:, lanes(k)], target.at[g, slot], dq_send, swap_recv,
                device_id=partner, device_id_type=MESH,
            )
            for source, target in ((q_hbm, q_buf), (og_hbm, og_buf))
        ]

    for g in range(2):
        for copy in swap_copies(g, c):
            copy.start()

    def arrived(j, i):
        landed_wait(edge_kv.at[j, i], edge_recv.at[j, i])

    hand_on = [
        pltpu.make_async_remote_copy(
            edge_kv.at[1 + g, i], buf.at[g, pl.ds(96, ABLOCK)], edge_send, halo_recv.at[g if i == 0 else 2],
            device_id=partner, device_id_type=MESH,
        )
        for g in range(2)
        for i, buf in enumerate((k_buf, v_buf))
    ]

    @pl.when(works_up & edge_early)
    def _():
        for j in range(CHIPS):
            arrived(j, 0)
            arrived(j, 1)
        for copy in hand_on:
            copy.start()

    low_copy.wait()
    high_copy.wait()
    lane = lax.broadcasted_iota(jnp.int32, (8, ROWS), 1)
    row = lax.broadcasted_iota(jnp.int32, (8, ROWS), 0)
    lows = jnp.where(lane < VBLOCK, low_smem[0], low_smem[1])
    highs = jnp.where(lane < VBLOCK, high_smem[0], high_smem[1])
    delta_copy.wait()
    small_buf[c, 0:8] = jnp.where(row == 0, lows, highs).astype(jnp.float32)
    small_buf[c, 8:20] = delta_own[...]
    small_buf[c, 20:24] = jnp.zeros((4, ROWS), jnp.float32)
    small = pltpu.make_async_remote_copy(
        small_buf.at[c], small_buf.at[c], small_send, small_recv, device_id=partner, device_id_type=MESH
    )
    small.start()
    small.wait_recv()

    row = lax.broadcasted_iota(jnp.int32, (REACH, ROWS), 0)
    for slot in range(2):
        blocks = 8 * v + 2 * y + jnp.where(row < 2 * ABLOCK, row // ABLOCK, 3 * slot - 1)
        blocks = blocks.astype(jnp.float32)
        inside = (blocks >= small_buf[slot, 0:1, :]) & (blocks < small_buf[slot, 1:2, :])
        bias_buf[slot] = jnp.where(inside, 0.0, masked_score)

    def part_copies(slot, groups, do, do_local):
        if slot is None:
            start, size, span, exists = ABLOCK, 2 * ABLOCK, v, True
        else:
            start, size = pl.multiple_of(REACH * slot, ABLOCK), ABLOCK
            down, up = is_first & (slot == 0), is_last & (slot == 1)
            span = v - jnp.where(down, 1, 0)
            exists = jnp.logical_not(down & jnp.logical_not(has_before)) & jnp.logical_not(up)
        for g in groups:
            k = group_of(y, c, g)
            for core in range(2):
                source = stage.at[g, core, :, pl.ds(start, size)]
                target = landed.at[y, :, pl.ds(start, size)]
                here = (span == v) & (2 * k + core == a) & exists
                away = jnp.logical_not(here) if g == 1 else True

                @pl.when(away & exists)
                def _():
                    do(
                        pltpu.make_async_remote_copy(
                            source, target, part_send, part_recv,
                            device_id=(span, 2 * k + core), device_id_type=MESH,
                        )
                    )

                if g == 1:

                    @pl.when(here)
                    def _():
                        do_local(pltpu.make_async_copy(source, target, part_recv))

    def dq_copies(g, slot):
        k = group_of(y, c, g)
        return (
            pltpu.make_async_copy(dq_buf.at[g, slot], dq_out.at[:, lanes(k)], out_sem),
            pltpu.make_async_remote_copy(
                dq_buf.at[g, slot], dq_out.at[:, lanes(k)], dq_send, dq_recv,
                device_id=partner, device_id_type=MESH,
            ),
        )

    def work(last):
        slot = jnp.where(is_first, 1, 0)
        if last:
            slot = 1 - slot

        @pl.when(slot == c)
        def _():
            landed_wait(rows_buf.at[:, :, slot], rows_sem)

        @pl.when(slot != c)
        def _():
            landed_wait(rows_buf.at[:, :, slot], swap_recv)

        def halo_wait(ref, sem):
            if last:

                @pl.when((is_first & has_before) | (is_last & has_after & (c == 0)))
                def _():
                    landed_wait(ref, sem)

        def start(copy):
            copy.start()

        def put(heads, rows, key_parts, value_parts):
            for (g, i, _), key_part, value_part in zip(heads, key_parts, value_parts):
                if i == 1:
                    half = lax.broadcasted_iota(jnp.int32, key_part.shape, 1) < HEAD_DIM // 2
                    stage[g, 0, 2, rows] = jnp.where(half, key_part, pltpu.roll(value_part, 64, 1)).astype(jnp.bfloat16)
                    stage[g, 1, 2, rows] = jnp.where(half, pltpu.roll(key_part, 64, 1), value_part).astype(jnp.bfloat16)
                else:
                    stage[g, i // 2, 0, rows] = key_part.astype(jnp.bfloat16)
                    stage[g, i // 2, 1, rows] = value_part.astype(jnp.bfloat16)

        if not last:
            audio_wait()
        middle = pl.ds(ABLOCK, 2 * ABLOCK)
        alone = pl.ds(pl.multiple_of(REACH * slot, ABLOCK), ABLOCK)
        bias = bias_buf[slot]

        def gradients(groups):
            heads = [(g, i, slice(i * HEAD_DIM, (i + 1) * HEAD_DIM)) for g in groups for i in range(3)]
            deltas = [small_buf[slot, pl.ds(8 + 3 * group_of(y, c, g) + i, 1), :] for g, i, _ in heads]

            for g in groups:
                halo_wait(k_buf.at[g, pl.ds(0, ABLOCK)], halo_recv.at[g])
            keys = [jnp.concatenate([k_buf[g, middle, cols], k_buf[g, alone, cols]], axis=0) for g, _, cols in heads]
            scores = [nt(key, q_buf[g, slot, :, cols]) for key, (g, _, cols) in zip(keys, heads)]
            prob_grads = [nt(v_buf[g, middle, cols], og_buf[g, slot, :, cols]) for g, _, cols in heads]
            probs, prob_halves, middle_halves = [], [], []
            for score, prob_grad, delta in zip(scores, prob_grads, deltas):
                score = score + bias
                peak = jnp.max(score, axis=0, keepdims=True)
                weights = jnp.exp2((score - peak) * (logit_scale * math.log2(math.e)))
                prob = weights * (1.0 / jnp.sum(weights, axis=0, keepdims=True))
                probs.append(prob[64:96])
                prob_halves.append(prob.astype(jnp.bfloat16))
                middle_halves.append((prob[0:64] * (prob_grad - delta)).astype(jnp.bfloat16))
            value_parts = [nn(prob, og_buf[g, slot, :, cols]) for prob, (g, _, cols) in zip(prob_halves, heads)]
            key_parts = [nn(score, q_buf[g, slot, :, cols]) * logit_scale for score, (g, _, cols) in zip(middle_halves, heads)]
            if last:
                key_parts = [part + key_sum[g, i] for part, (g, i, _) in zip(key_parts, heads)]
                middle_values = [part[0:64] + value_sum[g, i] for part, (g, i, _) in zip(value_parts, heads)]
                put(heads, middle, key_parts, middle_values)

                part_copies(None, groups, start, start)
            else:
                for key_part, value_part, (g, i, _) in zip(key_parts, value_parts, heads):
                    key_sum[g, i] = key_part
                    value_sum[g, i] = value_part[0:64]

            return heads, deltas, keys, probs, middle_halves, value_parts

        def edge_gradients(groups, heads, deltas, keys, probs, middle_halves, value_parts):
            halo_wait(v_buf.at[:, pl.ds(0, ABLOCK)], halo_recv.at[2])
            prob_grads = [nt(v_buf[g, alone, cols], og_buf[g, slot, :, cols]) for g, _, cols in heads]
            alone_halves = [
                (prob * (prob_grad - delta)).astype(jnp.bfloat16) for prob, prob_grad, delta in zip(probs, prob_grads, deltas)
            ]
            key_parts = [nn(score, q_buf[g, slot, :, cols]) * logit_scale for score, (g, _, cols) in zip(alone_halves, heads)]
            put(heads, alone, key_parts, [part[64:96] for part in value_parts])
            if last:

                @pl.when(is_first & has_before & (0 in groups))
                def _():
                    pl.semaphore_wait(part_ready, 4)

            part_copies(slot, groups if last else (0,), start, start)
            return list(zip(heads, keys, middle_halves, alone_halves))

        if last:
            first = gradients((0,))
            part_copies(1 - slot, (1,), start, start)
            second = gradients((1,))
            done = edge_gradients((0, 1), *[one + other for one, other in zip(first, second)])
        else:
            done = edge_gradients((0, 1), *gradients((0, 1)))
        for (g, _, cols), key, first, second in done:
            score_half = jnp.concatenate([first, second], axis=0)
            dq_buf[g, slot, :, cols] = (tn(score_half, key) * logit_scale).astype(jnp.bfloat16)

        @pl.when(slot == c)
        def _():
            for g in range(2):
                dq_copies(g, slot)[0].start()

        @pl.when(slot != c)
        def _():
            for g in range(2):
                dq_copies(g, slot)[1].start()

    def edge_part_copies(j):
        return [
            pltpu.make_async_remote_copy(
                edge_stage.at[j, core], landed.at[CHIPS - 1, :, pl.ds(96, ABLOCK)],
                edge_send, part_recv,
                device_id=(v + 1, 2 * j + core), device_id_type=MESH,
            )
            for core in range(2)
        ]

    def edge_work(j, wait):
        heads = [slice(i * HEAD_DIM, (i + 1) * HEAD_DIM) for i in range(3)]
        bias = bias_buf[1]
        deltas = [small_buf[1, pl.ds(8 + 3 * j + i, 1), :] for i in range(3)]
        wait(j, 0)
        keys = [jnp.concatenate([k_own[j, :, cols], edge_kv[j, 0, :, cols]], axis=0) for cols in heads]
        scores = [nt(key, q_own[j, :, cols]) + bias for key, cols in zip(keys, heads)]
        probs = []
        for score in scores:
            weights = jnp.exp2((score - jnp.max(score, axis=0, keepdims=True)) * (logit_scale * math.log2(math.e)))
            probs.append(weights[64:96] * (1.0 / jnp.sum(weights, axis=0, keepdims=True)))
        value_parts = [nn(prob.astype(jnp.bfloat16), og_own[j, :, cols]) for prob, cols in zip(probs, heads)]
        wait(j, 1)
        prob_grads = [nt(edge_kv[j, 1, :, cols], og_own[j, :, cols]) for cols in heads]
        halves = [(p * (grad - delta)).astype(jnp.bfloat16) for p, grad, delta in zip(probs, prob_grads, deltas)]
        key_parts = [nn(score, q_own[j, :, cols]) * logit_scale for score, cols in zip(halves, heads)]
        half = lax.broadcasted_iota(jnp.int32, (ABLOCK, HEAD_DIM), 1) < HEAD_DIM // 2
        for core in range(2):
            edge_stage[j, core, 0] = key_parts[2 * core].astype(jnp.bfloat16)
            edge_stage[j, core, 1] = value_parts[2 * core].astype(jnp.bfloat16)
        edge_stage[j, 0, 2] = jnp.where(half, key_parts[1], pltpu.roll(value_parts[1], 64, 1)).astype(jnp.bfloat16)
        edge_stage[j, 1, 2] = jnp.where(half, pltpu.roll(key_parts[1], 64, 1), value_parts[1]).astype(jnp.bfloat16)
        for copy in edge_part_copies(j):
            copy.start()

    @pl.when(works_up)
    def _():
        landed_wait(gauge, own_sem)

        @pl.when(edge_first)
        def _():
            lax.fori_loop(0, CHIPS, lambda j, carry: (edge_work(j, arrived), carry)[1], 0)

    work(False)

    @pl.when(works_up)
    def _():
        @pl.when(jnp.logical_not(edge_first | edge_early))
        def _():
            for j in range(CHIPS):
                arrived(j, 0)
                arrived(j, 1)

        @pl.when(jnp.logical_not(edge_early))
        def _():
            for copy in hand_on:
                copy.start()

        for g in range(2):
            for i in range(2):
                audio_buf[i, g, pl.ds(96, ABLOCK)] = edge_kv[3 * g, i]

    work(True)

    @pl.when(works_up & jnp.logical_not(edge_first))
    def _():
        lax.fori_loop(0, CHIPS, lambda j, carry: (edge_work(j, lambda j, i: None), carry)[1], 0)

    up = jnp.where(is_last, jnp.where(c == 1, 12, 2), jnp.where(c == 0, jnp.where(is_first, 4, jnp.where(y == 1, 2, 0)), 0))
    edge_units = jnp.where(has_after, up, 0) + jnp.where(sends_down, 4, 0)
    for count in (2, 4, 6, 12, 16):

        @pl.when(edge_units == count)
        def _():
            sent_wait(gauge.at[pl.ds(0, count)], edge_send)

    small.wait_send()
    landed_wait(dq_buf.at[:, c], out_sem)
    sent_wait(gauge.at[pl.ds(0, 24)], dq_send)
    landed_wait(dq_buf.at[:, other], dq_recv)

    copies = 4 - (1 - role(y, c))
    to_before = jnp.where(has_before, 4, 0)
    units = 3 * copies + jnp.where(is_first, to_before, jnp.where(is_last, 0, copies))
    for count in (9, 12, 13, 16):

        @pl.when(units == count)
        def _():
            sent_wait(gauge.at[pl.ds(0, count)], part_send)

    @pl.when(has_before & has_after)
    def _():
        landed_wait(gauge.at[pl.ds(0, 16)], part_recv)

    @pl.when(jnp.logical_not(has_before & has_after))
    def _():
        landed_wait(gauge.at[pl.ds(0, 15)], part_recv)


def finish(dq_in, landed, dq_hbm, dk_hbm, dv_hbm, dk_buf, dv_buf, sem):
    c = lax.axis_index("audio") % 2
    dq_copy = pltpu.make_async_copy(dq_in, dq_hbm, sem.at[0])
    dq_copy.start()
    head_rows = pl.ds(pl.multiple_of(64 * c, 64), 128)
    middle_rows = pl.ds(pl.multiple_of(128 - 128 * c, 64), 64)
    for pair in range(2):
        rows = slice(pair * 128, (pair + 1) * 128)
        tiles = []
        for t in range(3):
            blocks = []
            for chip in (2 * pair, 2 * pair + 1):
                for own, far_chip, far in ((32, (chip + 3) % CHIPS, 96), (64, (chip + 1) % CHIPS, 0)):
                    own_term = landed[chip, t, own : own + ABLOCK].astype(jnp.float32)
                    blocks.append(own_term + landed[far_chip, t, far : far + ABLOCK].astype(jnp.float32))
            tiles.append(jnp.concatenate(blocks, axis=0).T.astype(jnp.bfloat16))
        dk_buf[head_rows, rows] = tiles[0]
        dv_buf[head_rows, rows] = tiles[1]
        dk_buf[middle_rows, rows] = tiles[2][0:64]
        dv_buf[middle_rows, rows] = tiles[2][64:128]
    copies = [pltpu.make_async_copy(dk_buf, dk_hbm, sem.at[1]), pltpu.make_async_copy(dv_buf, dv_hbm, sem.at[2])]
    for copy in copies:
        copy.start()
    for copy in [dq_copy] + copies:
        copy.wait()


def on_device(queries, keys, values, out_grad, delta, window_low, window_high):
    bf16, f32 = jnp.bfloat16, jnp.float32
    hbm, vmem = pl.BlockSpec(memory_space=pltpu.HBM), pl.BlockSpec(memory_space=pltpu.VMEM)
    dma = pltpu.SemaphoreType.DMA
    arrays = (queries, keys, values, out_grad, delta, window_low, window_high)
    arrays = [pltpu.with_memory_space_constraint(array, pltpu.HBM) for array in arrays]
    query_grad, landed = pl.pallas_call(
        kernel,
        out_shape=(pltpu.VMEM((ROWS, 1536), bf16), pltpu.VMEM((CHIPS, 3, AROWS, HEAD_DIM), bf16)),
        in_specs=[hbm] * 7,
        out_specs=(vmem, vmem),
        scratch_shapes=[
            pltpu.VMEM((2, 2, 2, ROWS, GROUP), bf16),
            pltpu.VMEM((2, 2, AROWS, GROUP), bf16),
            pltpu.VMEM((2, 2, ABLOCK, GROUP), bf16),
            pltpu.VMEM((2, CHIPS, ROWS, GROUP), bf16),
            pltpu.VMEM((CHIPS, 2 * ABLOCK, GROUP), bf16),
            pltpu.VMEM((CHIPS, 2, ABLOCK, GROUP), bf16),
            pltpu.VMEM((CHIPS, 2, 3, ABLOCK, HEAD_DIM), bf16),
            pltpu.VMEM((12, ROWS), f32),
            pltpu.VMEM((2, 24, ROWS), f32),
            pltpu.VMEM((2, REACH, ROWS), f32),
            pltpu.VMEM((2, 2, ROWS, GROUP), bf16),
            pltpu.VMEM((2, 3, 2 * ABLOCK, HEAD_DIM), f32),
            pltpu.VMEM((2, 3, 2 * ABLOCK, HEAD_DIM), f32),
            pltpu.VMEM((2, 2, 3, AROWS, HEAD_DIM), bf16),
            pltpu.VMEM((40, ABLOCK, GROUP), bf16),
            pltpu.SMEM((2,), jnp.int32),
            pltpu.SMEM((2,), jnp.int32),
            dma((2,)),
            dma(()),
            dma(()),
            dma(()),
            dma(()),
            dma(()),
            dma(()),
            dma(()),
            dma(()),
            dma(()),
            dma(()),
            dma((3,)),
            dma((CHIPS, 2)),
            dma(()),
            dma(()),
            dma(()),
            dma(()),
            pltpu.SemaphoreType.REGULAR,
        ],
        compiler_params=pltpu.CompilerParams(
            collective_id=0, has_side_effects=True, vmem_limit_bytes=32 << 20
        ),
        name="attention_backward",
    )(*arrays)
    query_grad, key_grad, value_grad = pl.pallas_call(
        finish,
        out_shape=(
            jax.ShapeDtypeStruct((ROWS, 1536), bf16),
            jax.ShapeDtypeStruct((192, 256), bf16),
            jax.ShapeDtypeStruct((192, 256), bf16),
        ),
        in_specs=[vmem, vmem],
        out_specs=(hbm, hbm, hbm),
        scratch_shapes=[pltpu.VMEM((192, 256), bf16), pltpu.VMEM((192, 256), bf16), dma((3,))],
        compiler_params=pltpu.CompilerParams(vmem_limit_bytes=32 << 20),
        name="sum_partials",
    )(query_grad, landed)
    return query_grad, key_grad.T, value_grad.T


def solution(mesh):
    return jax.shard_map(
        on_device,
        mesh=mesh,
        in_specs=(
            P(("video", "audio"), None),
            P("video", None),
            P("video", None),
            P(("video", "audio"), None),
            P(None, ("video", "audio")),
            P(("video", "audio")),
            P(("video", "audio")),
        ),
        out_specs=(P(("video", "audio"), None), P("video", "audio"), P("video", "audio")),
        check_vma=False,
    )
```

```python
import math

import jax
import jax.numpy as jnp
from jax import lax
from jax.experimental import pallas as pl
from jax.experimental.pallas import tpu as pltpu
from jax.sharding import PartitionSpec as P

HEAD_DIM = 128
VBLOCK = 64
ABLOCK = 32
SPANS = 64
CHIPS = 4
ROWS = 128
AROWS = 128
REACH = 96
GROUP = 384

MESH = pl.DeviceIdType.MESH
masked_score = -1e30
logit_scale = 1.0 / math.sqrt(HEAD_DIM)


def nt(a, b):
    return lax.dot_general(a, b, (((1,), (1,)), ((), ())), preferred_element_type=jnp.float32)


def nn(a, b):
    return lax.dot_general(a, b, (((1,), (0,)), ((), ())), preferred_element_type=jnp.float32)


def tn(a, b):
    return lax.dot_general(a, b, (((0,), (0,)), ((), ())), preferred_element_type=jnp.float32)


def kernel(
    q_hbm, k_hbm, v_hbm, og_hbm, delta_hbm, low_hbm, high_hbm,
    dq_out, landed,
    rows_buf, audio_buf, edge_buf, own_rows, k_own, edge_kv, edge_stage, delta_own, small_buf, bias_buf, dq_buf,
    key_sum, value_sum, stage, gauge,
    low_smem, high_smem,
    win_sem, delta_sem, rows_sem, audio_sem, edge_sem, own_sem, out_sem,
    swap_send, swap_recv, small_send, small_recv, halo_send, halo_recv, edge_send, edge_recv, edge_part_send,
    part_send, part_recv, dq_send, dq_recv, part_ready,
):
    v = lax.axis_index("video")
    a = lax.axis_index("audio")
    y, c = a // 2, a % 2
    other = 1 - c
    partner = (v, 2 * y + other)
    q_buf, og_buf = rows_buf.at[0], rows_buf.at[1]
    k_buf, v_buf = audio_buf.at[0], audio_buf.at[1]
    q_own, og_own = own_rows.at[0], own_rows.at[1]
    has_before, has_after = v > 0, v < SPANS - 1
    is_first, is_last = y == 0, y == CHIPS - 1

    def role(chip, core):
        return jnp.where(chip == CHIPS - 1, 1 - core, core)

    def group_of(chip, core, g):
        return (chip + jnp.where(role(chip, core) == 0, 1 - g, 2 + g)) % CHIPS

    def signal(semaphore, device):
        pl.semaphore_signal(semaphore, inc=1, device_id=device, device_id_type=MESH)

    barrier = pltpu.get_barrier_semaphore()

    @pl.when(is_last & has_after & (c == 1))
    def _():
        signal(barrier, (v + 1, 7))
        signal(barrier, (v + 1, 6))

    signal(barrier, partner)

    @pl.when(has_before)
    def _():
        signal(barrier, (v - 1, 7))

        @pl.when(is_first)
        def _():
            for i in range(4):
                signal(barrier, (v - 1, 4 * c + i))

        @pl.when(is_first & (c == 1))
        def _():
            signal(barrier, (v - 1, 0))

    for ahead, part in ((3, 0), (2, 1), (1, 1)):
        chip = (y + ahead) % CHIPS
        signal(barrier, (v, 2 * chip + role(chip, part)))

    low_copy = pltpu.make_async_copy(low_hbm, low_smem, win_sem.at[0])
    high_copy = pltpu.make_async_copy(high_hbm, high_smem, win_sem.at[1])
    delta_copy = pltpu.make_async_copy(delta_hbm, delta_own, delta_sem)
    low_copy.start()
    high_copy.start()
    delta_copy.start()

    def lanes(k):
        return pl.ds(k * GROUP if isinstance(k, int) else pl.multiple_of(k * GROUP, GROUP), GROUP)

    def landed_wait(ref, sem):
        pltpu.make_async_copy(ref, ref, sem).wait()

    def sent_wait(ref, sem):
        pltpu.make_async_remote_copy(
            ref, ref, sem, dq_recv, device_id=partner, device_id_type=MESH
        ).wait_send()

    def row_copies(g):
        k = group_of(y, c, g)
        return [
            pltpu.make_async_copy(q_hbm.at[:, lanes(k)], q_buf.at[g, c], rows_sem),
            pltpu.make_async_copy(og_hbm.at[:, lanes(k)], og_buf.at[g, c], rows_sem),
        ]

    reaches = ((is_first, 0, 32, 96), (is_last, 160, 0, 96), ((y > 0) & (y < CHIPS - 1), 64 * y - 32, 0, AROWS))

    def audio_start(g):
        k = group_of(y, c, g)
        for chosen, first, target, count in reaches:

            @pl.when(chosen)
            def _():
                for source, buf in ((k_hbm, k_buf), (v_hbm, v_buf)):
                    rows = pl.ds(first if isinstance(first, int) else pl.multiple_of(first, 32), count)
                    pltpu.make_async_copy(source.at[rows, lanes(k)], buf.at[g, pl.ds(target, count)], audio_sem).start()

    def audio_wait():
        for chosen, _, target, count in reaches:

            @pl.when(chosen)
            def _():
                landed_wait(audio_buf.at[:, :, pl.ds(target, count)], audio_sem)

    sends_down = is_last & has_before
    works_up = is_last & has_after & (c == 1)
    edge_first, edge_early = v % 16 == 15, v % 16 == 0

    edge_orders = (((1, 1), (0, 2), (1, 2), (1, 3)), ((0, 0), (1, 0), (0, 1), (0, 3)))
    for core, order in enumerate(edge_orders):

        @pl.when(sends_down & (c == core))
        def _():
            for n, (i, j) in enumerate(order):
                source = (k_hbm, v_hbm)[i].at[pl.ds(0, ABLOCK), lanes(j)]
                pltpu.make_async_copy(source, edge_buf.at[n], edge_sem).start()

    own_copies = []
    for j in range(CHIPS):
        k = j
        own_copies += [
            pltpu.make_async_copy(q_hbm.at[:, lanes(k)], q_own.at[j], own_sem.at[0]),
            pltpu.make_async_copy(og_hbm.at[:, lanes(k)], og_own.at[j], own_sem.at[0]),
            pltpu.make_async_copy(k_hbm.at[pl.ds(192, 2 * ABLOCK), lanes(k)], k_own.at[j], own_sem.at[1]),
        ]

    for g in range(2):
        for copy in row_copies(g):
            copy.start()
        audio_start(g)

    @pl.when(works_up)
    def _():
        for copy in own_copies:
            copy.start()

    @pl.when(sends_down)
    def _():
        landed_wait(edge_buf, edge_sem)

    @pl.when(jnp.logical_not(has_before))
    def _():
        landed[3, :, 96:128] = jnp.zeros((3, ABLOCK, HEAD_DIM), jnp.bfloat16)

        @pl.when(is_first)
        def _():
            audio_buf[:, :, 0:32] = jnp.zeros((2, 2, ABLOCK, GROUP), jnp.bfloat16)

    @pl.when(jnp.logical_not(has_after))
    def _():
        landed[0, :, 0:32] = jnp.zeros((3, ABLOCK, HEAD_DIM), jnp.bfloat16)

        @pl.when(is_last)
        def _():
            audio_buf[:, :, 96:128] = jnp.zeros((2, 2, ABLOCK, GROUP), jnp.bfloat16)

    from_after = 1 + jnp.where(is_last, 8 * c, 0) + jnp.where(is_first, other, 0)
    from_before = jnp.where(is_last, 1, 0)
    pl.semaphore_wait(barrier, 3 + 2 * role(y, c) + jnp.where(has_after, from_after, 0) + jnp.where(has_before, from_before, 0))

    def up_copies(i, core):
        return [
            pltpu.make_async_remote_copy(
                (k_hbm, v_hbm)[i].at[pl.ds(224, ABLOCK), lanes(group_of(0, core, g))],
                (k_buf, v_buf)[i].at[g, pl.ds(0, ABLOCK)],
                halo_send, halo_recv.at[g if i == 0 else 2], device_id=(v + 1, core), device_id_type=MESH,
            )
            for g in range(2)
        ]

    halo_up = (
        (0, [copy for pair in zip(up_copies(0, 0), up_copies(0, 1)) for copy in pair]),
        (1, up_copies(1, 0)),
        (CHIPS - 1, up_copies(1, 1)),
    )
    for core, order in enumerate(edge_orders):

        @pl.when(sends_down & (c == core))
        def _():
            for n, (i, j) in enumerate(order):
                pltpu.make_async_remote_copy(
                    edge_buf.at[n], edge_kv.at[j, i], edge_send, edge_recv.at[j, i],
                    device_id=(v - 1, 7), device_id_type=MESH,
                ).start()

    @pl.when(has_after)
    def _():
        for chip, copies in halo_up:

            @pl.when((y == chip) & (c == 0))
            def _():
                for copy in copies:
                    copy.start()

        signal(part_ready, (v + 1, y // 2))

    def swap_copies(g, slot):
        k = group_of(y, other, g)
        return [
            pltpu.make_async_remote_copy(
                source.at[:, lanes(k)], target.at[g, slot], swap_send, swap_recv,
                device_id=partner, device_id_type=MESH,
            )
            for source, target in ((q_hbm, q_buf), (og_hbm, og_buf))
        ]

    for g in range(2):
        for copy in swap_copies(g, c):
            copy.start()

    def arrived(j, i):
        landed_wait(edge_kv.at[j, i], edge_recv.at[j, i])

    hand_on = [
        pltpu.make_async_remote_copy(
            edge_kv.at[1 + g, i], buf.at[g, pl.ds(96, ABLOCK)], halo_send, halo_recv.at[g if i == 0 else 2],
            device_id=partner, device_id_type=MESH,
        )
        for g in range(2)
        for i, buf in enumerate((k_buf, v_buf))
    ]

    @pl.when(works_up & edge_early)
    def _():
        for j in range(CHIPS):
            arrived(j, 0)
            arrived(j, 1)
        for copy in hand_on:
            copy.start()

    low_copy.wait()
    high_copy.wait()
    lane = lax.broadcasted_iota(jnp.int32, (8, ROWS), 1)
    row = lax.broadcasted_iota(jnp.int32, (8, ROWS), 0)
    lows = jnp.where(lane < VBLOCK, low_smem[0], low_smem[1])
    highs = jnp.where(lane < VBLOCK, high_smem[0], high_smem[1])
    delta_copy.wait()
    small_buf[c, 0:8] = jnp.where(row == 0, lows, highs).astype(jnp.float32)
    small_buf[c, 8:20] = delta_own[...]
    small_buf[c, 20:24] = jnp.zeros((4, ROWS), jnp.float32)
    small = pltpu.make_async_remote_copy(
        small_buf.at[c], small_buf.at[c], small_send, small_recv, device_id=partner, device_id_type=MESH
    )
    small.start()
    small.wait_recv()

    row = lax.broadcasted_iota(jnp.int32, (REACH, ROWS), 0)
    for slot in range(2):
        blocks = 8 * v + 2 * y + jnp.where(row < 2 * ABLOCK, row // ABLOCK, 3 * slot - 1)
        blocks = blocks.astype(jnp.float32)
        inside = (blocks >= small_buf[slot, 0:1, :]) & (blocks < small_buf[slot, 1:2, :])
        bias_buf[slot] = jnp.where(inside, 0.0, masked_score)

    def part_copies(slot, groups, do, do_local):
        if slot is None:
            start, size, span, exists = ABLOCK, 2 * ABLOCK, v, True
        else:
            start, size = pl.multiple_of(REACH * slot, ABLOCK), ABLOCK
            down, up = is_first & (slot == 0), is_last & (slot == 1)
            span = v - jnp.where(down, 1, 0)
            exists = jnp.logical_not(down & jnp.logical_not(has_before)) & jnp.logical_not(up)
        for g in groups:
            k = group_of(y, c, g)
            for core in range(2):
                source = stage.at[g, core, :, pl.ds(start, size)]
                target = landed.at[y, :, pl.ds(start, size)]
                here = (span == v) & (2 * k + core == a) & exists
                away = jnp.logical_not(here) if g == 1 else True

                @pl.when(away & exists)
                def _():
                    do(
                        pltpu.make_async_remote_copy(
                            source, target, part_send, part_recv,
                            device_id=(span, 2 * k + core), device_id_type=MESH,
                        )
                    )

                if g == 1:

                    @pl.when(here)
                    def _():
                        do_local(pltpu.make_async_copy(source, target, part_recv))

    def dq_copies(g, slot):
        k = group_of(y, c, g)
        return (
            pltpu.make_async_copy(dq_buf.at[g, slot], dq_out.at[:, lanes(k)], out_sem),
            pltpu.make_async_remote_copy(
                dq_buf.at[g, slot], dq_out.at[:, lanes(k)], dq_send, dq_recv,
                device_id=partner, device_id_type=MESH,
            ),
        )

    def work(last):
        slot = jnp.where(is_first, 1, 0)
        if last:
            slot = 1 - slot

        @pl.when(slot == c)
        def _():
            landed_wait(rows_buf.at[:, :, slot], rows_sem)

        @pl.when(slot != c)
        def _():
            landed_wait(rows_buf.at[:, :, slot], swap_recv)

        def halo_wait(ref, sem):
            if last:

                @pl.when((is_first & has_before) | (is_last & has_after & (c == 0)))
                def _():
                    landed_wait(ref, sem)

        def start(copy):
            copy.start()

        def put(heads, rows, key_parts, value_parts):
            for (g, i, _), key_part, value_part in zip(heads, key_parts, value_parts):
                if i == 1:
                    half = lax.broadcasted_iota(jnp.int32, key_part.shape, 1) < HEAD_DIM // 2
                    stage[g, 0, 2, rows] = jnp.where(half, key_part, pltpu.roll(value_part, 64, 1)).astype(jnp.bfloat16)
                    stage[g, 1, 2, rows] = jnp.where(half, pltpu.roll(key_part, 64, 1), value_part).astype(jnp.bfloat16)
                else:
                    stage[g, i // 2, 0, rows] = key_part.astype(jnp.bfloat16)
                    stage[g, i // 2, 1, rows] = value_part.astype(jnp.bfloat16)

        if not last:
            audio_wait()
        middle = pl.ds(ABLOCK, 2 * ABLOCK)
        alone = pl.ds(pl.multiple_of(REACH * slot, ABLOCK), ABLOCK)
        bias = bias_buf[slot]

        def gradients(groups):
            heads = [(g, i, slice(i * HEAD_DIM, (i + 1) * HEAD_DIM)) for g in groups for i in range(3)]
            deltas = [small_buf[slot, pl.ds(8 + 3 * group_of(y, c, g) + i, 1), :] for g, i, _ in heads]

            for g in groups:
                halo_wait(k_buf.at[g, pl.ds(0, ABLOCK)], halo_recv.at[g])
            keys = [jnp.concatenate([k_buf[g, middle, cols], k_buf[g, alone, cols]], axis=0) for g, _, cols in heads]
            scores = [nt(key, q_buf[g, slot, :, cols]) for key, (g, _, cols) in zip(keys, heads)]
            prob_grads = [nt(v_buf[g, middle, cols], og_buf[g, slot, :, cols]) for g, _, cols in heads]
            probs, prob_halves, middle_halves = [], [], []
            for score, prob_grad, delta in zip(scores, prob_grads, deltas):
                score = score + bias
                peak = jnp.max(score, axis=0, keepdims=True)
                weights = jnp.exp2((score - peak) * (logit_scale * math.log2(math.e)))
                prob = weights * (1.0 / jnp.sum(weights, axis=0, keepdims=True))
                probs.append(prob[64:96])
                prob_halves.append(prob.astype(jnp.bfloat16))
                middle_halves.append((prob[0:64] * (prob_grad - delta)).astype(jnp.bfloat16))
            value_parts = [nn(prob, og_buf[g, slot, :, cols]) for prob, (g, _, cols) in zip(prob_halves, heads)]
            key_parts = [nn(score, q_buf[g, slot, :, cols]) * logit_scale for score, (g, _, cols) in zip(middle_halves, heads)]
            if last:
                key_parts = [part + key_sum[g, i] for part, (g, i, _) in zip(key_parts, heads)]
                middle_values = [part[0:64] + value_sum[g, i] for part, (g, i, _) in zip(value_parts, heads)]
                put(heads, middle, key_parts, middle_values)

                part_copies(None, groups, start, start)
            else:
                for key_part, value_part, (g, i, _) in zip(key_parts, value_parts, heads):
                    key_sum[g, i] = key_part
                    value_sum[g, i] = value_part[0:64]

            return heads, deltas, keys, probs, middle_halves, value_parts

        def edge_gradients(groups, heads, deltas, keys, probs, middle_halves, value_parts):
            halo_wait(v_buf.at[:, pl.ds(0, ABLOCK)], halo_recv.at[2])
            prob_grads = [nt(v_buf[g, alone, cols], og_buf[g, slot, :, cols]) for g, _, cols in heads]
            alone_halves = [
                (prob * (prob_grad - delta)).astype(jnp.bfloat16) for prob, prob_grad, delta in zip(probs, prob_grads, deltas)
            ]
            key_parts = [nn(score, q_buf[g, slot, :, cols]) * logit_scale for score, (g, _, cols) in zip(alone_halves, heads)]
            put(heads, alone, key_parts, [part[64:96] for part in value_parts])
            if last:

                @pl.when(is_first & has_before & (0 in groups))
                def _():
                    pl.semaphore_wait(part_ready, 4)

            part_copies(slot, groups if last else (0,), start, start)
            return list(zip(heads, keys, middle_halves, alone_halves))

        if last:
            first = gradients((0,))
            part_copies(1 - slot, (1,), start, start)
            second = gradients((1,))
            done = edge_gradients((0, 1), *[one + other for one, other in zip(first, second)])
        else:
            done = edge_gradients((0, 1), *gradients((0, 1)))
        for (g, _, cols), key, first, second in done:
            score_half = jnp.concatenate([first, second], axis=0)
            dq_buf[g, slot, :, cols] = (tn(score_half, key) * logit_scale).astype(jnp.bfloat16)

        @pl.when(slot == c)
        def _():
            for g in range(2):
                dq_copies(g, slot)[0].start()

        @pl.when(slot != c)
        def _():
            for g in range(2):
                dq_copies(g, slot)[1].start()

    def edge_part_copies(j):
        return [
            pltpu.make_async_remote_copy(
                edge_stage.at[j, core], landed.at[CHIPS - 1, :, pl.ds(96, ABLOCK)],
                edge_part_send, part_recv,
                device_id=(v + 1, 2 * j + core), device_id_type=MESH,
            )
            for core in range(2)
        ]

    def edge_work(j, wait):
        heads = [slice(i * HEAD_DIM, (i + 1) * HEAD_DIM) for i in range(3)]
        bias = bias_buf[1]
        deltas = [small_buf[1, pl.ds(8 + 3 * j + i, 1), :] for i in range(3)]
        wait(j, 0)
        keys = [jnp.concatenate([k_own[j, :, cols], edge_kv[j, 0, :, cols]], axis=0) for cols in heads]
        scores = [nt(key, q_own[j, :, cols]) + bias for key, cols in zip(keys, heads)]
        probs = []
        for score in scores:
            weights = jnp.exp2((score - jnp.max(score, axis=0, keepdims=True)) * (logit_scale * math.log2(math.e)))
            probs.append(weights[64:96] * (1.0 / jnp.sum(weights, axis=0, keepdims=True)))
        value_parts = [nn(prob.astype(jnp.bfloat16), og_own[j, :, cols]) for prob, cols in zip(probs, heads)]
        wait(j, 1)
        prob_grads = [nt(edge_kv[j, 1, :, cols], og_own[j, :, cols]) for cols in heads]
        halves = [(p * (grad - delta)).astype(jnp.bfloat16) for p, grad, delta in zip(probs, prob_grads, deltas)]
        key_parts = [nn(score, q_own[j, :, cols]) * logit_scale for score, cols in zip(halves, heads)]
        half = lax.broadcasted_iota(jnp.int32, (ABLOCK, HEAD_DIM), 1) < HEAD_DIM // 2
        for core in range(2):
            edge_stage[j, core, 0] = key_parts[2 * core].astype(jnp.bfloat16)
            edge_stage[j, core, 1] = value_parts[2 * core].astype(jnp.bfloat16)
        edge_stage[j, 0, 2] = jnp.where(half, key_parts[1], pltpu.roll(value_parts[1], 64, 1)).astype(jnp.bfloat16)
        edge_stage[j, 1, 2] = jnp.where(half, pltpu.roll(key_parts[1], 64, 1), value_parts[1]).astype(jnp.bfloat16)
        for copy in edge_part_copies(j):
            copy.start()

    @pl.when(works_up)
    def _():
        landed_wait(own_rows, own_sem.at[0])
        landed_wait(k_own, own_sem.at[1])

        @pl.when(edge_first)
        def _():
            lax.fori_loop(0, CHIPS, lambda j, carry: (edge_work(j, arrived), carry)[1], 0)

    work(False)

    @pl.when(works_up)
    def _():
        @pl.when(jnp.logical_not(edge_first | edge_early))
        def _():
            for j in range(CHIPS):
                arrived(j, 0)
                arrived(j, 1)

        @pl.when(jnp.logical_not(edge_early))
        def _():
            for copy in hand_on:
                copy.start()

        for g in range(2):
            for i in range(2):
                audio_buf[i, g, pl.ds(96, ABLOCK)] = edge_kv[3 * g, i]

    work(True)

    @pl.when(works_up & jnp.logical_not(edge_first))
    def _():
        lax.fori_loop(0, CHIPS, lambda j, carry: (edge_work(j, lambda j, i: None), carry)[1], 0)

    @pl.when(sends_down)
    def _():
        sent_wait(edge_buf, edge_send)

    @pl.when(works_up)
    def _():
        sent_wait(gauge.at[pl.ds(0, 4)], halo_send)
        sent_wait(edge_stage, edge_part_send)

    for chip, copies in halo_up:

        @pl.when((y == chip) & (c == 0) & has_after)
        def _():
            sent_wait(gauge.at[pl.ds(0, len(copies))], halo_send)

    small.wait_send()
    sent_wait(rows_buf.at[:, :, c], swap_send)
    landed_wait(dq_buf.at[:, c], out_sem)
    sent_wait(dq_buf.at[:, other], dq_send)
    landed_wait(dq_buf.at[:, other], dq_recv)

    copies = 4 - (1 - role(y, c))
    to_before = jnp.where(has_before, 4, 0)
    units = 3 * copies + jnp.where(is_first, to_before, jnp.where(is_last, 0, copies))
    for count in (9, 12, 13, 16):

        @pl.when(units == count)
        def _():
            sent_wait(gauge.at[pl.ds(0, count)], part_send)

    @pl.when(has_before & has_after)
    def _():
        landed_wait(gauge, part_recv)

    @pl.when(jnp.logical_not(has_before & has_after))
    def _():
        landed_wait(gauge.at[pl.ds(0, 15)], part_recv)


def finish(dq_in, landed, dq_hbm, dk_hbm, dv_hbm, dk_buf, dv_buf, sem):
    c = lax.axis_index("audio") % 2
    dq_copy = pltpu.make_async_copy(dq_in, dq_hbm, sem.at[0])
    dq_copy.start()
    head_rows = pl.ds(pl.multiple_of(64 * c, 64), 128)
    middle_rows = pl.ds(pl.multiple_of(128 - 128 * c, 64), 64)
    for pair in range(2):
        rows = slice(pair * 128, (pair + 1) * 128)
        tiles = []
        for t in range(3):
            blocks = []
            for chip in (2 * pair, 2 * pair + 1):
                for own, far_chip, far in ((32, (chip + 3) % CHIPS, 96), (64, (chip + 1) % CHIPS, 0)):
                    own_term = landed[chip, t, own : own + ABLOCK].astype(jnp.float32)
                    blocks.append(own_term + landed[far_chip, t, far : far + ABLOCK].astype(jnp.float32))
            tiles.append(jnp.concatenate(blocks, axis=0).T.astype(jnp.bfloat16))
        dk_buf[head_rows, rows] = tiles[0]
        dv_buf[head_rows, rows] = tiles[1]
        dk_buf[middle_rows, rows] = tiles[2][0:64]
        dv_buf[middle_rows, rows] = tiles[2][64:128]
    copies = [pltpu.make_async_copy(dk_buf, dk_hbm, sem.at[1]), pltpu.make_async_copy(dv_buf, dv_hbm, sem.at[2])]
    for copy in copies:
        copy.start()
    for copy in [dq_copy] + copies:
        copy.wait()


def on_device(queries, keys, values, out_grad, delta, window_low, window_high):
    bf16, f32 = jnp.bfloat16, jnp.float32
    hbm, vmem = pl.BlockSpec(memory_space=pltpu.HBM), pl.BlockSpec(memory_space=pltpu.VMEM)
    dma = pltpu.SemaphoreType.DMA
    arrays = (queries, keys, values, out_grad, delta, window_low, window_high)
    arrays = [pltpu.with_memory_space_constraint(array, pltpu.HBM) for array in arrays]
    query_grad, landed = pl.pallas_call(
        kernel,
        out_shape=(pltpu.VMEM((ROWS, 1536), bf16), pltpu.VMEM((CHIPS, 3, AROWS, HEAD_DIM), bf16)),
        in_specs=[hbm] * 7,
        out_specs=(vmem, vmem),
        scratch_shapes=[
            pltpu.VMEM((2, 2, 2, ROWS, GROUP), bf16),
            pltpu.VMEM((2, 2, AROWS, GROUP), bf16),
            pltpu.VMEM((4, ABLOCK, GROUP), bf16),
            pltpu.VMEM((2, CHIPS, ROWS, GROUP), bf16),
            pltpu.VMEM((CHIPS, 2 * ABLOCK, GROUP), bf16),
            pltpu.VMEM((CHIPS, 2, ABLOCK, GROUP), bf16),
            pltpu.VMEM((CHIPS, 2, 3, ABLOCK, HEAD_DIM), bf16),
            pltpu.VMEM((12, ROWS), f32),
            pltpu.VMEM((2, 24, ROWS), f32),
            pltpu.VMEM((2, REACH, ROWS), f32),
            pltpu.VMEM((2, 2, ROWS, GROUP), bf16),
            pltpu.VMEM((2, 3, 2 * ABLOCK, HEAD_DIM), f32),
            pltpu.VMEM((2, 3, 2 * ABLOCK, HEAD_DIM), f32),
            pltpu.VMEM((2, 2, 3, AROWS, HEAD_DIM), bf16),
            pltpu.VMEM((16, ABLOCK, GROUP), bf16),
            pltpu.SMEM((2,), jnp.int32),
            pltpu.SMEM((2,), jnp.int32),
            dma((2,)),
            dma(()),
            dma(()),
            dma(()),
            dma(()),
            dma((2,)),
            dma(()),
            dma(()),
            dma(()),
            dma(()),
            dma(()),
            dma(()),
            dma((3,)),
            dma(()),
            dma((CHIPS, 2)),
            dma(()),
            dma(()),
            dma(()),
            dma(()),
            dma(()),
            pltpu.SemaphoreType.REGULAR,
        ],
        compiler_params=pltpu.CompilerParams(
            collective_id=0, has_side_effects=True, vmem_limit_bytes=32 << 20
        ),
        name="attention_backward",
    )(*arrays)
    query_grad, key_grad, value_grad = pl.pallas_call(
        finish,
        out_shape=(
            jax.ShapeDtypeStruct((ROWS, 1536), bf16),
            jax.ShapeDtypeStruct((192, 256), bf16),
            jax.ShapeDtypeStruct((192, 256), bf16),
        ),
        in_specs=[vmem, vmem],
        out_specs=(hbm, hbm, hbm),
        scratch_shapes=[pltpu.VMEM((192, 256), bf16), pltpu.VMEM((192, 256), bf16), dma((3,))],
        compiler_params=pltpu.CompilerParams(vmem_limit_bytes=32 << 20),
        name="sum_partials",
    )(query_grad, landed)
    return query_grad, key_grad.T, value_grad.T


def solution(mesh):
    return jax.shard_map(
        on_device,
        mesh=mesh,
        in_specs=(
            P(("video", "audio"), None),
            P("video", None),
            P("video", None),
            P(("video", "audio"), None),
            P(None, ("video", "audio")),
            P(("video", "audio")),
            P(("video", "audio")),
        ),
        out_specs=(P(("video", "audio"), None), P("video", "audio"), P("video", "audio")),
        check_vma=False,
    )
```

```python
import math

import jax
import jax.numpy as jnp
from jax import lax
from jax.experimental import pallas as pl
from jax.experimental.pallas import tpu as pltpu
from jax.sharding import PartitionSpec as P

HEAD_DIM = 128
VBLOCK = 64
ABLOCK = 32
SPANS = 64
CHIPS = 4
ROWS = 128
AROWS = 128
REACH = 96
GROUP = 384

MESH = pl.DeviceIdType.MESH
masked_score = -1e30
logit_scale = 1.0 / math.sqrt(HEAD_DIM)


def nt(a, b):
    return lax.dot_general(a, b, (((1,), (1,)), ((), ())), preferred_element_type=jnp.float32)


def nn(a, b):
    return lax.dot_general(a, b, (((1,), (0,)), ((), ())), preferred_element_type=jnp.float32)


def tn(a, b):
    return lax.dot_general(a, b, (((0,), (0,)), ((), ())), preferred_element_type=jnp.float32)


def kernel(
    q_hbm, k_hbm, v_hbm, og_hbm, delta_hbm, low_hbm, high_hbm,
    dq_out, landed,
    rows_buf, audio_buf, edge_buf, own_rows, k_own, edge_kv, edge_stage, delta_own, small_buf, bias_buf, dq_buf,
    key_sum, value_sum, stage, gauge,
    low_smem, high_smem,
    win_sem, delta_sem, rows_sem, audio_sem, edge_sem, own_sem, out_sem,
    swap_recv, small_send, small_recv, edge_send, halo_recv, edge_recv,
    part_send, part_recv, dq_send, dq_recv, part_ready,
):
    v = lax.axis_index("video")
    a = lax.axis_index("audio")
    y, c = a // 2, a % 2
    other = 1 - c
    partner = (v, 2 * y + other)
    q_buf, og_buf = rows_buf.at[0], rows_buf.at[1]
    k_buf, v_buf = audio_buf.at[0], audio_buf.at[1]
    q_own, og_own = own_rows.at[0], own_rows.at[1]
    has_before, has_after = v > 0, v < SPANS - 1
    is_first, is_last = y == 0, y == CHIPS - 1

    def role(chip, core):
        return jnp.where(chip == CHIPS - 1, 1 - core, core)

    def group_of(chip, core, g):
        return (chip + jnp.where(role(chip, core) == 0, 1 - g, 2 + g)) % CHIPS

    def signal(semaphore, device):
        pl.semaphore_signal(semaphore, inc=1, device_id=device, device_id_type=MESH)

    barrier = pltpu.get_barrier_semaphore()

    @pl.when(is_last & has_after & (c == 1))
    def _():
        signal(barrier, (v + 1, 7))
        signal(barrier, (v + 1, 6))

    signal(barrier, partner)

    @pl.when(has_before)
    def _():
        signal(barrier, (v - 1, 7))

        @pl.when(is_first)
        def _():
            for i in range(4):
                signal(barrier, (v - 1, 4 * c + i))

        @pl.when(is_first & (c == 1))
        def _():
            signal(barrier, (v - 1, 0))

    for ahead, part in ((3, 0), (2, 1), (1, 1)):
        chip = (y + ahead) % CHIPS
        signal(barrier, (v, 2 * chip + role(chip, part)))

    low_copy = pltpu.make_async_copy(low_hbm, low_smem, win_sem.at[0])
    high_copy = pltpu.make_async_copy(high_hbm, high_smem, win_sem.at[1])
    delta_copy = pltpu.make_async_copy(delta_hbm, delta_own, delta_sem)
    low_copy.start()
    high_copy.start()
    delta_copy.start()

    def lanes(k):
        return pl.ds(k * GROUP if isinstance(k, int) else pl.multiple_of(k * GROUP, GROUP), GROUP)

    def landed_wait(ref, sem):
        pltpu.make_async_copy(ref, ref, sem).wait()

    def sent_wait(ref, sem):
        pltpu.make_async_remote_copy(
            ref, ref, sem, dq_recv, device_id=partner, device_id_type=MESH
        ).wait_send()

    def row_copies(g):
        k = group_of(y, c, g)
        return [
            pltpu.make_async_copy(q_hbm.at[:, lanes(k)], q_buf.at[g, c], rows_sem),
            pltpu.make_async_copy(og_hbm.at[:, lanes(k)], og_buf.at[g, c], rows_sem),
        ]

    reaches = ((is_first, 0, 32, 96), (is_last, 160, 0, 96), ((y > 0) & (y < CHIPS - 1), 64 * y - 32, 0, AROWS))

    def audio_start(g):
        k = group_of(y, c, g)
        for chosen, first, target, count in reaches:

            @pl.when(chosen)
            def _():
                for source, buf in ((k_hbm, k_buf), (v_hbm, v_buf)):
                    rows = pl.ds(first if isinstance(first, int) else pl.multiple_of(first, 32), count)
                    pltpu.make_async_copy(source.at[rows, lanes(k)], buf.at[g, pl.ds(target, count)], audio_sem).start()

    def audio_wait():
        for chosen, _, target, count in reaches:

            @pl.when(chosen)
            def _():
                landed_wait(audio_buf.at[:, :, pl.ds(target, count)], audio_sem)

    sends_down = is_last & has_before
    works_up = is_last & has_after & (c == 1)
    edge_first, edge_early = v % 16 == 15, v % 16 == 0

    edge_orders = (((1, 1), (0, 2), (1, 2), (1, 3)), ((0, 0), (1, 0), (0, 1), (0, 3)))
    for core, order in enumerate(edge_orders):

        @pl.when(sends_down & (c == core))
        def _():
            for n, (i, j) in enumerate(order):
                source = (k_hbm, v_hbm)[i].at[pl.ds(0, ABLOCK), lanes(j)]
                pltpu.make_async_copy(source, edge_buf.at[n], edge_sem).start()

    own_copies = []
    for j in range(CHIPS):
        k = j
        own_copies += [
            pltpu.make_async_copy(q_hbm.at[:, lanes(k)], q_own.at[j], own_sem),
            pltpu.make_async_copy(og_hbm.at[:, lanes(k)], og_own.at[j], own_sem),
            pltpu.make_async_copy(k_hbm.at[pl.ds(192, 2 * ABLOCK), lanes(k)], k_own.at[j], own_sem),
        ]

    for g in range(2):
        for copy in row_copies(g):
            copy.start()
        audio_start(g)

    @pl.when(works_up)
    def _():
        for copy in own_copies:
            copy.start()

    @pl.when(sends_down)
    def _():
        landed_wait(edge_buf, edge_sem)

    @pl.when(jnp.logical_not(has_before))
    def _():
        landed[3, :, 96:128] = jnp.zeros((3, ABLOCK, HEAD_DIM), jnp.bfloat16)

        @pl.when(is_first)
        def _():
            audio_buf[:, :, 0:32] = jnp.zeros((2, 2, ABLOCK, GROUP), jnp.bfloat16)

    @pl.when(jnp.logical_not(has_after))
    def _():
        landed[0, :, 0:32] = jnp.zeros((3, ABLOCK, HEAD_DIM), jnp.bfloat16)

        @pl.when(is_last)
        def _():
            audio_buf[:, :, 96:128] = jnp.zeros((2, 2, ABLOCK, GROUP), jnp.bfloat16)

    from_after = 1 + jnp.where(is_last, 8 * c, 0) + jnp.where(is_first, other, 0)
    from_before = jnp.where(is_last, 1, 0)
    pl.semaphore_wait(barrier, 3 + 2 * role(y, c) + jnp.where(has_after, from_after, 0) + jnp.where(has_before, from_before, 0))

    def up_copies(i, core):
        return [
            pltpu.make_async_remote_copy(
                (k_hbm, v_hbm)[i].at[pl.ds(224, ABLOCK), lanes(group_of(0, core, g))],
                (k_buf, v_buf)[i].at[g, pl.ds(0, ABLOCK)],
                edge_send, halo_recv.at[g if i == 0 else 2], device_id=(v + 1, core), device_id_type=MESH,
            )
            for g in range(2)
        ]

    halo_up = (
        (0, [copy for pair in zip(up_copies(0, 0), up_copies(0, 1)) for copy in pair]),
        (1, up_copies(1, 0)),
        (CHIPS - 1, up_copies(1, 1)),
    )
    for core, order in enumerate(edge_orders):

        @pl.when(sends_down & (c == core))
        def _():
            for n, (i, j) in enumerate(order):
                pltpu.make_async_remote_copy(
                    edge_buf.at[n], edge_kv.at[j, i], edge_send, edge_recv.at[j, i],
                    device_id=(v - 1, 7), device_id_type=MESH,
                ).start()

    @pl.when(has_after)
    def _():
        for chip, copies in halo_up:

            @pl.when((y == chip) & (c == 0))
            def _():
                for copy in copies:
                    copy.start()

        signal(part_ready, (v + 1, y // 2))

    def swap_copies(g, slot):
        k = group_of(y, other, g)
        return [
            pltpu.make_async_remote_copy(
                source.at[:, lanes(k)], target.at[g, slot], dq_send, swap_recv,
                device_id=partner, device_id_type=MESH,
            )
            for source, target in ((q_hbm, q_buf), (og_hbm, og_buf))
        ]

    for g in range(2):
        for copy in swap_copies(g, c):
            copy.start()

    def arrived(j, i):
        landed_wait(edge_kv.at[j, i], edge_recv.at[j, i])

    hand_on = [
        pltpu.make_async_remote_copy(
            edge_kv.at[1 + g, i], buf.at[g, pl.ds(96, ABLOCK)], edge_send, halo_recv.at[g if i == 0 else 2],
            device_id=partner, device_id_type=MESH,
        )
        for g in range(2)
        for i, buf in enumerate((k_buf, v_buf))
    ]

    @pl.when(works_up & edge_early)
    def _():
        for j in range(CHIPS):
            arrived(j, 0)
            arrived(j, 1)
        for copy in hand_on:
            copy.start()

    low_copy.wait()
    high_copy.wait()
    lane = lax.broadcasted_iota(jnp.int32, (8, ROWS), 1)
    row = lax.broadcasted_iota(jnp.int32, (8, ROWS), 0)
    lows = jnp.where(lane < VBLOCK, low_smem[0], low_smem[1])
    highs = jnp.where(lane < VBLOCK, high_smem[0], high_smem[1])
    delta_copy.wait()
    small_buf[c, 0:8] = jnp.where(row == 0, lows, highs).astype(jnp.float32)
    small_buf[c, 8:20] = delta_own[...]
    small_buf[c, 20:24] = jnp.zeros((4, ROWS), jnp.float32)
    small = pltpu.make_async_remote_copy(
        small_buf.at[c], small_buf.at[c], small_send, small_recv, device_id=partner, device_id_type=MESH
    )
    small.start()
    small.wait_recv()

    row = lax.broadcasted_iota(jnp.int32, (REACH, ROWS), 0)
    for slot in range(2):
        blocks = 8 * v + 2 * y + jnp.where(row < 2 * ABLOCK, row // ABLOCK, 3 * slot - 1)
        blocks = blocks.astype(jnp.float32)
        inside = (blocks >= small_buf[slot, 0:1, :]) & (blocks < small_buf[slot, 1:2, :])
        bias_buf[slot] = jnp.where(inside, 0.0, masked_score)

    def part_copies(slot, groups, do, do_local):
        if slot is None:
            start, size, span, exists = ABLOCK, 2 * ABLOCK, v, True
        else:
            start, size = pl.multiple_of(REACH * slot, ABLOCK), ABLOCK
            down, up = is_first & (slot == 0), is_last & (slot == 1)
            span = v - jnp.where(down, 1, 0)
            exists = jnp.logical_not(down & jnp.logical_not(has_before)) & jnp.logical_not(up)
        for g in groups:
            k = group_of(y, c, g)
            for core in range(2):
                source = stage.at[g, core, :, pl.ds(start, size)]
                target = landed.at[y, :, pl.ds(start, size)]
                here = (span == v) & (2 * k + core == a) & exists
                away = jnp.logical_not(here) if g == 1 else True

                @pl.when(away & exists)
                def _():
                    do(
                        pltpu.make_async_remote_copy(
                            source, target, part_send, part_recv,
                            device_id=(span, 2 * k + core), device_id_type=MESH,
                        )
                    )

                if g == 1:

                    @pl.when(here)
                    def _():
                        do_local(pltpu.make_async_copy(source, target, part_recv))

    def dq_copies(g, slot):
        k = group_of(y, c, g)
        return (
            pltpu.make_async_copy(dq_buf.at[g, slot], dq_out.at[:, lanes(k)], out_sem),
            pltpu.make_async_remote_copy(
                dq_buf.at[g, slot], dq_out.at[:, lanes(k)], dq_send, dq_recv,
                device_id=partner, device_id_type=MESH,
            ),
        )

    def work(last):
        slot = jnp.where(is_first, 1, 0)
        if last:
            slot = 1 - slot

        @pl.when(slot == c)
        def _():
            landed_wait(rows_buf.at[:, :, slot], rows_sem)

        @pl.when(slot != c)
        def _():
            landed_wait(rows_buf.at[:, :, slot], swap_recv)

        def halo_wait(ref, sem):
            if last:

                @pl.when((is_first & has_before) | (is_last & has_after & (c == 0)))
                def _():
                    landed_wait(ref, sem)

        def start(copy):
            copy.start()

        def put(heads, rows, key_parts, value_parts):
            for (g, i, _), key_part, value_part in zip(heads, key_parts, value_parts):
                if i == 1:
                    half = lax.broadcasted_iota(jnp.int32, key_part.shape, 1) < HEAD_DIM // 2
                    stage[g, 0, 2, rows] = jnp.where(half, key_part, pltpu.roll(value_part, 64, 1)).astype(jnp.bfloat16)
                    stage[g, 1, 2, rows] = jnp.where(half, pltpu.roll(key_part, 64, 1), value_part).astype(jnp.bfloat16)
                else:
                    stage[g, i // 2, 0, rows] = key_part.astype(jnp.bfloat16)
                    stage[g, i // 2, 1, rows] = value_part.astype(jnp.bfloat16)

        if not last:
            audio_wait()
        middle = pl.ds(ABLOCK, 2 * ABLOCK)
        alone = pl.ds(pl.multiple_of(REACH * slot, ABLOCK), ABLOCK)
        bias = bias_buf[slot]

        def gradients(groups):
            heads = [(g, i, slice(i * HEAD_DIM, (i + 1) * HEAD_DIM)) for g in groups for i in range(3)]
            deltas = [small_buf[slot, pl.ds(8 + 3 * group_of(y, c, g) + i, 1), :] for g, i, _ in heads]

            for g in groups:
                halo_wait(k_buf.at[g, pl.ds(0, ABLOCK)], halo_recv.at[g])
            keys = [jnp.concatenate([k_buf[g, middle, cols], k_buf[g, alone, cols]], axis=0) for g, _, cols in heads]
            scores = [nt(key, q_buf[g, slot, :, cols]) for key, (g, _, cols) in zip(keys, heads)]
            prob_grads = [nt(v_buf[g, middle, cols], og_buf[g, slot, :, cols]) for g, _, cols in heads]
            probs, prob_halves, middle_halves = [], [], []
            for score, prob_grad, delta in zip(scores, prob_grads, deltas):
                score = score + bias
                peak = jnp.max(score, axis=0, keepdims=True)
                weights = jnp.exp2((score - peak) * (logit_scale * math.log2(math.e)))
                prob = weights * (1.0 / jnp.sum(weights, axis=0, keepdims=True))
                probs.append(prob[64:96])
                prob_halves.append(prob.astype(jnp.bfloat16))
                middle_halves.append((prob[0:64] * (prob_grad - delta)).astype(jnp.bfloat16))
            value_parts = [nn(prob, og_buf[g, slot, :, cols]) for prob, (g, _, cols) in zip(prob_halves, heads)]
            key_parts = [nn(score, q_buf[g, slot, :, cols]) * logit_scale for score, (g, _, cols) in zip(middle_halves, heads)]
            if last:
                key_parts = [part + key_sum[g, i] for part, (g, i, _) in zip(key_parts, heads)]
                middle_values = [part[0:64] + value_sum[g, i] for part, (g, i, _) in zip(value_parts, heads)]
                put(heads, middle, key_parts, middle_values)

                part_copies(None, groups, start, start)
            else:
                for key_part, value_part, (g, i, _) in zip(key_parts, value_parts, heads):
                    key_sum[g, i] = key_part
                    value_sum[g, i] = value_part[0:64]

            return heads, deltas, keys, probs, middle_halves, value_parts

        def edge_gradients(groups, heads, deltas, keys, probs, middle_halves, value_parts):
            halo_wait(v_buf.at[:, pl.ds(0, ABLOCK)], halo_recv.at[2])
            prob_grads = [nt(v_buf[g, alone, cols], og_buf[g, slot, :, cols]) for g, _, cols in heads]
            alone_halves = [
                (prob * (prob_grad - delta)).astype(jnp.bfloat16) for prob, prob_grad, delta in zip(probs, prob_grads, deltas)
            ]
            key_parts = [nn(score, q_buf[g, slot, :, cols]) * logit_scale for score, (g, _, cols) in zip(alone_halves, heads)]
            put(heads, alone, key_parts, [part[64:96] for part in value_parts])
            if last:

                @pl.when(is_first & has_before & (0 in groups))
                def _():
                    pl.semaphore_wait(part_ready, 4)

            part_copies(slot, groups if last else (0,), start, start)
            return list(zip(heads, keys, middle_halves, alone_halves))

        if last:
            first = gradients((0,))
            part_copies(1 - slot, (1,), start, start)
            second = gradients((1,))
            done = edge_gradients((0, 1), *[one + other for one, other in zip(first, second)])
        else:
            done = edge_gradients((0, 1), *gradients((0, 1)))
        for (g, _, cols), key, first, second in done:
            score_half = jnp.concatenate([first, second], axis=0)
            dq_buf[g, slot, :, cols] = (tn(score_half, key) * logit_scale).astype(jnp.bfloat16)

        @pl.when(slot == c)
        def _():
            for g in range(2):
                dq_copies(g, slot)[0].start()

        @pl.when(slot != c)
        def _():
            for g in range(2):
                dq_copies(g, slot)[1].start()

    def edge_part_copies(j):
        return [
            pltpu.make_async_remote_copy(
                edge_stage.at[j, core], landed.at[CHIPS - 1, :, pl.ds(96, ABLOCK)],
                edge_send, part_recv,
                device_id=(v + 1, 2 * j + core), device_id_type=MESH,
            )
            for core in range(2)
        ]

    def edge_work(j, wait):
        heads = [slice(i * HEAD_DIM, (i + 1) * HEAD_DIM) for i in range(3)]
        bias = bias_buf[1]
        deltas = [small_buf[1, pl.ds(8 + 3 * j + i, 1), :] for i in range(3)]
        wait(j, 0)
        keys = [jnp.concatenate([k_own[j, :, cols], edge_kv[j, 0, :, cols]], axis=0) for cols in heads]
        scores = [nt(key, q_own[j, :, cols]) + bias for key, cols in zip(keys, heads)]
        probs = []
        for score in scores:
            weights = jnp.exp2((score - jnp.max(score, axis=0, keepdims=True)) * (logit_scale * math.log2(math.e)))
            probs.append(weights[64:96] * (1.0 / jnp.sum(weights, axis=0, keepdims=True)))
        value_parts = [nn(prob.astype(jnp.bfloat16), og_own[j, :, cols]) for prob, cols in zip(probs, heads)]
        wait(j, 1)
        prob_grads = [nt(edge_kv[j, 1, :, cols], og_own[j, :, cols]) for cols in heads]
        halves = [(p * (grad - delta)).astype(jnp.bfloat16) for p, grad, delta in zip(probs, prob_grads, deltas)]
        key_parts = [nn(score, q_own[j, :, cols]) * logit_scale for score, cols in zip(halves, heads)]
        half = lax.broadcasted_iota(jnp.int32, (ABLOCK, HEAD_DIM), 1) < HEAD_DIM // 2
        for core in range(2):
            edge_stage[j, core, 0] = key_parts[2 * core].astype(jnp.bfloat16)
            edge_stage[j, core, 1] = value_parts[2 * core].astype(jnp.bfloat16)
        edge_stage[j, 0, 2] = jnp.where(half, key_parts[1], pltpu.roll(value_parts[1], 64, 1)).astype(jnp.bfloat16)
        edge_stage[j, 1, 2] = jnp.where(half, pltpu.roll(key_parts[1], 64, 1), value_parts[1]).astype(jnp.bfloat16)
        for copy in edge_part_copies(j):
            copy.start()

    @pl.when(works_up)
    def _():
        landed_wait(gauge, own_sem)

        @pl.when(edge_first)
        def _():
            lax.fori_loop(0, CHIPS, lambda j, carry: (edge_work(j, arrived), carry)[1], 0)

    work(False)

    @pl.when(works_up)
    def _():
        @pl.when(jnp.logical_not(edge_first | edge_early))
        def _():
            for j in range(CHIPS):
                arrived(j, 0)
                arrived(j, 1)

        @pl.when(jnp.logical_not(edge_early))
        def _():
            for copy in hand_on:
                copy.start()

        for g in range(2):
            for i in range(2):
                audio_buf[i, g, pl.ds(96, ABLOCK)] = edge_kv[3 * g, i]

    work(True)

    @pl.when(works_up & jnp.logical_not(edge_first))
    def _():
        lax.fori_loop(0, CHIPS, lambda j, carry: (edge_work(j, lambda j, i: None), carry)[1], 0)

    up = jnp.where(is_last, jnp.where(c == 1, 12, 2), jnp.where(c == 0, jnp.where(is_first, 4, jnp.where(y == 1, 2, 0)), 0))
    edge_units = jnp.where(has_after, up, 0) + jnp.where(sends_down, 4, 0)
    for count in (2, 4, 6, 12, 16):

        @pl.when(edge_units == count)
        def _():
            sent_wait(gauge.at[pl.ds(0, count)], edge_send)

    small.wait_send()
    landed_wait(dq_buf.at[:, c], out_sem)
    sent_wait(gauge.at[pl.ds(0, 24)], dq_send)
    landed_wait(dq_buf.at[:, other], dq_recv)

    copies = 4 - (1 - role(y, c))
    to_before = jnp.where(has_before, 4, 0)
    units = 3 * copies + jnp.where(is_first, to_before, jnp.where(is_last, 0, copies))
    for count in (9, 12, 13, 16):

        @pl.when(units == count)
        def _():
            sent_wait(gauge.at[pl.ds(0, count)], part_send)

    @pl.when(has_before & has_after)
    def _():
        landed_wait(gauge.at[pl.ds(0, 16)], part_recv)

    @pl.when(jnp.logical_not(has_before & has_after))
    def _():
        landed_wait(gauge.at[pl.ds(0, 15)], part_recv)


def finish(dq_in, landed, dq_hbm, dk_hbm, dv_hbm, dk_buf, dv_buf, sem):
    c = lax.axis_index("audio") % 2
    dq_copy = pltpu.make_async_copy(dq_in, dq_hbm, sem.at[0])
    dq_copy.start()
    head_rows = pl.ds(pl.multiple_of(64 * c, 64), 128)
    middle_rows = pl.ds(pl.multiple_of(128 - 128 * c, 64), 64)
    for pair in range(2):
        rows = slice(pair * 128, (pair + 1) * 128)
        tiles = []
        for t in range(3):
            blocks = []
            for chip in (2 * pair, 2 * pair + 1):
                for own, far_chip, far in ((32, (chip + 3) % CHIPS, 96), (64, (chip + 1) % CHIPS, 0)):
                    own_term = landed[chip, t, own : own + ABLOCK].astype(jnp.float32)
                    blocks.append(own_term + landed[far_chip, t, far : far + ABLOCK].astype(jnp.float32))
            tiles.append(jnp.concatenate(blocks, axis=0).T.astype(jnp.bfloat16))
        dk_buf[head_rows, rows] = tiles[0]
        dv_buf[head_rows, rows] = tiles[1]
        dk_buf[middle_rows, rows] = tiles[2][0:64]
        dv_buf[middle_rows, rows] = tiles[2][64:128]
    copies = [pltpu.make_async_copy(dk_buf, dk_hbm, sem.at[1]), pltpu.make_async_copy(dv_buf, dv_hbm, sem.at[2])]
    for copy in copies:
        copy.start()
    for copy in [dq_copy] + copies:
        copy.wait()


def on_device(queries, keys, values, out_grad, delta, window_low, window_high):
    bf16, f32 = jnp.bfloat16, jnp.float32
    hbm, vmem = pl.BlockSpec(memory_space=pltpu.HBM), pl.BlockSpec(memory_space=pltpu.VMEM)
    dma = pltpu.SemaphoreType.DMA
    arrays = (queries, keys, values, out_grad, delta, window_low, window_high)
    arrays = [pltpu.with_memory_space_constraint(array, pltpu.HBM) for array in arrays]
    query_grad, landed = pl.pallas_call(
        kernel,
        out_shape=(pltpu.VMEM((ROWS, 1536), bf16), pltpu.VMEM((CHIPS, 3, AROWS, HEAD_DIM), bf16)),
        in_specs=[hbm] * 7,
        out_specs=(vmem, vmem),
        scratch_shapes=[
            pltpu.VMEM((2, 2, 2, ROWS, GROUP), bf16),
            pltpu.VMEM((2, 2, AROWS, GROUP), bf16),
            pltpu.VMEM((4, ABLOCK, GROUP), bf16),
            pltpu.VMEM((2, CHIPS, ROWS, GROUP), bf16),
            pltpu.VMEM((CHIPS, 2 * ABLOCK, GROUP), bf16),
            pltpu.VMEM((CHIPS, 2, ABLOCK, GROUP), bf16),
            pltpu.VMEM((CHIPS, 2, 3, ABLOCK, HEAD_DIM), bf16),
            pltpu.VMEM((12, ROWS), f32),
            pltpu.VMEM((2, 24, ROWS), f32),
            pltpu.VMEM((2, REACH, ROWS), f32),
            pltpu.VMEM((2, 2, ROWS, GROUP), bf16),
            pltpu.VMEM((2, 3, 2 * ABLOCK, HEAD_DIM), f32),
            pltpu.VMEM((2, 3, 2 * ABLOCK, HEAD_DIM), f32),
            pltpu.VMEM((2, 2, 3, AROWS, HEAD_DIM), bf16),
            pltpu.VMEM((40, ABLOCK, GROUP), bf16),
            pltpu.SMEM((2,), jnp.int32),
            pltpu.SMEM((2,), jnp.int32),
            dma((2,)),
            dma(()),
            dma(()),
            dma(()),
            dma(()),
            dma(()),
            dma(()),
            dma(()),
            dma(()),
            dma(()),
            dma(()),
            dma((3,)),
            dma((CHIPS, 2)),
            dma(()),
            dma(()),
            dma(()),
            dma(()),
            pltpu.SemaphoreType.REGULAR,
        ],
        compiler_params=pltpu.CompilerParams(
            collective_id=0, has_side_effects=True, vmem_limit_bytes=32 << 20
        ),
        name="attention_backward",
    )(*arrays)
    query_grad, key_grad, value_grad = pl.pallas_call(
        finish,
        out_shape=(
            jax.ShapeDtypeStruct((ROWS, 1536), bf16),
            jax.ShapeDtypeStruct((192, 256), bf16),
            jax.ShapeDtypeStruct((192, 256), bf16),
        ),
        in_specs=[vmem, vmem],
        out_specs=(hbm, hbm, hbm),
        scratch_shapes=[pltpu.VMEM((192, 256), bf16), pltpu.VMEM((192, 256), bf16), dma((3,))],
        compiler_params=pltpu.CompilerParams(vmem_limit_bytes=32 << 20),
        name="sum_partials",
    )(query_grad, landed)
    return query_grad, key_grad.T, value_grad.T


def solution(mesh):
    return jax.shard_map(
        on_device,
        mesh=mesh,
        in_specs=(
            P(("video", "audio"), None),
            P("video", None),
            P("video", None),
            P(("video", "audio"), None),
            P(None, ("video", "audio")),
            P(("video", "audio")),
            P(("video", "audio")),
        ),
        out_specs=(P(("video", "audio"), None), P("video", "audio"), P("video", "audio")),
        check_vma=False,
    )
```
